32 devices in a mesh: ctxouter: 4 (over y, x), ctxinner: 8 (over z, core).
Axes of the slice: x: 2, y: 2, z: 4, core: 2. Of those that a mesh axis runs over, the one named last changes fastest.
Arguments:
- lin_qk: bfloat16 [4096, 512], P(('ctxouter', 'ctxinner')), may hold values from -8 to 8, as said below
- lin_v: bfloat16 [4096, 1024], P(('ctxouter', 'ctxinner')), may hold values from -6 to 6
- conv_w: float32 [3, 1024], replicated, may hold values from -2.5 to 2.5
- swa_qkv: bfloat16 [4096, 3072], P(('ctxouter', 'ctxinner')), may hold values from -8 to 8
Outputs:
- mixed: bfloat16 [4096, 1024], P(('ctxouter', 'ctxinner'))
The draws below stay inside these ranges and needn't reach their ends.
Inputs may be any that keep to these rules, and one draw needn't show every extreme that they name: `lin_qk`: keys have a scale of their own in each context block and head.
All inputs are finite; a program needn't handle non-finite values.
Results may differ from the reference program's by a relative error of at most 0.0045.
Values may be sent and summed in bfloat16 or wider, within the bound.
No kernel may reach another device: no remote copies, remote signals or barrier semaphores. Data moves between devices by JAX's collectives and lax.ppermute only.
A program may use at most 128 MiB of HBM per device.

```python
import math
import jax
import jax.numpy as jnp
import numpy as np
from jax import lax

HEADS = 16
FEAT = 16
VHEAD = 64
SWA_HEADS = 8
SWA_HEAD = 128
WINDOW = 64
CONV = 3
TOK_DEV = 128
TOKENS = 4096


def draw_lin_qk(key, part):
    first, second = jax.random.split(key, 2)
    blocks = TOKENS // TOK_DEV
    shape = (blocks, TOK_DEV, 2, HEADS, FEAT)
    base = jnp.clip(jax.random.normal(first, shape, jnp.float32), -4.0, 4.0)
    key_scale = jnp.exp(jax.random.uniform(second, (blocks, 1, 1, HEADS, 1), jnp.float32, math.log(0.5), math.log(2.0)))
    both_scale = jnp.concatenate([jnp.ones_like(key_scale), key_scale], axis=2)
    result = (base * both_scale).reshape(TOKENS, 2 * HEADS * FEAT)
    return jnp.clip(result, -8.0, 8.0).astype(jnp.bfloat16)


def draw_lin_v(key, part):
    first, second = jax.random.split(key, 2)
    blocks = TOKENS // TOK_DEV
    shape = (blocks, TOK_DEV, HEADS * VHEAD)
    base = jnp.clip(jax.random.normal(first, shape, jnp.float32), -3.0, 3.0)
    offset = jax.random.uniform(second, (blocks, 1, HEADS * VHEAD), jnp.float32, -1.5, 1.5)
    result = (base + offset).reshape(TOKENS, HEADS * VHEAD)
    return jnp.clip(result, -6.0, 6.0).astype(jnp.bfloat16)


def draw_swa_qkv(key, part):
    first = jax.random.fold_in(key, 0)
    swa_width = SWA_HEADS * SWA_HEAD
    result = jnp.clip(jax.random.normal(first, (TOKENS, 3 * swa_width), jnp.float32), -4.0, 4.0)
    return jnp.clip(result, -8.0, 8.0).astype(jnp.bfloat16)


def normal_values(key, shape, spread, limit, held_as=jnp.bfloat16):
    values = spread * jax.random.normal(key, shape, jnp.float32)
    return jnp.clip(values, min=-limit, max=limit).astype(held_as)


def setup_inputs(seed: int = 0) -> dict:
    key_of = jax.random.split(jax.random.key(seed), 5)
    return {
        "lin_qk": draw_lin_qk(jax.random.fold_in(key_of[4], 71), 0),
        "lin_v": draw_lin_v(jax.random.fold_in(key_of[4], 71), 0),
        "conv_w": normal_values(key_of[2], (CONV, HEADS * VHEAD), 0.6, 2.5, jnp.float32),
        "swa_qkv": draw_swa_qkv(jax.random.fold_in(key_of[4], 71), 0),
    }


def features(values):
    size = values.shape[1]
    upper, lower = np.triu_indices(size)
    factor = np.where(upper == lower, np.sqrt(0.5), 1.0).astype(np.float32)
    second = values[:, upper, :] * values[:, lower, :] * jnp.asarray(factor)[None, :, None]
    return jnp.concatenate([jnp.ones_like(values[:, :1, :]), values, second], axis=1)

def split_heads(block_qk):
    count = block_qk.shape[0]
    scaled = block_qk.astype(jnp.float32).reshape(count, 2, HEADS, FEAT) * FEAT ** (-0.25)
    return (jnp.transpose(scaled[:, 0], (1, 2, 0)), jnp.transpose(scaled[:, 1], (1, 2, 0)))

def reference(lin_qk, lin_v, conv_w, swa_qkv):
    total = lin_qk.shape[0]
    blocks = total // TOK_DEV
    conv_taps = conv_w.shape[0]
    padded_v = jnp.pad(lin_v.astype(jnp.float32), ((conv_taps - 1, 0), (0, 0)))
    conved = conv_w[0] * padded_v[conv_taps - 1:]
    for conv_lag in range(1, conv_taps):
        conved = conved + conv_w[conv_lag] * padded_v[conv_taps - 1 - conv_lag:conv_taps - 1 - conv_lag + total]
    conved = conved.astype(jnp.bfloat16)
    qk_blocks = lin_qk.reshape(blocks, TOK_DEV, 2 * HEADS * FEAT)
    v_blocks = conved.reshape(blocks, TOK_DEV, HEADS, VHEAD)

    def own_state(inputs):
        block_qk, block_v = inputs
        query_t, key_t = split_heads(block_qk)
        phi_key = features(key_t)
        state = jnp.einsum('het,thv->hev', phi_key, block_v.astype(jnp.float32), precision=lax.Precision.HIGHEST)
        return (state, lax.optimization_barrier(jnp.sum(phi_key, axis=-1)))
    states, norms = lax.map(own_state, (qk_blocks, v_blocks))
    past_states = jnp.concatenate([jnp.zeros_like(states[:1]), jnp.cumsum(states, axis=0)[:-1]], axis=0)
    past_norms = jnp.concatenate([jnp.zeros_like(norms[:1]), jnp.cumsum(norms, axis=0)[:-1]], axis=0)
    step_rows = min(512, TOK_DEV)

    def readout(inputs):
        block_qk, block_v, past_state, past_norm = inputs
        query_t, key_t = split_heads(block_qk)
        phi_query = features(query_t)
        numer = jnp.einsum('het,hev->htv', phi_query, past_state, precision=lax.Precision.HIGHEST)
        denom = jnp.einsum('het,he->ht', phi_query, past_norm, precision=lax.Precision.HIGHEST)
        value_f = block_v.astype(jnp.float32)
        numer_parts = []
        denom_parts = []
        for block_num in range(TOK_DEV // step_rows):
            finish = (block_num + 1) * step_rows
            score = jnp.einsum('hfq,hfk->hqk', query_t[:, :, block_num * step_rows:finish], key_t[:, :, :finish], precision=lax.Precision.HIGHEST)
            weight = 1.0 + score + 0.5 * score * score
            query_pos = block_num * step_rows + jnp.arange(step_rows)[:, None]
            key_pos = jnp.arange(finish)[None, :]
            weight = jnp.where(key_pos <= query_pos, weight, 0.0)
            weight = lax.optimization_barrier(weight.astype(jnp.bfloat16)).astype(jnp.float32)
            numer_parts.append(jnp.einsum('hqk,khv->hqv', weight, value_f[:finish], precision=lax.Precision.HIGHEST))
            denom_parts.append(lax.optimization_barrier(jnp.sum(weight, axis=-1)))
        numer = numer + jnp.concatenate(numer_parts, axis=1)
        denom = denom + jnp.concatenate(denom_parts, axis=1)
        result = numer / denom[..., None]
        return jnp.transpose(result, (1, 0, 2)).reshape(TOK_DEV, HEADS * VHEAD)
    lin_out = lax.map(readout, (qk_blocks, v_blocks, past_states, past_norms)).reshape(total, HEADS * VHEAD)
    swa_width = SWA_HEADS * SWA_HEAD
    reach = WINDOW - 1
    query_rows = min(128, TOK_DEV)
    query_all = swa_qkv[:, :swa_width]
    padded_kv = jnp.pad(swa_qkv[:, swa_width:], ((reach, 0), (0, 0)))

    def attend(start):
        query = lax.dynamic_slice_in_dim(query_all, start, query_rows, 0).astype(jnp.float32).reshape(query_rows, SWA_HEADS, SWA_HEAD)
        segment = lax.dynamic_slice_in_dim(padded_kv, start, query_rows + reach, 0).astype(jnp.float32)
        keys = segment[:, :swa_width].reshape(query_rows + reach, SWA_HEADS, SWA_HEAD)
        values = segment[:, swa_width:].reshape(query_rows + reach, SWA_HEADS, SWA_HEAD)
        score = jnp.einsum('qhd,khd->hqk', query, keys, precision=lax.Precision.HIGHEST) * SWA_HEAD ** (-0.5)
        query_pos = jnp.arange(query_rows)[:, None]
        key_pos = jnp.arange(query_rows + reach)[None, :]
        valid = (key_pos >= query_pos) & (key_pos <= query_pos + reach) & (start + key_pos >= reach)
        score = jnp.where(valid, score, -jnp.inf)
        top = lax.optimization_barrier(jnp.max(score, axis=-1, keepdims=True))
        expo = jnp.exp(score - top)
        probs = expo / lax.optimization_barrier(jnp.sum(expo, axis=-1, keepdims=True))
        probs = lax.optimization_barrier(probs.astype(jnp.bfloat16)).astype(jnp.float32)
        result = jnp.einsum('hqk,khd->qhd', probs, values, precision=lax.Precision.HIGHEST)
        return result.reshape(query_rows, swa_width)
    starts = (jnp.arange(total // query_rows) * query_rows).astype(jnp.int32)
    swa_out = lax.map(attend, starts).reshape(total, swa_width)
    return (lin_out + swa_out).astype(jnp.bfloat16)
```

```python
import functools

import jax
import jax.numpy as jnp
import numpy as np
from jax import lax
from jax.experimental import pallas as pl
from jax.experimental.pallas import tpu as pltpu
from jax.sharding import PartitionSpec as P

HEADS = 16
FEAT = 16
VHEAD = 64
SWA_HEADS = 8
SWA_HEAD = 128
WINDOW = 64

AXES = ("ctxouter", "ctxinner")
LANES = 128
PAIRS = HEADS // 2
QUADS = FEAT * (FEAT + 1) // 2
CONST = QUADS + FEAT
ROWS = 160
TAIL = 16
VMEM_LIMIT = 48 * 1024 * 1024

NT = (((1,), (1,)), ((), ()))
NN = (((1,), (0,)), ((), ()))


def dot(a, b, dims=NN):
    return lax.dot_general(a, b, dims, preferred_element_type=jnp.float32)


def selectors():
    upper, lower = np.triu_indices(FEAT)
    scale = FEAT ** (-0.25)
    first = np.zeros((FEAT, ROWS), np.float32)
    second = np.zeros((FEAT, ROWS), np.float32)
    first[upper, np.arange(QUADS)] = scale
    second[lower, np.arange(QUADS)] = scale
    first[np.arange(FEAT), QUADS + np.arange(FEAT)] = scale
    halved = first.copy()
    halved[:, np.arange(QUADS)[upper == lower]] *= 0.5
    add_first = np.zeros((8, ROWS), np.float32)
    add_first[:, CONST] = 1.0
    add_second = np.zeros((8, ROWS), np.float32)
    add_second[:, QUADS : CONST + 1] = 1.0
    return first, second, halved, add_first, add_second


def split_hi_lo(values):
    high = values.astype(jnp.bfloat16)
    return high, (values - high.astype(jnp.float32)).astype(jnp.bfloat16)


def head_mask(head, shape):
    place = lax.broadcasted_iota(jnp.int32, shape, 1)
    return (place >= head * FEAT) & (place < (head + 1) * FEAT)


def state_kernel(first_ref, second_ref, qk_ref, v_ref, tail_ref, conv_ref, cv_ref, state_ref):
    rows = v_ref.shape[0]
    taps = conv_ref.shape[0]
    width = HEADS * FEAT
    key = qk_ref[:, width : 2 * width]
    row_id = lax.broadcasted_iota(jnp.int32, (rows, LANES), 0)
    lane_id = lax.broadcasted_iota(jnp.int32, (ROWS, LANES), 1)
    low_row = lax.broadcasted_iota(jnp.int32, (8, LANES), 0)
    const_rows = jnp.where(lax.broadcasted_iota(jnp.int32, (8, rows), 0) == 0, 1.0, 0.0)
    ones = jnp.ones((8, rows), jnp.bfloat16)
    for pair in range(PAIRS):
        lanes = slice(pair * LANES, (pair + 1) * LANES)
        value = v_ref[:, lanes].astype(jnp.float32)
        tail = tail_ref[:, lanes].astype(jnp.float32)
        conved = conv_ref[0:1, lanes] * value
        for lag in range(1, taps):
            shifted = pltpu.roll(value, lag, 0)
            for row in range(lag):
                source = TAIL - lag + row
                shifted = jnp.where(row_id == row, tail[source : source + 1], shifted)
            conved = conved + conv_ref[lag : lag + 1, lanes] * shifted
        conved = conved.astype(jnp.bfloat16)
        cv_ref[:, lanes] = conved
        states = []
        norms = []
        for head in (2 * pair, 2 * pair + 1):
            own = jnp.where(head_mask(head, key.shape), key, jnp.zeros_like(key))
            one = dot(first_ref[...], own, NT)
            two = dot(second_ref[...], own, NT)
            phi = jnp.concatenate(
                [one[:QUADS] * two[:QUADS], one[QUADS:CONST], const_rows], axis=0
            )
            high, low = split_hi_lo(phi)
            states.append(dot(high, conved) + dot(low, conved))
            norm = dot(ones, high, NT) + dot(ones, low, NT)
            norms.append(norm[:, :LANES])
            norms.append(
                jnp.concatenate(
                    [norm[:, LANES:], jnp.zeros((8, 2 * LANES - ROWS), jnp.float32)], axis=1
                )
            )
        state = jnp.where(lane_id < VHEAD, states[0], states[1])
        last = state[CONST:]
        for place, norm in enumerate(norms):
            last = jnp.where(low_row == 1 + place, norm, last)
        state = jnp.concatenate([state[:CONST], last], axis=0)
        state_ref[pair * ROWS : (pair + 1) * ROWS, :] = state.astype(jnp.bfloat16)


def local_kernel(first_ref, qk_ref, cv_ref, swa_ref, kv_ref, numer_ref, denom_ref, swa_out_ref):
    rows = cv_ref.shape[0]
    width = HEADS * FEAT
    query = qk_ref[:, :width]
    key = qk_ref[:, width : 2 * width]
    lane_id = lax.broadcasted_iota(jnp.int32, (rows, LANES), 1)
    causal = lax.broadcasted_iota(jnp.int32, (rows, rows), 1) <= lax.broadcasted_iota(
        jnp.int32, (rows, rows), 0
    )
    ones = jnp.ones((rows, LANES), jnp.bfloat16)
    for pair in range(PAIRS):
        lanes = slice(pair * LANES, (pair + 1) * LANES)
        conved = cv_ref[:, lanes]
        numers = []
        denoms = []
        for head in (2 * pair, 2 * pair + 1):
            own = jnp.where(head_mask(head, query.shape), query, jnp.zeros_like(query))
            score = dot(own, key, NT) * FEAT ** (-0.5)
            weight = 1.0 + score + 0.5 * score * score
            weight = jnp.where(causal, weight, 0.0).astype(jnp.bfloat16)
            numers.append(dot(weight, conved))
            denoms.append(dot(weight, ones))
        numer_ref[:, lanes] = jnp.where(lane_id < VHEAD, numers[0], numers[1])
        denom_ref[:, lanes] = jnp.where(lane_id < VHEAD, denoms[0], denoms[1])
    swa_width = SWA_HEADS * SWA_HEAD
    not_before = jnp.where(first_ref[0] == 0, WINDOW, 0)
    span = 2 * WINDOW
    place = lax.broadcasted_iota(jnp.int32, (WINDOW, span), 1)
    row = lax.broadcasted_iota(jnp.int32, (WINDOW, span), 0)
    inside = (place > row) & (place <= row + WINDOW)
    inside_first = inside & (place >= not_before)
    for head in range(SWA_HEADS):
        at = head * SWA_HEAD
        for step in range(rows // WINDOW):
            mine = slice(step * WINDOW, (step + 1) * WINDOW)
            query = swa_ref[mine, at : at + SWA_HEAD]
            both = []
            for start in (swa_width + at, 2 * swa_width + at):
                if step == 0:
                    before = kv_ref[:, start - swa_width : start - swa_width + SWA_HEAD]
                    both.append(
                        jnp.concatenate([before, swa_ref[mine, start : start + SWA_HEAD]], axis=0)
                    )
                else:
                    both.append(
                        swa_ref[(step - 1) * WINDOW : (step + 1) * WINDOW, start : start + SWA_HEAD]
                    )
            score = dot(query, both[0], NT) * SWA_HEAD ** (-0.5)
            score = jnp.where(inside_first if step == 0 else inside, score, -jnp.inf)
            expo = jnp.exp(score - jnp.max(score, axis=-1, keepdims=True))
            probs = (expo / jnp.sum(expo, axis=-1, keepdims=True)).astype(jnp.bfloat16)
            swa_out_ref[mine, at : at + SWA_HEAD] = dot(probs, both[1])


def readout_kernel(
    first_ref, second_ref, add_first_ref, add_second_ref,
    qk_ref, past_ref, numer_ref, denom_ref, swa_ref, out_ref,
):
    rows = qk_ref.shape[0]
    query = qk_ref[:, : HEADS * FEAT]
    lane_id = lax.broadcasted_iota(jnp.int32, (rows, LANES), 1)
    for pair in range(PAIRS):
        lanes = slice(pair * LANES, (pair + 1) * LANES)
        past = past_ref[pair * ROWS : (pair + 1) * ROWS, :]
        last = past[ROWS - 16 :].astype(jnp.float32)
        numers = []
        denoms = []
        for place, head in enumerate((2 * pair, 2 * pair + 1)):
            own = jnp.where(head_mask(head, query.shape), query, jnp.zeros_like(query))
            one = dot(own, first_ref[...]) + add_first_ref[0:1]
            two = dot(own, second_ref[...]) + add_second_ref[0:1]
            high, low = split_hi_lo(one * two)
            numers.append(dot(high, past) + dot(low, past))
            at = 16 - (ROWS - CONST) + 1 + 2 * place
            norm = jnp.concatenate([last[at : at + 1], last[at + 1 : at + 2, : ROWS - LANES]], axis=1)
            norm = jnp.broadcast_to(norm, (LANES, ROWS)).astype(jnp.bfloat16)
            denoms.append(dot(high, norm, NT) + dot(low, norm, NT))
        numer = jnp.where(lane_id < VHEAD, numers[0], numers[1]) + numer_ref[:, lanes]
        denom = jnp.where(lane_id < VHEAD, denoms[0], denoms[1]) + denom_ref[:, lanes]
        out_ref[:, lanes] = (numer / denom + swa_ref[:, lanes]).astype(out_ref.dtype)


def call(kernel, outs, args, specs=None):
    whole = pl.BlockSpec(memory_space=pltpu.VMEM)
    return pl.pallas_call(
        kernel,
        out_shape=outs,
        in_specs=specs or [whole] * len(args),
        out_specs=jax.tree.map(lambda _: whole, outs),
        compiler_params=pltpu.CompilerParams(vmem_limit_bytes=VMEM_LIMIT),
    )(*args)


def shards(lin_qk, lin_v, conv_w, swa_qkv):
    rows = lin_qk.shape[0]
    devices = lax.axis_size("ctxouter") * lax.axis_size("ctxinner")
    swa_width = swa_qkv.shape[1] // 3
    shift = [(i, i + 1) for i in range(devices - 1)]
    bf16 = jnp.bfloat16
    first, second, halved, add_first, add_second = selectors()
    stacked = lambda a: jnp.asarray(np.tile(a, (HEADS, 1)), bf16)
    stacked_t = lambda a: jnp.asarray(np.tile(a, (HEADS, 1)).T, bf16)

    tail_v = lax.ppermute(lin_v[rows - TAIL :], AXES, shift)
    conved, state = call(
        state_kernel,
        [
            jax.ShapeDtypeStruct(lin_v.shape, bf16),
            jax.ShapeDtypeStruct((PAIRS * ROWS, LANES), bf16),
        ],
        [stacked_t(first), stacked_t(second), lin_qk, lin_v, tail_v, conv_w],
    )
    tail_kv = lax.ppermute(swa_qkv[rows - WINDOW :, swa_width:], AXES, shift)
    parts = lax.all_to_all(state.reshape(devices, -1, LANES), AXES, 0, 0, tiled=True)
    before = jnp.asarray(np.tril(np.ones((devices, devices), np.float32), -1), bf16)
    past = jnp.einsum("ij,jrl->irl", before, parts, preferred_element_type=jnp.float32).astype(bf16)
    past = lax.all_to_all(past, AXES, 0, 0, tiled=True).reshape(PAIRS * ROWS, LANES)
    whole = pl.BlockSpec(memory_space=pltpu.VMEM)
    numer, denom, swa = call(
        local_kernel,
        [jax.ShapeDtypeStruct(lin_v.shape, jnp.float32)] * 3,
        [lax.axis_index(AXES).reshape(1), lin_qk, conved, swa_qkv, tail_kv],
        [pl.BlockSpec(memory_space=pltpu.SMEM)] + [whole] * 4,
    )
    return call(
        readout_kernel,
        jax.ShapeDtypeStruct(lin_v.shape, bf16),
        [
            stacked(halved),
            stacked(second),
            jnp.asarray(add_first),
            jnp.asarray(add_second),
            lin_qk,
            past,
            numer,
            denom,
            swa,
        ],
    )


def solution(mesh):
    return jax.shard_map(
        shards,
        mesh=mesh,
        in_specs=(P(AXES, None), P(AXES, None), P(), P(AXES, None)),
        out_specs=P(AXES, None),
        check_vma=False,
    )
```

```python
import functools

import jax
import jax.numpy as jnp
import numpy as np
from jax import lax
from jax.experimental import pallas as pl
from jax.experimental.pallas import tpu as pltpu
from jax.sharding import PartitionSpec as P

HEADS = 16
FEAT = 16
VHEAD = 64
SWA_HEADS = 8
SWA_HEAD = 128
WINDOW = 64

AXES = ("ctxouter", "ctxinner")
LANES = 128
PAIRS = HEADS // 2
QUADS = FEAT * (FEAT + 1) // 2
CONST = QUADS + FEAT
ROWS = 160
TAIL = 16
EXTRA = 8
VMEM_LIMIT = 48 * 1024 * 1024


NT = (((1,), (1,)), ((), ()))
NN = (((1,), (0,)), ((), ()))
BF16 = jnp.bfloat16


def dot(a, b, dims=NN):
    return lax.dot_general(a, b, dims, preferred_element_type=jnp.float32)


def iota(shape, dim):
    return lax.broadcasted_iota(jnp.int32, shape, dim)


def selector(feature, lane, second, halved=False):
    scale = FEAT ** (-0.25)
    quad = feature < QUADS
    entry = feature % FEAT
    if second:
        wanted = (feature + feature // FEAT) % FEAT
        return jnp.where((lane % FEAT == wanted) & quad, scale, 0.0)
    linear = (feature >= QUADS) & (feature < CONST)
    wanted = jnp.where(quad, entry, (feature - QUADS) % FEAT)
    weight = jnp.where((feature < FEAT) & halved, 0.5 * scale, scale)
    return jnp.where((lane % FEAT == wanted) & (quad | linear), weight, 0.0)


def adders(feature):
    first = jnp.where(feature == CONST, 1.0, 0.0)
    second = jnp.where((feature >= QUADS) & (feature <= CONST), 1.0, 0.0)
    return first, second


def head_mask(head, shape):
    place = iota(shape, 1)
    return (place >= head * FEAT) & (place < (head + 1) * FEAT)


def hi_lo(values):
    high = values.astype(BF16)
    return high, (values - high.astype(jnp.float32)).astype(BF16)


def convolved(value, tail, conv_ref, lanes):
    row_id = iota(value.shape, 0)
    result = conv_ref[0:1, lanes] * value
    for lag in range(1, conv_ref.shape[0]):
        shifted = pltpu.roll(value, lag, 0)
        for row in range(lag):
            source = TAIL - lag + row
            before = 0.0 if tail is None else tail[source : source + 1]
            shifted = jnp.where(row_id == row, before, shifted)
        result = result + conv_ref[lag : lag + 1, lanes] * shifted
    return result.astype(BF16)


def state_kernel(part, qk_hbm, v_hbm, conv_hbm, out_ref, key_ref, v_ref, conv_ref, sems):
    rows = v_ref.shape[0]
    taps = conv_ref.shape[0]
    width = HEADS * FEAT
    copies = [
        pltpu.make_async_copy(qk_hbm.at[:, width : 2 * width], key_ref, sems.at[0]),
        pltpu.make_async_copy(conv_hbm, conv_ref, sems.at[1]),
        pltpu.make_async_copy(v_hbm, v_ref, sems.at[2]),
    ]
    for copy in copies:
        copy.start()
    for copy in copies:
        copy.wait()
    key_t = (key_ref[...].astype(jnp.float32) * FEAT ** (-0.25)).T
    const_rows = jnp.where(iota((EXTRA, rows), 0) == 0, 1.0, 0.0)
    lane_id = iota((ROWS, LANES), 1)
    low_row = iota((EXTRA, LANES), 0)
    ones = jnp.ones((rows, LANES), BF16)
    half = FEAT // 2
    padded = (part + 7) // 8 * 8
    states = []
    norms = jnp.zeros((ROWS, LANES), jnp.float32)
    extras = []
    for pair in range(PAIRS):
        lanes = slice(pair * LANES, (pair + 1) * LANES)
        value = v_ref[:, lanes].astype(jnp.float32)
        conved = convolved(value, None, conv_ref, lanes)
        right = jnp.concatenate([conved, ones], axis=1)
        right = jnp.concatenate([right, right], axis=0)
        both = []
        for head in (2 * pair, 2 * pair + 1):
            x = key_t[head * FEAT : (head + 1) * FEAT]
            blocks = [x * x]
            for by in range(1, half):
                blocks.append(x * jnp.concatenate([x[by:], x[:by]], axis=0))
            blocks += [x[:half] * x[half:], x, const_rows]
            left = jnp.concatenate(hi_lo(jnp.concatenate(blocks, axis=0)), axis=1)
            result = dot(left, right)
            both.append(result[:, :LANES])
            norms = jnp.where(lane_id // 8 == head, result[:, LANES:], norms)
        states.append(jnp.where(lane_id < VHEAD, both[0], both[1]))
        group = pair * 2 * FEAT // LANES * LANES
        extra = jnp.zeros((EXTRA, LANES), jnp.float32)
        for row in range(taps - 1):
            share = jnp.zeros((1, LANES), jnp.float32)
            for lag in range(row + 1, taps):
                share = share + conv_ref[lag : lag + 1, lanes] * value[rows + row - lag : rows + row - lag + 1]
            extra = jnp.where(low_row == row, share, extra)
            first = key_ref[0:16, group : group + LANES].astype(jnp.float32)[row : row + 1]
            extra = jnp.where(low_row == taps - 1 + row, first, extra)
        extras.append(extra)
    norms_t = norms.T
    for pair in range(PAIRS):
        last = states[pair][CONST:]
        for place in range(2):
            at = 8 * (2 * pair + place)
            norm = norms_t[at : at + 8]
            rest = jnp.concatenate(
                [norm[:, LANES:], jnp.zeros((8, 2 * LANES - ROWS), jnp.float32)], axis=1
            )
            last = jnp.where(low_row == 1 + 2 * place, norm[:, :LANES], last)
            last = jnp.where(low_row == 2 + 2 * place, rest, last)
        state = jnp.concatenate([states[pair][:CONST], last], axis=0)
        for piece in range(ROWS // part):
            rows_of = [state[piece * part : (piece + 1) * part]]
            if padded != part:
                rows_of.append(jnp.zeros((padded - part, LANES), jnp.float32))
            message = jnp.concatenate(rows_of + [extras[pair]], axis=0)
            out_ref[pair * (ROWS // part) + piece] = message.astype(BF16)


def prefix_kernel(taps, place_ref, parts_ref, out_ref):
    blocks, held, _ = parts_ref.shape
    part = out_ref.shape[1]
    padded = held - EXTRA
    start = place_ref[0] * part
    head = start // ROWS * 2 % (LANES // FEAT)
    feature = start % ROWS + iota((padded, LANES), 0)
    lane = iota((padded, LANES), 1)
    one = selector(feature, lane, False)
    two = selector(feature, lane, True)
    add_one, add_two = adders(feature[:, 0:1])
    extras = parts_ref[:, padded:, :].astype(jnp.float32).reshape(blocks * EXTRA, LANES)
    extras_low = extras.astype(BF16)
    lefts = []
    rights = []
    for place in range(2):
        mine = lane // FEAT == head + place
        first = dot(jnp.where(mine, one, 0.0).astype(BF16), extras_low, NT) + add_one
        second = dot(jnp.where(mine, two, 0.0).astype(BF16), extras_low, NT) + add_two
        width = blocks * EXTRA
        shift = width - EXTRA - (taps - 1)
        lefts.append(pltpu.roll(first * second, shift, 1))
        upper = iota((width, LANES), 1) >= VHEAD
        rights.append(jnp.where(upper == (place == 1), extras, 0.0).astype(BF16))
    left = jnp.concatenate(lefts, axis=1)
    right = jnp.concatenate(rights, axis=0)
    column = iota(left.shape, 1) % (blocks * EXTRA)
    from_block = jnp.where(column % EXTRA < taps - 1, column // EXTRA + 1, blocks)

    def one_block(block, total):
        seen = jnp.where(from_block < block, left, 0.0).astype(BF16)
        result = total + dot(seen, right)
        out_ref[block] = result[:part].astype(BF16)
        return total + parts_ref[block].astype(jnp.float32)[:padded]

    total = jnp.zeros((padded, LANES), jnp.float32)
    if blocks <= 32:
        for block in range(blocks):
            total = one_block(block, total)
    else:
        lax.fori_loop(0, blocks, one_block, total)


def local_kernel(
    place_ref, qk_ref, v_ref, conv_ref, swa_ref, kv_ref, tail_ref, numer_ref, denom_ref, swa_out_ref, phi_ref
):
    rows = v_ref.shape[0]
    width = HEADS * FEAT
    query = qk_ref[:, :width]
    key = qk_ref[:, width : 2 * width]
    lane_id = iota((rows, LANES), 1)
    causal = iota((rows, rows), 1) <= iota((rows, rows), 0)
    ones = jnp.ones((rows, LANES), BF16)
    feature = iota((width, ROWS), 1)
    lane = iota((width, ROWS), 0)
    one = selector(feature, lane, False, halved=True).astype(BF16)
    two = selector(feature, lane, True).astype(BF16)
    add_one, add_two = adders(iota((8, ROWS), 1)[0:1])
    for pair in range(PAIRS):
        lanes = slice(pair * LANES, (pair + 1) * LANES)
        tail = tail_ref[:, lanes].astype(jnp.float32)
        tail = jnp.where(place_ref[0] == 0, 0.0, tail)
        conved = convolved(v_ref[:, lanes].astype(jnp.float32), tail, conv_ref, lanes)
        right = jnp.concatenate([conved, ones], axis=1)
        results = []
        for head in (2 * pair, 2 * pair + 1):
            own = jnp.where(head_mask(head, query.shape), query, jnp.zeros_like(query))
            score = dot(own, key, NT) * FEAT ** (-0.5)
            weight = 1.0 + score + 0.5 * score * score
            weight = jnp.where(causal, weight, 0.0).astype(BF16)
            results.append(dot(weight, right))
            high, low = hi_lo((dot(own, one) + add_one) * (dot(own, two) + add_two))
            phi_ref[head, :rows, :] = high
            phi_ref[head, rows:, :] = low
        lower = lane_id < VHEAD
        numer_ref[:, lanes] = jnp.where(lower, results[0][:, :LANES], results[1][:, :LANES])
        denom_ref[:, lanes] = jnp.where(lower, results[0][:, LANES:], results[1][:, LANES:])
    swa_width = SWA_HEADS * SWA_HEAD
    not_before = jnp.where(place_ref[0] == 0, WINDOW, 0)
    span = 2 * WINDOW
    place = iota((WINDOW, span), 1)
    row = iota((WINDOW, span), 0)
    inside = (place > row) & (place <= row + WINDOW)
    inside_first = inside & (place >= not_before)
    for head in range(SWA_HEADS):
        at = head * SWA_HEAD
        for step in range(rows // WINDOW):
            mine = slice(step * WINDOW, (step + 1) * WINDOW)
            window = slice((step - 1) * WINDOW, (step + 1) * WINDOW)
            both = []
            for start in (swa_width + at, 2 * swa_width + at):
                here = slice(start, start + SWA_HEAD)
                there = slice(start - swa_width, start - swa_width + SWA_HEAD)
                if step == 0:
                    both.append(jnp.concatenate([kv_ref[:, there], swa_ref[mine, here]], axis=0))
                else:
                    both.append(swa_ref[window, here])
            score = dot(swa_ref[mine, at : at + SWA_HEAD], both[0], NT) * SWA_HEAD ** (-0.5)
            score = jnp.where(inside_first if step == 0 else inside, score, -jnp.inf)
            expo = jnp.exp(score - jnp.max(score, axis=-1, keepdims=True))
            probs = (expo / jnp.sum(expo, axis=-1, keepdims=True)).astype(BF16)
            swa_out_ref[mine, at : at + SWA_HEAD] = dot(probs, both[1])


def readout_kernel(phi_ref, past_ref, numer_ref, denom_ref, swa_ref, out_ref):
    rows = out_ref.shape[0]
    lower = iota((rows, LANES), 1) < VHEAD
    norms = []
    for pair in range(PAIRS):
        last = past_ref[(pair + 1) * ROWS - 16 : (pair + 1) * ROWS, :].astype(jnp.float32)
        for place in range(2):
            at = 16 - (ROWS - CONST) + 1 + 2 * place
            norm = jnp.concatenate([last[at : at + 1], last[at + 1 : at + 2, : ROWS - LANES]], axis=1)
            norms.append(jnp.broadcast_to(norm, (8, ROWS)))
    norms = jnp.concatenate(norms, axis=0).T.astype(BF16)
    source = iota((LANES, LANES), 0)
    target = iota((LANES, LANES), 1)
    for pair in range(PAIRS):
        lanes = slice(pair * LANES, (pair + 1) * LANES)
        wanted = jnp.where(target < VHEAD, 16 * pair, 16 * pair + 8)
        spread = dot(norms, jnp.where(source == wanted, 1.0, 0.0).astype(BF16)).astype(BF16)
        right = jnp.concatenate([past_ref[pair * ROWS : (pair + 1) * ROWS, :], spread], axis=1)
        results = []
        for head in (2 * pair, 2 * pair + 1):
            result = dot(phi_ref[head], right)
            results.append(result[:rows] + result[rows:])
        numer = jnp.where(lower, results[0][:, :LANES], results[1][:, :LANES]) + numer_ref[:, lanes]
        denom = jnp.where(lower, results[0][:, LANES:], results[1][:, LANES:]) + denom_ref[:, lanes]
        out_ref[:, lanes] = (numer / denom + swa_ref[:, lanes]).astype(out_ref.dtype)


IN_VMEM = pl.BlockSpec(memory_space=pltpu.VMEM)
IN_SMEM = pl.BlockSpec(memory_space=pltpu.SMEM)
IN_PLACE = pl.BlockSpec(memory_space=pl.ANY)


def call(kernel, outs, args, specs, scratch=()):
    return pl.pallas_call(
        kernel,
        out_shape=outs,
        in_specs=specs,
        out_specs=jax.tree.map(lambda _: IN_VMEM, outs),
        scratch_shapes=scratch,
        compiler_params=pltpu.CompilerParams(vmem_limit_bytes=VMEM_LIMIT),
    )(*args)


def shards(lin_qk, lin_v, conv_w, swa_qkv):
    rows = lin_qk.shape[0]
    devices = lax.axis_size("ctxouter") * lax.axis_size("ctxinner")
    place = lax.axis_index(AXES).reshape(1)
    swa_width = swa_qkv.shape[1] // 3
    shift = [(i, i + 1) for i in range(devices - 1)]
    part = PAIRS * ROWS // devices
    held = (part + 7) // 8 * 8 + EXTRA
    shape = jax.ShapeDtypeStruct

    messages = call(
        functools.partial(state_kernel, part),
        shape((devices, held, LANES), BF16),
        [lin_qk, lin_v, conv_w],
        [IN_PLACE] * 3,
        [
            pltpu.VMEM((rows, HEADS * FEAT), BF16),
            pltpu.VMEM(lin_v.shape, BF16),
            pltpu.VMEM(conv_w.shape, jnp.float32),
            pltpu.SemaphoreType.DMA((3,)),
        ],
    )
    messages, lin_v, swa_qkv = lax.optimization_barrier((messages, lin_v, swa_qkv))
    parts = lax.all_to_all(messages, AXES, 0, 0, tiled=True)
    tail_kv = lax.ppermute(swa_qkv[rows - WINDOW :, swa_width:], AXES, shift)
    tail_v = lax.ppermute(lin_v[rows - TAIL :], AXES, shift)
    parts, tail_kv, tail_v = lax.optimization_barrier((parts, tail_kv, tail_v))
    past = call(
        functools.partial(prefix_kernel, conv_w.shape[0]),
        shape((devices, part, LANES), BF16),
        [place, parts],
        [IN_SMEM, IN_VMEM],
    )
    past, tail_kv, tail_v = lax.optimization_barrier((past, tail_kv, tail_v))
    past = lax.all_to_all(past, AXES, 0, 0, tiled=True).reshape(PAIRS * ROWS, LANES)
    numer, denom, swa, phi = call(
        local_kernel,
        [shape(lin_v.shape, jnp.float32)] * 3 + [shape((HEADS, 2 * rows, ROWS), BF16)],
        [place, lin_qk, lin_v, conv_w, swa_qkv, tail_kv, tail_v],
        [IN_SMEM] + [IN_VMEM] * 6,
    )
    return call(
        readout_kernel,
        shape(lin_v.shape, BF16),
        [phi, past, numer, denom, swa],
        [IN_VMEM] * 5,
    )


def solution(mesh):
    return jax.shard_map(
        shards,
        mesh=mesh,
        in_specs=(P(AXES, None), P(AXES, None), P(), P(AXES, None)),
        out_specs=P(AXES, None),
        check_vma=False,
    )
```

```python
import functools

import jax
import jax.numpy as jnp
import numpy as np
from jax import lax
from jax.experimental import pallas as pl
from jax.experimental.pallas import tpu as pltpu
from jax.sharding import PartitionSpec as P

HEADS = 16
FEAT = 16
VHEAD = 64
SWA_HEADS = 8
SWA_HEAD = 128
WINDOW = 64

AXES = ("ctxouter", "ctxinner")
LANES = 128
PAIRS = HEADS // 2
QUADS = FEAT * (FEAT + 1) // 2
CONST = QUADS + FEAT
ROWS = 160
TAIL = 16
EXTRA = 8


NT = (((1,), (1,)), ((), ()))
NN = (((1,), (0,)), ((), ()))
BF16 = jnp.bfloat16


def dot(a, b, dims=NN):
    return lax.dot_general(a, b, dims, preferred_element_type=jnp.float32)


def iota(shape, dim):
    return lax.broadcasted_iota(jnp.int32, shape, dim)


def selector(feature, lane, second, halved=False):
    scale = FEAT ** (-0.25)
    quad = feature < QUADS
    entry = feature % FEAT
    if second:
        wanted = (feature + feature // FEAT) % FEAT
        return jnp.where((lane % FEAT == wanted) & quad, scale, 0.0)
    linear = (feature >= QUADS) & (feature < CONST)
    wanted = jnp.where(quad, entry, (feature - QUADS) % FEAT)
    weight = jnp.where((feature < FEAT) & halved, 0.5 * scale, scale)
    return jnp.where((lane % FEAT == wanted) & (quad | linear), weight, 0.0)


def adders(feature):
    first = jnp.where(feature == CONST, 1.0, 0.0)
    second = jnp.where((feature >= QUADS) & (feature <= CONST), 1.0, 0.0)
    return first, second


def head_mask(head, shape):
    place = iota(shape, 1)
    return (place >= head * FEAT) & (place < (head + 1) * FEAT)


def hi_lo(values):
    high = values.astype(BF16)
    return high, (values - high.astype(jnp.float32)).astype(BF16)


def convolved(value, tail, conv_ref, lanes):
    row_id = iota(value.shape, 0)
    result = conv_ref[0:1, lanes] * value
    for lag in range(1, conv_ref.shape[0]):
        shifted = pltpu.roll(value, lag, 0)
        for row in range(lag):
            source = TAIL - lag + row
            before = 0.0 if tail is None else tail[source : source + 1]
            shifted = jnp.where(row_id == row, before, shifted)
        result = result + conv_ref[lag : lag + 1, lanes] * shifted
    return result.astype(BF16)


def state_kernel(part, qk_hbm, v_hbm, conv_hbm, out_ref, key_ref, v_ref, conv_ref, sems):
    rows = v_ref.shape[0]
    taps = conv_ref.shape[0]
    width = HEADS * FEAT
    copies = [
        pltpu.make_async_copy(qk_hbm.at[:, width : 2 * width], key_ref, sems.at[0]),
        pltpu.make_async_copy(conv_hbm, conv_ref, sems.at[1]),
        pltpu.make_async_copy(v_hbm, v_ref, sems.at[2]),
    ]
    for copy in copies:
        copy.start()
    for copy in copies:
        copy.wait()
    key_t = (key_ref[...].astype(jnp.float32) * FEAT ** (-0.25)).T
    const_rows = jnp.where(iota((EXTRA, rows), 0) == 0, 1.0, 0.0)
    lane_id = iota((ROWS, LANES), 1)
    low_row = iota((EXTRA, LANES), 0)
    ones = jnp.ones((rows, LANES), BF16)
    half = FEAT // 2
    padded = (part + 7) // 8 * 8
    states = []
    norms = jnp.zeros((ROWS, LANES), jnp.float32)
    extras = []
    for pair in range(PAIRS):
        lanes = slice(pair * LANES, (pair + 1) * LANES)
        value = v_ref[:, lanes].astype(jnp.float32)
        conved = convolved(value, None, conv_ref, lanes)
        right = jnp.concatenate([conved, ones], axis=1)
        right = jnp.concatenate([right, right], axis=0)
        both = []
        for head in (2 * pair, 2 * pair + 1):
            x = key_t[head * FEAT : (head + 1) * FEAT]
            blocks = [x * x]
            for by in range(1, half):
                blocks.append(x * jnp.concatenate([x[by:], x[:by]], axis=0))
            blocks += [x[:half] * x[half:], x, const_rows]
            left = jnp.concatenate(hi_lo(jnp.concatenate(blocks, axis=0)), axis=1)
            result = dot(left, right)
            both.append(result[:, :LANES])
            norms = jnp.where(lane_id // 8 == head, result[:, LANES:], norms)
        states.append(jnp.where(lane_id < VHEAD, both[0], both[1]))
        group = pair * 2 * FEAT // LANES * LANES
        extra = jnp.zeros((EXTRA, LANES), jnp.float32)
        for row in range(taps - 1):
            share = jnp.zeros((1, LANES), jnp.float32)
            for lag in range(row + 1, taps):
                share = share + conv_ref[lag : lag + 1, lanes] * value[rows + row - lag : rows + row - lag + 1]
            extra = jnp.where(low_row == row, share, extra)
            first = key_ref[0:16, group : group + LANES].astype(jnp.float32)[row : row + 1]
            extra = jnp.where(low_row == taps - 1 + row, first, extra)
        extras.append(extra)
    norms_t = norms.T
    for pair in range(PAIRS):
        last = states[pair][CONST:]
        for place in range(2):
            at = 8 * (2 * pair + place)
            norm = norms_t[at : at + 8]
            rest = jnp.concatenate(
                [norm[:, LANES:], jnp.zeros((8, 2 * LANES - ROWS), jnp.float32)], axis=1
            )
            last = jnp.where(low_row == 1 + 2 * place, norm[:, :LANES], last)
            last = jnp.where(low_row == 2 + 2 * place, rest, last)
        state = jnp.concatenate([states[pair][:CONST], last], axis=0)
        for piece in range(ROWS // part):
            rows_of = [state[piece * part : (piece + 1) * part]]
            if padded != part:
                rows_of.append(jnp.zeros((padded - part, LANES), jnp.float32))
            message = jnp.concatenate(rows_of + [extras[pair]], axis=0)
            out_ref[pair * (ROWS // part) + piece] = message.astype(BF16)


def prefix_kernel(taps, place_ref, parts_ref, out_ref):
    blocks, held, _ = parts_ref.shape
    part = out_ref.shape[1]
    padded = held - EXTRA
    start = place_ref[0] * part
    head = start // ROWS * 2 % (LANES // FEAT)
    feature = start % ROWS + iota((padded, LANES), 0)
    lane = iota((padded, LANES), 1)
    one = selector(feature, lane, False)
    two = selector(feature, lane, True)
    add_one, add_two = adders(feature[:, 0:1])
    extras = parts_ref[:, padded:, :].astype(jnp.float32).reshape(blocks * EXTRA, LANES)
    extras_low = extras.astype(BF16)
    lefts = []
    rights = []
    for place in range(2):
        mine = lane // FEAT == head + place
        first = dot(jnp.where(mine, one, 0.0).astype(BF16), extras_low, NT) + add_one
        second = dot(jnp.where(mine, two, 0.0).astype(BF16), extras_low, NT) + add_two
        width = blocks * EXTRA
        shift = width - EXTRA - (taps - 1)
        lefts.append(pltpu.roll(first * second, shift, 1))
        upper = iota((width, LANES), 1) >= VHEAD
        rights.append(jnp.where(upper == (place == 1), extras, 0.0).astype(BF16))
    left = jnp.concatenate(lefts, axis=1)
    right = jnp.concatenate(rights, axis=0)
    column = iota(left.shape, 1) % (blocks * EXTRA)
    from_block = jnp.where(column % EXTRA < taps - 1, column // EXTRA + 1, blocks)

    def one_block(block, total):
        seen = jnp.where(from_block < block, left, 0.0).astype(BF16)
        result = total + dot(seen, right)
        out_ref[block] = result[:part].astype(BF16)
        return total + parts_ref[block].astype(jnp.float32)[:padded]

    total = jnp.zeros((padded, LANES), jnp.float32)
    if blocks <= 32:
        for block in range(blocks):
            total = one_block(block, total)
    else:
        lax.fori_loop(0, blocks, one_block, total)


def local_kernel(
    place_ref, qk_hbm, v_hbm, conv_hbm, swa_hbm, kv_hbm, tail_hbm,
    numer_hbm, denom_hbm, swa_out_hbm, phi_hbm,
    qk_ref, v_ref, conv_ref, swa_ref, kv_ref, tail_ref,
    numer_ref, denom_ref, swa_out_ref, phi_ref, sems_in, sems_out,
):
    pairs = (
        (qk_hbm, qk_ref), (v_hbm, v_ref), (conv_hbm, conv_ref), (tail_hbm, tail_ref),
        (swa_hbm, swa_ref), (kv_hbm, kv_ref),
    )
    copies = [pltpu.make_async_copy(a, b, sems_in.at[i]) for i, (a, b) in enumerate(pairs)]
    for copy in copies:
        copy.start()
    for copy in copies[:4]:
        copy.wait()
    results_out = []

    def send(here, there):
        copy = pltpu.make_async_copy(here, there, sems_out.at[len(results_out)])
        copy.start()
        results_out.append(copy)

    rows = v_ref.shape[0]
    width = HEADS * FEAT
    query = qk_ref[:, :width]
    key = qk_ref[:, width : 2 * width]
    lane_id = iota((rows, LANES), 1)
    causal = iota((rows, rows), 1) <= iota((rows, rows), 0)
    ones = jnp.ones((rows, LANES), BF16)
    feature = iota((width, ROWS), 1)
    lane = iota((width, ROWS), 0)
    one = selector(feature, lane, False, halved=True).astype(BF16)
    two = selector(feature, lane, True).astype(BF16)
    add_one, add_two = adders(iota((8, ROWS), 1)[0:1])
    for pair in range(PAIRS):
        lanes = slice(pair * LANES, (pair + 1) * LANES)
        tail = tail_ref[:, lanes].astype(jnp.float32)
        tail = jnp.where(place_ref[0] == 0, 0.0, tail)
        conved = convolved(v_ref[:, lanes].astype(jnp.float32), tail, conv_ref, lanes)
        right = jnp.concatenate([conved, ones], axis=1)
        results = []
        for head in (2 * pair, 2 * pair + 1):
            own = jnp.where(head_mask(head, query.shape), query, jnp.zeros_like(query))
            score = dot(own, key, NT) * FEAT ** (-0.5)
            weight = 1.0 + score + 0.5 * score * score
            weight = jnp.where(causal, weight, 0.0).astype(BF16)
            results.append(dot(weight, right))
            high, low = hi_lo((dot(own, one) + add_one) * (dot(own, two) + add_two))
            phi_ref[head, :rows, :] = high
            phi_ref[head, rows:, :] = low
        lower = lane_id < VHEAD
        numer_ref[:, lanes] = jnp.where(lower, results[0][:, :LANES], results[1][:, :LANES])
        denom_ref[:, lanes] = jnp.where(lower, results[0][:, LANES:], results[1][:, LANES:])
        send(phi_ref.at[2 * pair : 2 * pair + 2], phi_hbm.at[2 * pair : 2 * pair + 2])
    send(numer_ref, numer_hbm)
    send(denom_ref, denom_hbm)
    for copy in copies[4:]:
        copy.wait()
    swa_width = SWA_HEADS * SWA_HEAD
    not_before = jnp.where(place_ref[0] == 0, WINDOW, 0)
    span = 2 * WINDOW
    place = iota((WINDOW, span), 1)
    row = iota((WINDOW, span), 0)
    inside = (place > row) & (place <= row + WINDOW)
    inside_first = inside & (place >= not_before)
    for head in range(SWA_HEADS):
        at = head * SWA_HEAD
        for step in range(rows // WINDOW):
            mine = slice(step * WINDOW, (step + 1) * WINDOW)
            window = slice((step - 1) * WINDOW, (step + 1) * WINDOW)
            both = []
            for start in (swa_width + at, 2 * swa_width + at):
                here = slice(start, start + SWA_HEAD)
                there = slice(start - swa_width, start - swa_width + SWA_HEAD)
                if step == 0:
                    both.append(jnp.concatenate([kv_ref[:, there], swa_ref[mine, here]], axis=0))
                else:
                    both.append(swa_ref[window, here])
            score = dot(swa_ref[mine, at : at + SWA_HEAD], both[0], NT) * SWA_HEAD ** (-0.5)
            score = jnp.where(inside_first if step == 0 else inside, score, -jnp.inf)
            expo = jnp.exp(score - jnp.max(score, axis=-1, keepdims=True))
            probs = (expo / jnp.sum(expo, axis=-1, keepdims=True)).astype(BF16)
            swa_out_ref[mine, at : at + SWA_HEAD] = dot(probs, both[1])
    send(swa_out_ref, swa_out_hbm)
    for copy in results_out:
        copy.wait()


def readout_kernel(
    past_hbm, phi_hbm, numer_hbm, denom_hbm, swa_hbm, out_ref,
    past_ref, phi_ref, numer_ref, denom_ref, swa_ref, sems,
):
    copies = [
        pltpu.make_async_copy(
            phi_hbm.at[2 * pair : 2 * pair + 2], phi_ref.at[2 * pair : 2 * pair + 2], sems.at[pair]
        )
        for pair in range(PAIRS)
    ]
    shares = ((past_hbm, past_ref), (numer_hbm, numer_ref), (denom_hbm, denom_ref), (swa_hbm, swa_ref))
    rest = [pltpu.make_async_copy(a, b, sems.at[PAIRS + i]) for i, (a, b) in enumerate(shares)]
    for copy in rest[:1] + copies[:1] + rest[1:] + copies[1:]:
        copy.start()
    rest[0].wait()
    rows = out_ref.shape[0]
    lower = iota((rows, LANES), 1) < VHEAD
    norms = []
    for pair in range(PAIRS):
        last = past_ref[(pair + 1) * ROWS - 16 : (pair + 1) * ROWS, :].astype(jnp.float32)
        for place in range(2):
            at = 16 - (ROWS - CONST) + 1 + 2 * place
            norm = jnp.concatenate([last[at : at + 1], last[at + 1 : at + 2, : ROWS - LANES]], axis=1)
            norms.append(jnp.broadcast_to(norm, (8, ROWS)))
    norms = jnp.concatenate(norms, axis=0).T.astype(BF16)
    source = iota((LANES, LANES), 0)
    target = iota((LANES, LANES), 1)
    for pair in range(PAIRS):
        lanes = slice(pair * LANES, (pair + 1) * LANES)
        wanted = jnp.where(target < VHEAD, 16 * pair, 16 * pair + 8)
        spread = dot(norms, jnp.where(source == wanted, 1.0, 0.0).astype(BF16)).astype(BF16)
        right = jnp.concatenate([past_ref[pair * ROWS : (pair + 1) * ROWS, :], spread], axis=1)
        results = []
        copies[pair].wait()
        for copy in rest[1:] if pair == 0 else ():
            copy.wait()
        for head in (2 * pair, 2 * pair + 1):
            result = dot(phi_ref[head], right)
            results.append(result[:rows] + result[rows:])
        numer = jnp.where(lower, results[0][:, :LANES], results[1][:, :LANES]) + numer_ref[:, lanes]
        denom = jnp.where(lower, results[0][:, LANES:], results[1][:, LANES:]) + denom_ref[:, lanes]
        out_ref[:, lanes] = (numer / denom + swa_ref[:, lanes]).astype(out_ref.dtype)


IN_VMEM = pl.BlockSpec(memory_space=pltpu.VMEM)
IN_SMEM = pl.BlockSpec(memory_space=pltpu.SMEM)
IN_HBM = pl.BlockSpec(memory_space=pltpu.HBM)


def call(kernel, outs, args, specs, out_spec, scratch=(), grant=60):
    return pl.pallas_call(
        kernel,
        out_shape=outs,
        in_specs=specs,
        out_specs=jax.tree.map(lambda _: out_spec, outs),
        scratch_shapes=scratch,
        compiler_params=pltpu.CompilerParams(vmem_limit_bytes=grant * 1024 * 1024),
    )(*args)


def like(*arrays):
    return [pltpu.VMEM(a.shape, a.dtype) for a in arrays]


def shards(lin_qk, lin_v, conv_w, swa_qkv):
    rows = lin_qk.shape[0]
    devices = lax.axis_size("ctxouter") * lax.axis_size("ctxinner")
    place = lax.axis_index(AXES).reshape(1)
    swa_width = swa_qkv.shape[1] // 3
    shift = [(i, i + 1) for i in range(devices - 1)]
    part = PAIRS * ROWS // devices
    held = (part + 7) // 8 * 8 + EXTRA
    shape = jax.ShapeDtypeStruct
    sems = pltpu.SemaphoreType.DMA

    messages = call(
        functools.partial(state_kernel, part),
        shape((devices, held, LANES), BF16),
        [lin_qk, lin_v, conv_w],
        [IN_HBM] * 3,
        IN_VMEM,
        [pltpu.VMEM((rows, HEADS * FEAT), BF16)] + like(lin_v, conv_w) + [sems((3,))],
    )
    messages, lin_v, swa_qkv = lax.optimization_barrier((messages, lin_v, swa_qkv))
    parts = lax.all_to_all(messages, AXES, 0, 0, tiled=True)
    tail_kv = lax.ppermute(swa_qkv[rows - WINDOW :, swa_width:], AXES, shift)
    tail_v = lax.ppermute(lin_v[rows - TAIL :], AXES, shift)
    parts, tail_kv, tail_v = lax.optimization_barrier((parts, tail_kv, tail_v))
    past = call(
        functools.partial(prefix_kernel, conv_w.shape[0]),
        shape((devices, part, LANES), BF16),
        [place, parts],
        [IN_SMEM, IN_VMEM],
        IN_VMEM,
        grant=16,
    )
    past, tail_kv, tail_v = lax.optimization_barrier((past, tail_kv, tail_v))
    past = lax.all_to_all(past, AXES, 0, 0, tiled=True).reshape(PAIRS * ROWS, LANES)
    wide = shape(lin_v.shape, jnp.float32)
    phis = shape((HEADS, 2 * rows, ROWS), BF16)
    numer, denom, swa, phi = call(
        local_kernel,
        [wide, wide, wide, phis],
        [place, lin_qk, lin_v, conv_w, swa_qkv, tail_kv, tail_v],
        [IN_SMEM] + [IN_HBM] * 6,
        IN_HBM,
        like(lin_qk, lin_v, conv_w, swa_qkv, tail_kv, tail_v, wide, wide, wide, phis)
        + [sems((6,)), sems((PAIRS + 3,))],
    )
    return call(
        readout_kernel,
        shape(lin_v.shape, BF16),
        [past, phi, numer, denom, swa],
        [IN_HBM] * 5,
        IN_VMEM,
        like(past, phis, wide, wide, wide) + [sems((PAIRS + 4,))],
    )


def solution(mesh):
    return jax.shard_map(
        shards,
        mesh=mesh,
        in_specs=(P(AXES, None), P(AXES, None), P(), P(AXES, None)),
        out_specs=P(AXES, None),
        check_vma=False,
    )
```

```python
import functools

import jax
import jax.numpy as jnp
import numpy as np
from jax import lax
from jax.experimental import pallas as pl
from jax.experimental.pallas import tpu as pltpu
from jax.sharding import PartitionSpec as P

HEADS = 16
FEAT = 16
VHEAD = 64
SWA_HEADS = 8
SWA_HEAD = 128
WINDOW = 64

AXES = ("ctxouter", "ctxinner")
SPLIT = ("outer", "z", "core")
CHIPS = ("outer", "z")
LANES = 128
PAIRS = HEADS // 2
QUADS = FEAT * (FEAT + 1) // 2
CONST = QUADS + FEAT
ROWS = 160
TAIL = 16
EXTRA = 8


NT = (((1,), (1,)), ((), ()))
NN = (((1,), (0,)), ((), ()))
BF16 = jnp.bfloat16


def dot(a, b, dims=NN):
    return lax.dot_general(a, b, dims, preferred_element_type=jnp.float32)


def iota(shape, dim):
    return lax.broadcasted_iota(jnp.int32, shape, dim)


def selector(feature, lane, second, halved=False):
    scale = FEAT ** (-0.25)
    quad = feature < QUADS
    entry = feature % FEAT
    if second:
        wanted = (feature + feature // FEAT) % FEAT
        return jnp.where((lane % FEAT == wanted) & quad, scale, 0.0)
    linear = (feature >= QUADS) & (feature < CONST)
    wanted = jnp.where(quad, entry, (feature - QUADS) % FEAT)
    weight = jnp.where((feature < FEAT) & halved, 0.5 * scale, scale)
    return jnp.where((lane % FEAT == wanted) & (quad | linear), weight, 0.0)


def adders(feature):
    first = jnp.where(feature == CONST, 1.0, 0.0)
    second = jnp.where((feature >= QUADS) & (feature <= CONST), 1.0, 0.0)
    return first, second


def head_mask(head, shape):
    place = iota(shape, 1)
    return (place >= head * FEAT) & (place < (head + 1) * FEAT)


def hi_lo(values):
    high = values.astype(BF16)
    return high, (values - high.astype(jnp.float32)).astype(BF16)


def convolved(value, tail, conv_ref, lanes):
    row_id = iota(value.shape, 0)
    result = conv_ref[0:1, lanes] * value
    for lag in range(1, conv_ref.shape[0]):
        shifted = pltpu.roll(value, lag, 0)
        for row in range(lag):
            source = TAIL - lag + row
            before = 0.0 if tail is None else tail[source : source + 1]
            shifted = jnp.where(row_id == row, before, shifted)
        result = result + conv_ref[lag : lag + 1, lanes] * shifted
    return result.astype(BF16)


def state_kernel(
    part, qk_hbm, v_hbm, other_qk_hbm, other_v_hbm, conv_hbm, swa_hbm, out_ref, tails_ref,
    key_ref, v_ref, conv_ref, sems,
):
    rows, wide = v_hbm.shape
    taps = conv_ref.shape[0]
    core = lax.axis_index("core")
    mine = pl.ds(pl.multiple_of(core * (wide // 2), wide // 2), wide // 2)
    keys = pl.ds(pl.multiple_of(HEADS * FEAT + core * LANES, LANES), LANES)
    here = pl.ds(pl.multiple_of(core * rows, rows), rows)
    there = pl.ds(pl.multiple_of((1 - core) * rows, rows), rows)
    copies = [
        pltpu.make_async_copy(qk_hbm.at[:, keys], key_ref.at[here, :], sems.at[0]),
        pltpu.make_async_copy(other_qk_hbm.at[:, keys], key_ref.at[there, :], sems.at[1]),
        pltpu.make_async_copy(conv_hbm.at[:, mine], conv_ref, sems.at[2]),
        pltpu.make_async_copy(v_hbm.at[:, mine], v_ref.at[here, :], sems.at[3]),
        pltpu.make_async_copy(other_v_hbm.at[:, mine], v_ref.at[there, :], sems.at[4]),
        pltpu.make_async_copy(
            swa_hbm.at[rows - WINDOW :, tails_ref.shape[1] // 2 :], tails_ref.at[:WINDOW, :], sems.at[5]
        ),
        pltpu.make_async_copy(v_hbm.at[rows - TAIL :, :], tails_ref.at[WINDOW:, :wide], sems.at[6]),
    ]
    for copy in copies:
        copy.start()
    for copy in copies[:2]:
        copy.wait()
    tokens = 2 * rows
    key_t = (key_ref[...].astype(jnp.float32) * FEAT ** (-0.25)).T
    const_rows = jnp.where(iota((EXTRA, tokens), 0) == 0, 1.0, 0.0)
    lane_id = iota((ROWS, LANES), 1)
    low_row = iota((EXTRA, LANES), 0)
    ones = jnp.ones((tokens, LANES), BF16)
    half = FEAT // 2
    padded = (part + 7) // 8 * 8
    lefts = []
    for head in range(HEADS // 2):
        x = key_t[head * FEAT : (head + 1) * FEAT]
        blocks = [x * x]
        for by in range(1, half):
            blocks.append(x * jnp.concatenate([x[by:], x[:by]], axis=0))
        blocks += [x[:half] * x[half:], x, const_rows]
        lefts.append(jnp.concatenate(hi_lo(jnp.concatenate(blocks, axis=0)), axis=1))
    first_keys = key_ref[0:16].astype(jnp.float32)
    for copy in copies[2:5]:
        copy.wait()
    states = []
    extras = []
    norms = jnp.zeros((ROWS, LANES), jnp.float32)
    for pair in range(PAIRS // 2):
        lanes = slice(pair * LANES, (pair + 1) * LANES)
        value = v_ref[:, lanes].astype(jnp.float32)
        conved = convolved(value, None, conv_ref, lanes)
        right = jnp.concatenate([conved, ones], axis=1)
        right = jnp.concatenate([right, right], axis=0)
        both = []
        for head in (2 * pair, 2 * pair + 1):
            result = dot(lefts[head], right)
            both.append(result[:, :LANES])
            norms = jnp.where(lane_id // 8 == head, result[:, LANES:], norms)
        states.append(jnp.where(lane_id < VHEAD, both[0], both[1]))
        extra = jnp.zeros((EXTRA, LANES), jnp.float32)
        for row in range(taps - 1):
            share = jnp.zeros((1, LANES), jnp.float32)
            for lag in range(row + 1, taps):
                at = tokens + row - lag
                share = share + conv_ref[lag : lag + 1, lanes] * value[at : at + 1]
            extra = jnp.where(low_row == row, share, extra)
            extra = jnp.where(low_row == taps - 1 + row, first_keys[row : row + 1], extra)
        extras.append(extra)
    norms_t = norms.T
    for pair in range(PAIRS // 2):
        last = states[pair][CONST:]
        for place in range(2):
            at = 8 * (2 * pair + place)
            norm = norms_t[at : at + 8]
            rest = jnp.concatenate(
                [norm[:, LANES:], jnp.zeros((8, 2 * LANES - ROWS), jnp.float32)], axis=1
            )
            last = jnp.where(low_row == 1 + 2 * place, norm[:, :LANES], last)
            last = jnp.where(low_row == 2 + 2 * place, rest, last)
        state = jnp.concatenate([states[pair][:CONST], last], axis=0)
        for piece in range(ROWS // part):
            rows_of = [state[piece * part : (piece + 1) * part]]
            if padded != part:
                rows_of.append(jnp.zeros((padded - part, LANES), jnp.float32))
            message = jnp.concatenate(rows_of + [extras[pair]], axis=0)
            out_ref[pair * (ROWS // part) + piece] = message.astype(BF16)
    for copy in copies[5:]:
        copy.wait()


def prefix_kernel(taps, parts_ref, out_ref):
    chips, held, _ = parts_ref.shape
    part = out_ref.shape[1]
    padded = held - EXTRA
    width = chips * EXTRA
    chip, core = lax.axis_index(CHIPS), lax.axis_index("core")
    start = core * (ROWS * PAIRS // 2) + chip * part
    head = start // ROWS * 2 % (LANES // FEAT)
    feature = start % ROWS + iota((padded, LANES), 0)
    lane = iota((padded, LANES), 1)
    one = selector(feature, lane, False)
    two = selector(feature, lane, True)
    add_one, add_two = adders(feature[:, 0:1])
    extras = parts_ref[:, padded:, :].astype(jnp.float32).reshape(width, LANES)
    extras_low = extras.astype(BF16)
    upper = iota((width, LANES), 1) >= VHEAD
    lefts = []
    rights = []
    for place in range(2):
        mine = lane // FEAT == head + place
        first = dot(jnp.where(mine, one, 0.0).astype(BF16), extras_low, NT) + add_one
        second = dot(jnp.where(mine, two, 0.0).astype(BF16), extras_low, NT) + add_two
        lefts.append(pltpu.roll(first * second, width - EXTRA - (taps - 1), 1))
        rights.append(jnp.where(upper == (place == 1), extras, 0.0).astype(BF16))
    left = jnp.concatenate(lefts, axis=1)
    right = jnp.concatenate(rights, axis=0)
    column = iota(left.shape, 1) % width
    to_chip = jnp.where(column % EXTRA < taps - 1, column // EXTRA + 1, chips)

    def one_chip(chip, total):
        seen = jnp.where(to_chip <= chip, left, 0.0).astype(BF16)
        result = total + dot(seen, right)
        out_ref[chip] = result[:part].astype(BF16)
        return total + parts_ref[chip].astype(jnp.float32)[:padded]

    total = jnp.zeros((padded, LANES), jnp.float32)
    if chips <= 32:
        for chip in range(chips):
            total = one_chip(chip, total)
    else:
        lax.fori_loop(0, chips, one_chip, total)


def local_kernel(
    qk_ref, v_ref, conv_ref, swa_ref, tails_ref, other_qk_ref, other_v_ref,
    numer_ref, denom_ref, swa_out_ref,
):
    rows = v_ref.shape[0]
    taps = conv_ref.shape[0]
    width = HEADS * FEAT
    core = lax.axis_index("core")
    second = core == 1
    first_block = (lax.axis_index(CHIPS) == 0) & (core == 0)
    query = qk_ref[:, :width]
    key = qk_ref[:, width : 2 * width]
    lower = iota((rows, LANES), 1) < VHEAD
    causal = iota((rows, rows), 1) <= iota((rows, rows), 0)
    row_id = iota((rows, LANES), 0)
    ones = jnp.ones((rows, LANES), BF16)
    counted = jnp.where(second, ones, jnp.zeros_like(ones))
    more_key = jnp.where(second, other_qk_ref[:, width : 2 * width], key)
    all_keys = jnp.concatenate([key, more_key], axis=0)
    allowed = jnp.concatenate([causal, causal | True], axis=1)
    group_heads = 4
    for group in range(0, HEADS, group_heads):
        own = jnp.concatenate(
            [
                jnp.where(head_mask(head, query.shape), query, jnp.zeros_like(query))
                for head in range(group, group + group_heads)
            ],
            axis=0,
        )
        score = dot(own, all_keys, NT) * FEAT ** (-0.5)
        weight = 1.0 + score + 0.5 * score * score
        weight = jnp.where(jnp.concatenate([allowed] * group_heads, axis=0), weight, 0.0).astype(BF16)
        for at in range(group_heads // 2):
            pair = group // 2 + at
            lanes = slice(pair * LANES, (pair + 1) * LANES)
            tail = jnp.where(first_block, 0.0, tails_ref[WINDOW:, lanes].astype(jnp.float32))
            conved = convolved(v_ref[:, lanes].astype(jnp.float32), tail, conv_ref, lanes)
            before = convolved(other_v_ref[:, lanes].astype(jnp.float32), None, conv_ref, lanes)
            shares = jnp.zeros((rows, LANES), jnp.float32)
            for row in range(taps - 1):
                share = jnp.zeros((1, LANES), jnp.float32)
                for lag in range(row + 1, taps):
                    at_row = TAIL + row - lag
                    share = share + conv_ref[lag : lag + 1, lanes] * tail[at_row : at_row + 1]
                shares = jnp.where(row_id == row, -share, shares)
            before = jnp.where(second, before, shares.astype(BF16))
            right = jnp.concatenate([conved, ones], axis=1)
            right = jnp.concatenate([right, jnp.concatenate([before, counted], axis=1)], axis=0)
            result = dot(weight[2 * at * rows : (2 * at + 2) * rows], right)
            top, bottom = result[:rows], result[rows:]
            numer_ref[:, lanes] = jnp.where(lower, top[:, :LANES], bottom[:, :LANES])
            denom_ref[:, lanes] = jnp.where(lower, top[:, LANES:], bottom[:, LANES:])
    swa_width = SWA_HEADS * SWA_HEAD
    not_before = jnp.where(first_block, WINDOW, 0)
    span = 2 * WINDOW
    place = iota((WINDOW, span), 1)
    row = iota((WINDOW, span), 0)
    inside = (place > row) & (place <= row + WINDOW)
    inside_first = inside & (place >= not_before)
    for step in range(rows // WINDOW):
        mine = slice(step * WINDOW, (step + 1) * WINDOW)
        window = slice((step - 1) * WINDOW, (step + 1) * WINDOW)

        def around(head, start):
            here = slice(start + head * SWA_HEAD, start + (head + 1) * SWA_HEAD)
            if step:
                return swa_ref[window, here]
            there = slice(here.start - swa_width, here.stop - swa_width)
            return jnp.concatenate([tails_ref[:WINDOW, there], swa_ref[mine, here]], axis=0)

        scores = []
        for head in range(SWA_HEADS):
            own = swa_ref[mine, head * SWA_HEAD : (head + 1) * SWA_HEAD]
            score = dot(own, around(head, swa_width), NT) * SWA_HEAD ** (-0.5)
            scores.append(jnp.where(inside if step else inside_first, score, -jnp.inf))
        scores = jnp.concatenate(scores, axis=0)
        expo = jnp.exp(scores - jnp.max(scores, axis=-1, keepdims=True))
        probs = (expo / jnp.sum(expo, axis=-1, keepdims=True)).astype(BF16)
        for head in range(SWA_HEADS):
            own = probs[head * WINDOW : (head + 1) * WINDOW]
            swa_out_ref[mine, head * SWA_HEAD : (head + 1) * SWA_HEAD] = dot(
                own, around(head, 2 * swa_width)
            )


def readout_kernel(qk_ref, numer_ref, denom_ref, swa_ref, here_ref, there_ref, out_ref, past_ref):
    core = lax.axis_index("core")
    rows = out_ref.shape[0]
    half = PAIRS // 2 * ROWS
    past_ref[pl.ds(pl.multiple_of(core * half, half), half), :] = here_ref[...]
    past_ref[pl.ds(pl.multiple_of((1 - core) * half, half), half), :] = there_ref[...]
    lower = iota((rows, LANES), 1) < VHEAD
    query = qk_ref[:, : HEADS * FEAT]
    feature = iota((HEADS * FEAT, ROWS), 1)
    lane = iota((HEADS * FEAT, ROWS), 0)
    one = selector(feature, lane, False, halved=True).astype(BF16)
    two = selector(feature, lane, True).astype(BF16)
    add_one, add_two = adders(iota((8, ROWS), 1)[0:1])
    norms = []
    for pair in range(PAIRS):
        last = past_ref[(pair + 1) * ROWS - 16 : (pair + 1) * ROWS, :].astype(jnp.float32)
        for place in range(2):
            at = 16 - (ROWS - CONST) + 1 + 2 * place
            norm = jnp.concatenate([last[at : at + 1], last[at + 1 : at + 2, : ROWS - LANES]], axis=1)
            norms.append(jnp.broadcast_to(norm, (8, ROWS)))
    norms = jnp.concatenate(norms, axis=0).T.astype(BF16)
    source = iota((LANES, LANES), 0)
    target = iota((LANES, LANES), 1)
    group_heads = 8
    for group in range(0, HEADS, group_heads):
        own = jnp.concatenate(
            [
                jnp.where(head_mask(head, query.shape), query, jnp.zeros_like(query))
                for head in range(group, group + group_heads)
            ],
            axis=0,
        )
        high, low = hi_lo((dot(own, one) + add_one) * (dot(own, two) + add_two))
        for at in range(group_heads // 2):
            pair = group // 2 + at
            lanes = slice(pair * LANES, (pair + 1) * LANES)
            wanted = jnp.where(target < VHEAD, 16 * pair, 16 * pair + 8)
            spread = dot(norms, jnp.where(source == wanted, 1.0, 0.0).astype(BF16)).astype(BF16)
            right = jnp.concatenate([past_ref[pair * ROWS : (pair + 1) * ROWS, :], spread], axis=1)
            mine = slice(2 * at * rows, (2 * at + 2) * rows)
            result = dot(high[mine], right) + dot(low[mine], right)
            numer = jnp.where(lower, result[:rows, :LANES], result[rows:, :LANES]) + numer_ref[:, lanes]
            denom = jnp.where(lower, result[:rows, LANES:], result[rows:, LANES:]) + denom_ref[:, lanes]
            out_ref[:, lanes] = (numer / denom + swa_ref[:, lanes]).astype(out_ref.dtype)


IN_VMEM = pl.BlockSpec(memory_space=pltpu.VMEM)
IN_HBM = pl.BlockSpec(memory_space=pltpu.HBM)


def call(kernel, outs, args, specs, out_specs, scratch=(), grant=16):
    return pl.pallas_call(
        kernel,
        out_shape=outs,
        in_specs=specs,
        out_specs=out_specs,
        scratch_shapes=scratch,
        compiler_params=pltpu.CompilerParams(vmem_limit_bytes=grant * 1024 * 1024),
    )(*args)


def shards(lin_qk, lin_v, conv_w, swa_qkv):
    rows = lin_qk.shape[0]
    taps = conv_w.shape[0]
    chips = lax.axis_size("outer") * lax.axis_size("z")
    part = PAIRS // 2 * ROWS // chips
    held = (part + 7) // 8 * 8 + EXTRA
    shape = jax.ShapeDtypeStruct

    def swap(array):
        return lax.ppermute(array, "core", [(0, 1), (1, 0)])

    other_qk, other_v = swap(lin_qk), swap(lin_v)
    tokens = 2 * rows
    sums, tails = call(
        functools.partial(state_kernel, part),
        [
            shape((chips, held, LANES), BF16),
            shape((WINDOW + TAIL, swa_qkv.shape[1] // 3 * 2), BF16),
        ],
        [lin_qk, lin_v, other_qk, other_v, conv_w, swa_qkv],
        [IN_HBM] * 6,
        [IN_VMEM] * 2,
        [
            pltpu.VMEM((tokens, LANES), BF16),
            pltpu.VMEM((tokens, lin_v.shape[1] // 2), BF16),
            pltpu.VMEM((taps, lin_v.shape[1] // 2), jnp.float32),
            pltpu.SemaphoreType.DMA((7,)),
        ],
        grant=60,
    )
    sums, tails = lax.optimization_barrier((sums, tails))
    parts = lax.all_to_all(sums, CHIPS, 0, 0, tiled=True)
    tails = lax.ppermute(tails, SPLIT, [(i, i + 1) for i in range(2 * chips - 1)])
    past = call(
        functools.partial(prefix_kernel, taps),
        shape((chips, part, LANES), BF16),
        [parts],
        [IN_VMEM],
        IN_VMEM,
    )
    here = lax.all_to_all(past, CHIPS, 0, 0, tiled=True).reshape(chips * part, LANES)
    wide = shape(lin_v.shape, jnp.float32)
    numer, denom, swa = call(
        local_kernel,
        [wide, wide, wide],
        [lin_qk, lin_v, conv_w, swa_qkv, tails, other_qk, other_v],
        [IN_VMEM] * 7,
        [IN_VMEM] * 3,
    )
    here, numer, denom, swa = lax.optimization_barrier((here, numer, denom, swa))
    there = swap(here)
    return call(
        readout_kernel,
        shape(lin_v.shape, BF16),
        [lin_qk, numer, denom, swa, here, there],
        [IN_VMEM] * 6,
        IN_VMEM,
        [pltpu.VMEM((PAIRS * ROWS, LANES), BF16)],
    )


def solution(mesh):
    outer, inner = mesh.shape["ctxouter"], mesh.shape["ctxinner"]
    split = jax.sharding.Mesh(mesh.devices.reshape(outer, inner // 2, 2), SPLIT)
    return jax.shard_map(
        shards,
        mesh=split,
        in_specs=(P(SPLIT, None), P(SPLIT, None), P(), P(SPLIT, None)),
        out_specs=P(SPLIT, None),
        check_vma=False,
    )
```

```python
import functools

import jax
import jax.numpy as jnp
import numpy as np
from jax import lax
from jax.experimental import pallas as pl
from jax.experimental.pallas import tpu as pltpu
from jax.sharding import PartitionSpec as P

HEADS = 16
FEAT = 16
VHEAD = 64
SWA_HEADS = 8
SWA_HEAD = 128
WINDOW = 64

AXES = ("ctxouter", "ctxinner")
SPLIT = ("outer", "z", "core")
CHIPS = ("outer", "z")
LANES = 128
PAIRS = HEADS // 2
QUADS = FEAT * (FEAT + 1) // 2
CONST = QUADS + FEAT
ROWS = 160
TAIL = 16
EXTRA = 8
BLOCK_EXTRA = 4


NT = (((1,), (1,)), ((), ()))
NN = (((1,), (0,)), ((), ()))
BF16 = jnp.bfloat16


def dot(a, b, dims=NN):
    return lax.dot_general(a, b, dims, preferred_element_type=jnp.float32)


def iota(shape, dim):
    return lax.broadcasted_iota(jnp.int32, shape, dim)


def selector(feature, lane, second, halved=False):
    scale = FEAT ** (-0.25)
    quad = feature < QUADS
    entry = feature % FEAT
    if second:
        wanted = (feature + feature // FEAT) % FEAT
        return jnp.where((lane % FEAT == wanted) & quad, scale, 0.0)
    linear = (feature >= QUADS) & (feature < CONST)
    wanted = jnp.where(quad, entry, (feature - QUADS) % FEAT)
    weight = jnp.where((feature < FEAT) & halved, 0.5 * scale, scale)
    return jnp.where((lane % FEAT == wanted) & (quad | linear), weight, 0.0)


def adders(feature):
    first = jnp.where(feature == CONST, 1.0, 0.0)
    second = jnp.where((feature >= QUADS) & (feature <= CONST), 1.0, 0.0)
    return first, second


def head_mask(head, shape):
    place = iota(shape, 1)
    return (place >= head * FEAT) & (place < (head + 1) * FEAT)


def hi_lo(values):
    high = values.astype(BF16)
    return high, (values - high.astype(jnp.float32)).astype(BF16)


def convolved(value, tail, conv_ref, lanes):
    row_id = iota(value.shape, 0)
    result = conv_ref[0:1, lanes] * value
    for lag in range(1, conv_ref.shape[0]):
        shifted = pltpu.roll(value, lag, 0)
        for row in range(lag):
            source = TAIL - lag + row
            before = 0.0 if tail is None else tail[source : source + 1]
            shifted = jnp.where(row_id == row, before, shifted)
        result = result + conv_ref[lag : lag + 1, lanes] * shifted
    return result.astype(BF16)


def state_kernel(part, own, *refs):
    core = lax.axis_index("core")
    if own:
        qk_hbm, v_hbm, conv_hbm, swa_hbm, out_ref, tails_ref, conv_ref, key_ref, v_ref, sems = refs
        rows, wide = v_hbm.shape
    else:
        qk_ref, v_ref, conv_ref, own_ref, out_ref = refs
        rows, wide = v_ref.shape
    taps = conv_ref.shape[0]
    mine = pl.ds(pl.multiple_of(core * (wide // 2), wide // 2), wide // 2)
    keys = pl.ds(pl.multiple_of(HEADS * FEAT + core * LANES, LANES), LANES)
    if own:
        pieces = [
            (qk_hbm.at[:, keys], key_ref),
            (conv_hbm.at[:, mine], conv_ref),
            (v_hbm.at[:, mine], v_ref),
            (swa_hbm.at[rows - WINDOW :, tails_ref.shape[1] // 2 :], tails_ref.at[:WINDOW, :]),
            (v_hbm.at[rows - TAIL :, :], tails_ref.at[WINDOW:, :wide]),
        ]
        copies = [pltpu.make_async_copy(a, b, sems.at[i]) for i, (a, b) in enumerate(pieces)]
        for copy in copies:
            copy.start()
        copies[0].wait()
        key = key_ref[...]
    else:
        copies = []
        key = qk_ref[:, keys]
    key_t = (key.astype(jnp.float32) * FEAT ** (-0.25)).T
    const_rows = jnp.where(iota((EXTRA, rows), 0) == 0, 1.0, 0.0)
    lane_id = iota((ROWS, LANES), 1)
    low_row = iota((EXTRA, LANES), 0)
    ones = jnp.ones((rows, LANES), BF16)
    half = FEAT // 2
    padded = (part + 7) // 8 * 8
    lefts = []
    for head in range(HEADS // 2):
        x = key_t[head * FEAT : (head + 1) * FEAT]
        blocks = [x * x]
        for by in range(1, half):
            blocks.append(x * jnp.concatenate([x[by:], x[:by]], axis=0))
        blocks += [x[:half] * x[half:], x, const_rows]
        lefts.append(jnp.concatenate(hi_lo(jnp.concatenate(blocks, axis=0)), axis=1))
    first_keys = key[:16].astype(jnp.float32)
    slot = low_row - BLOCK_EXTRA * (core if own else 1 - core)
    for copy in copies[1:3]:
        copy.wait()
    states = []
    extras = []
    norms = jnp.zeros((ROWS, LANES), jnp.float32)
    for pair in range(PAIRS // 2):
        lanes = slice(pair * LANES, (pair + 1) * LANES)
        at = pl.multiple_of((0 if own else core * (wide // 2)) + pair * LANES, LANES)
        value = v_ref[:, pl.ds(at, LANES)].astype(jnp.float32)
        conved = convolved(value, None, conv_ref, lanes)
        right = jnp.concatenate([conved, ones], axis=1)
        right = jnp.concatenate([right, right], axis=0)
        both = []
        for head in (2 * pair, 2 * pair + 1):
            result = dot(lefts[head], right)
            both.append(result[:, :LANES])
            norms = jnp.where(lane_id // 8 == head, result[:, LANES:], norms)
        states.append(jnp.where(lane_id < VHEAD, both[0], both[1]))
        extra = jnp.zeros((EXTRA, LANES), jnp.float32)
        for row in range(taps - 1):
            share = jnp.zeros((1, LANES), jnp.float32)
            for lag in range(row + 1, taps):
                last = rows + row - lag
                share = share + conv_ref[lag : lag + 1, lanes] * value[last : last + 1]
            extra = jnp.where(slot == row, share, extra)
            extra = jnp.where(slot == taps - 1 + row, first_keys[row : row + 1], extra)
        extras.append(extra)
    norms_t = norms.T
    for pair in range(PAIRS // 2):
        last = states[pair][CONST:]
        for place in range(2):
            at = 8 * (2 * pair + place)
            norm = norms_t[at : at + 8]
            rest = jnp.concatenate(
                [norm[:, LANES:], jnp.zeros((8, 2 * LANES - ROWS), jnp.float32)], axis=1
            )
            last = jnp.where(low_row == 1 + 2 * place, norm[:, :LANES], last)
            last = jnp.where(low_row == 2 + 2 * place, rest, last)
        state = jnp.concatenate([states[pair][:CONST], last], axis=0)
        for piece in range(ROWS // part):
            rows_of = [state[piece * part : (piece + 1) * part]]
            if padded != part:
                rows_of.append(jnp.zeros((padded - part, LANES), jnp.float32))
            message = jnp.concatenate(rows_of + [extras[pair]], axis=0)
            chunk = pair * (ROWS // part) + piece
            if own:
                out_ref[chunk] = message
            else:
                out_ref[chunk] = (own_ref[chunk] + message).astype(BF16)
    for copy in copies[3:]:
        copy.wait()


def prefix_kernel(taps, parts_ref, out_ref):
    chips, held, _ = parts_ref.shape
    part = out_ref.shape[1]
    padded = held - EXTRA
    width = chips * EXTRA
    chip, core = lax.axis_index(CHIPS), lax.axis_index("core")
    start = core * (ROWS * PAIRS // 2) + chip * part
    head = start // ROWS * 2 % (LANES // FEAT)
    feature = start % ROWS + iota((padded, LANES), 0)
    lane = iota((padded, LANES), 1)
    one = selector(feature, lane, False)
    two = selector(feature, lane, True)
    add_one, add_two = adders(feature[:, 0:1])
    extras = parts_ref[:, padded:, :].astype(jnp.float32).reshape(width, LANES)
    extras_low = extras.astype(BF16)
    upper = iota((width, LANES), 1) >= VHEAD
    lefts = []
    rights = []
    for place in range(2):
        mine = lane // FEAT == head + place
        first = dot(jnp.where(mine, one, 0.0).astype(BF16), extras_low, NT) + add_one
        second = dot(jnp.where(mine, two, 0.0).astype(BF16), extras_low, NT) + add_two
        lefts.append(pltpu.roll(first * second, width - BLOCK_EXTRA - (taps - 1), 1))
        rights.append(jnp.where(upper == (place == 1), extras, 0.0).astype(BF16))
    left = jnp.concatenate(lefts, axis=1)
    right = jnp.concatenate(rights, axis=0)
    column = iota(left.shape, 1) % width
    to_block = jnp.where(column % BLOCK_EXTRA < taps - 1, column // BLOCK_EXTRA + 1, 2 * chips)

    def one_chip(chip, total):
        seen = jnp.where(to_block <= 2 * chip, left, 0.0).astype(BF16)
        result = total + dot(seen, right)
        out_ref[chip] = result[:part].astype(BF16)
        return total + parts_ref[chip].astype(jnp.float32)[:padded]

    total = jnp.zeros((padded, LANES), jnp.float32)
    if chips <= 32:
        for chip in range(chips):
            total = one_chip(chip, total)
    else:
        lax.fori_loop(0, chips, one_chip, total)


def local_kernel(
    qk_ref, v_ref, conv_ref, swa_ref, tails_ref, other_qk_ref, other_v_ref,
    numer_ref, denom_ref, swa_out_ref,
):
    rows = v_ref.shape[0]
    taps = conv_ref.shape[0]
    width = HEADS * FEAT
    core = lax.axis_index("core")
    second = core == 1
    first_block = (lax.axis_index(CHIPS) == 0) & (core == 0)
    query = qk_ref[:, :width]
    key = qk_ref[:, width : 2 * width]
    lower = iota((rows, LANES), 1) < VHEAD
    causal = iota((rows, rows), 1) <= iota((rows, rows), 0)
    row_id = iota((rows, LANES), 0)
    ones = jnp.ones((rows, LANES), BF16)
    counted = jnp.where(second, ones, jnp.zeros_like(ones))
    more_key = jnp.where(second, other_qk_ref[:, width : 2 * width], key)
    all_keys = jnp.concatenate([key, more_key], axis=0)
    allowed = jnp.concatenate([causal, causal | True], axis=1)
    group_heads = 4
    for group in range(0, HEADS, group_heads):
        own = jnp.concatenate(
            [
                jnp.where(head_mask(head, query.shape), query, jnp.zeros_like(query))
                for head in range(group, group + group_heads)
            ],
            axis=0,
        )
        score = dot(own, all_keys, NT) * FEAT ** (-0.5)
        weight = 1.0 + score + 0.5 * score * score
        weight = jnp.where(jnp.concatenate([allowed] * group_heads, axis=0), weight, 0.0).astype(BF16)
        for at in range(group_heads // 2):
            pair = group // 2 + at
            lanes = slice(pair * LANES, (pair + 1) * LANES)
            tail = jnp.where(first_block, 0.0, tails_ref[WINDOW:, lanes].astype(jnp.float32))
            conved = convolved(v_ref[:, lanes].astype(jnp.float32), tail, conv_ref, lanes)
            before = convolved(other_v_ref[:, lanes].astype(jnp.float32), None, conv_ref, lanes)
            shares = jnp.zeros((rows, LANES), jnp.float32)
            for row in range(taps - 1):
                share = jnp.zeros((1, LANES), jnp.float32)
                for lag in range(row + 1, taps):
                    at_row = TAIL + row - lag
                    share = share + conv_ref[lag : lag + 1, lanes] * tail[at_row : at_row + 1]
                shares = jnp.where(row_id == row, -share, shares)
            before = jnp.where(second, before, shares.astype(BF16))
            right = jnp.concatenate([conved, ones], axis=1)
            right = jnp.concatenate([right, jnp.concatenate([before, counted], axis=1)], axis=0)
            result = dot(weight[2 * at * rows : (2 * at + 2) * rows], right)
            top, bottom = result[:rows], result[rows:]
            numer_ref[:, lanes] = jnp.where(lower, top[:, :LANES], bottom[:, :LANES])
            denom_ref[:, lanes] = jnp.where(lower, top[:, LANES:], bottom[:, LANES:])
    swa_width = SWA_HEADS * SWA_HEAD
    not_before = jnp.where(first_block, WINDOW, 0)
    span = 2 * WINDOW
    place = iota((WINDOW, span), 1)
    row = iota((WINDOW, span), 0)
    inside = (place > row) & (place <= row + WINDOW)
    inside_first = inside & (place >= not_before)
    for step in range(rows // WINDOW):
        mine = slice(step * WINDOW, (step + 1) * WINDOW)
        window = slice((step - 1) * WINDOW, (step + 1) * WINDOW)

        def around(head, start):
            here = slice(start + head * SWA_HEAD, start + (head + 1) * SWA_HEAD)
            if step:
                return swa_ref[window, here]
            there = slice(here.start - swa_width, here.stop - swa_width)
            return jnp.concatenate([tails_ref[:WINDOW, there], swa_ref[mine, here]], axis=0)

        scores = []
        for head in range(SWA_HEADS):
            own = swa_ref[mine, head * SWA_HEAD : (head + 1) * SWA_HEAD]
            score = dot(own, around(head, swa_width), NT) * SWA_HEAD ** (-0.5)
            scores.append(jnp.where(inside if step else inside_first, score, -jnp.inf))
        scores = jnp.concatenate(scores, axis=0)
        expo = jnp.exp(scores - jnp.max(scores, axis=-1, keepdims=True))
        probs = (expo / jnp.sum(expo, axis=-1, keepdims=True)).astype(BF16)
        for head in range(SWA_HEADS):
            own = probs[head * WINDOW : (head + 1) * WINDOW]
            swa_out_ref[mine, head * SWA_HEAD : (head + 1) * SWA_HEAD] = dot(
                own, around(head, 2 * swa_width)
            )


def readout_kernel(own, qk_ref, numer_ref, denom_ref, swa_ref, past_ref, *refs):
    core = lax.axis_index("core")
    half = core if own else 1 - core
    rows = qk_ref.shape[0]
    wide = PAIRS // 2 * LANES
    copies = []
    if own:
        (out_ref,) = refs
    else:
        own_ref, out_hbm, out_ref, sems = refs
        there = pl.ds(pl.multiple_of(core * wide, wide), wide)
        copies.append(pltpu.make_async_copy(own_ref, out_hbm.at[:, there], sems.at[PAIRS // 2]))
        copies[0].start()
    lower = iota((rows, LANES), 1) < VHEAD
    query = qk_ref[:, pl.ds(pl.multiple_of(half * LANES, LANES), LANES)]
    feature = iota((LANES, ROWS), 1)
    lane = iota((LANES, ROWS), 0)
    one = selector(feature, lane, False, halved=True).astype(BF16)
    two = selector(feature, lane, True).astype(BF16)
    add_one, add_two = adders(iota((8, ROWS), 1)[0:1])
    norms = []
    for pair in range(PAIRS // 2):
        last = past_ref[(pair + 1) * ROWS - 16 : (pair + 1) * ROWS, :].astype(jnp.float32)
        for place in range(2):
            at = 16 - (ROWS - CONST) + 1 + 2 * place
            norm = jnp.concatenate([last[at : at + 1], last[at + 1 : at + 2, : ROWS - LANES]], axis=1)
            norms.append(jnp.broadcast_to(norm, (8, ROWS)))
    norms = jnp.concatenate(norms + [jnp.zeros((LANES // 2, ROWS), jnp.float32)], axis=0).T.astype(BF16)
    source = iota((LANES, LANES), 0)
    target = iota((LANES, LANES), 1)
    own_heads = [
        jnp.where(head_mask(head, query.shape), query, jnp.zeros_like(query)) for head in range(HEADS // 2)
    ]
    stacked = jnp.concatenate(own_heads, axis=0)
    high, low = hi_lo((dot(stacked, one) + add_one) * (dot(stacked, two) + add_two))
    for pair in range(PAIRS // 2):
        here = pl.ds(pl.multiple_of(half * wide + pair * LANES, LANES), LANES)
        wanted = jnp.where(target < VHEAD, 16 * pair, 16 * pair + 8)
        spread = dot(norms, jnp.where(source == wanted, 1.0, 0.0).astype(BF16)).astype(BF16)
        right = jnp.concatenate([past_ref[pair * ROWS : (pair + 1) * ROWS, :], spread], axis=1)
        mine = slice(2 * pair * rows, (2 * pair + 2) * rows)
        result = dot(high[mine], right) + dot(low[mine], right)
        numer = jnp.where(lower, result[:rows, :LANES], result[rows:, :LANES]) + numer_ref[:, here]
        denom = jnp.where(lower, result[:rows, LANES:], result[rows:, LANES:]) + denom_ref[:, here]
        mixed = (numer / denom + swa_ref[:, here]).astype(BF16)
        out_ref[:, pair * LANES : (pair + 1) * LANES] = mixed
        if not own:
            done = out_ref.at[:, pair * LANES : (pair + 1) * LANES]
            copies.append(pltpu.make_async_copy(done, out_hbm.at[:, here], sems.at[pair]))
            copies[-1].start()
    for copy in copies:
        copy.wait()


IN_VMEM = pl.BlockSpec(memory_space=pltpu.VMEM)
IN_HBM = pl.BlockSpec(memory_space=pltpu.HBM)


def call(kernel, outs, args, specs, out_specs, scratch=()):
    placed = [pltpu.with_memory_space_constraint(a, spec.memory_space) for a, spec in zip(args, specs)]
    results = jax.tree.map(lambda out, spec: spec.memory_space(out.shape, out.dtype), outs, out_specs)
    return pl.pallas_call(
        kernel,
        out_shape=results,
        in_specs=specs,
        out_specs=out_specs,
        scratch_shapes=scratch,
        compiler_params=pltpu.CompilerParams(vmem_limit_bytes=16 * 1024 * 1024),
    )(*placed)


def shards(lin_qk, lin_v, conv_w, swa_qkv):
    rows = lin_qk.shape[0]
    taps = conv_w.shape[0]
    chips = lax.axis_size("outer") * lax.axis_size("z")
    part = PAIRS // 2 * ROWS // chips
    held = (part + 7) // 8 * 8 + EXTRA
    shape = jax.ShapeDtypeStruct

    def swap(array):
        return lax.ppermute(array, "core", [(0, 1), (1, 0)])

    other_qk, other_v = swap(lin_qk), swap(lin_v)
    half_wide = lin_v.shape[1] // 2
    own_sums, tails, conv_half = call(
        functools.partial(state_kernel, part, True),
        [
            shape((chips, held, LANES), jnp.float32),
            shape((WINDOW + TAIL, swa_qkv.shape[1] // 3 * 2), BF16),
            shape((taps, half_wide), jnp.float32),
        ],
        [lin_qk, lin_v, conv_w, swa_qkv],
        [IN_HBM] * 4,
        [IN_VMEM] * 3,
        [
            pltpu.VMEM((rows, LANES), BF16),
            pltpu.VMEM((rows, half_wide), BF16),
            pltpu.SemaphoreType.DMA((5,)),
        ],
    )
    sums = call(
        functools.partial(state_kernel, part, False),
        shape((chips, held, LANES), BF16),
        [other_qk, other_v, conv_half, own_sums],
        [IN_VMEM] * 4,
        IN_VMEM,
    )
    sums, tails = lax.optimization_barrier((sums, tails))
    parts = lax.all_to_all(sums, CHIPS, 0, 0, tiled=True)
    tails = lax.ppermute(tails, SPLIT, [(i, i + 1) for i in range(2 * chips - 1)])
    past = call(
        functools.partial(prefix_kernel, taps),
        shape((chips, part, LANES), BF16),
        [parts],
        [IN_VMEM],
        IN_VMEM,
    )
    here = lax.all_to_all(past, CHIPS, 0, 0, tiled=True).reshape(chips * part, LANES)
    wide = shape(lin_v.shape, jnp.float32)
    numer, denom, swa = call(
        local_kernel,
        [wide, wide, wide],
        [lin_qk, lin_v, conv_w, swa_qkv, tails, other_qk, other_v],
        [IN_VMEM] * 7,
        [IN_VMEM] * 3,
    )
    here, numer, denom, swa = lax.optimization_barrier((here, numer, denom, swa))
    there = swap(here)
    own_out = call(
        functools.partial(readout_kernel, True),
        shape((rows, half_wide), BF16),
        [lin_qk, numer, denom, swa, here],
        [IN_VMEM] * 5,
        IN_VMEM,
    )
    return call(
        functools.partial(readout_kernel, False),
        shape(lin_v.shape, BF16),
        [lin_qk, numer, denom, swa, there, own_out],
        [IN_VMEM] * 6,
        IN_HBM,
        [pltpu.VMEM((rows, half_wide), BF16), pltpu.SemaphoreType.DMA((PAIRS // 2 + 1,))],
    )


def solution(mesh):
    outer, inner = mesh.shape["ctxouter"], mesh.shape["ctxinner"]
    split = jax.sharding.Mesh(mesh.devices.reshape(outer, inner // 2, 2), SPLIT)
    return jax.shard_map(
        shards,
        mesh=split,
        in_specs=(P(SPLIT, None), P(SPLIT, None), P(), P(SPLIT, None)),
        out_specs=P(SPLIT, None),
        check_vma=False,
    )
```

```python
import functools

import jax
import jax.numpy as jnp
import numpy as np
from jax import lax
from jax.experimental import pallas as pl
from jax.experimental.pallas import tpu as pltpu
from jax.sharding import PartitionSpec as P

HEADS = 16
FEAT = 16
VHEAD = 64
SWA_HEADS = 8
SWA_HEAD = 128
WINDOW = 64

BLOCK = "block"
LANES = 128
PAIRS = HEADS // 2
QUADS = FEAT * (FEAT + 1) // 2
CONST = QUADS + FEAT
ROWS = 160
TAIL = 16
EXTRA = 8
BLOCK_EXTRA = 4


NT = (((1,), (1,)), ((), ()))
NN = (((1,), (0,)), ((), ()))
BF16 = jnp.bfloat16


def dot(a, b, dims=NN):
    return lax.dot_general(a, b, dims, preferred_element_type=jnp.float32)


def iota(shape, dim):
    return lax.broadcasted_iota(jnp.int32, shape, dim)


def selector(feature, lane, second, halved=False):
    scale = FEAT ** (-0.25)
    quad = feature < QUADS
    entry = feature % FEAT
    if second:
        wanted = (feature + feature // FEAT) % FEAT
        return jnp.where((lane % FEAT == wanted) & quad, scale, 0.0)
    linear = (feature >= QUADS) & (feature < CONST)
    wanted = jnp.where(quad, entry, (feature - QUADS) % FEAT)
    weight = jnp.where((feature < FEAT) & halved, 0.5 * scale, scale)
    return jnp.where((lane % FEAT == wanted) & (quad | linear), weight, 0.0)


def adders(feature):
    first = jnp.where(feature == CONST, 1.0, 0.0)
    second = jnp.where((feature >= QUADS) & (feature <= CONST), 1.0, 0.0)
    return first, second


def head_mask(head, shape):
    place = iota(shape, 1)
    return (place >= head * FEAT) & (place < (head + 1) * FEAT)


def hi_lo(values):
    high = values.astype(BF16)
    return high, (values - high.astype(jnp.float32)).astype(BF16)


def convolved(value, tail, conv_ref, lanes):
    row_id = iota(value.shape, 0)
    result = conv_ref[0:1, lanes] * value
    for lag in range(1, conv_ref.shape[0]):
        shifted = pltpu.roll(value, lag, 0)
        for row in range(lag):
            source = TAIL - lag + row
            before = 0.0 if tail is None else tail[source : source + 1]
            shifted = jnp.where(row_id == row, before, shifted)
        result = result + conv_ref[lag : lag + 1, lanes] * shifted
    return result.astype(BF16)


def state_kernel(part, own, *refs):
    core = lax.axis_index(BLOCK) % 2
    if own:
        qk_hbm, v_hbm, conv_hbm, swa_hbm, out_ref, tails_ref, conv_ref, key_ref, v_ref, sems = refs
        rows, wide = v_hbm.shape
    else:
        qk_ref, v_ref, conv_ref, own_ref, out_ref = refs
        rows, wide = v_ref.shape
    taps = conv_ref.shape[0]
    mine = pl.ds(pl.multiple_of(core * (wide // 2), wide // 2), wide // 2)
    keys = pl.ds(pl.multiple_of(HEADS * FEAT + core * LANES, LANES), LANES)
    if own:
        pieces = [
            (qk_hbm.at[:, keys], key_ref),
            (conv_hbm.at[:, mine], conv_ref),
            (v_hbm.at[:, mine], v_ref),
            (swa_hbm.at[rows - WINDOW :, tails_ref.shape[1] // 2 :], tails_ref.at[:WINDOW, :]),
            (v_hbm.at[rows - TAIL :, :], tails_ref.at[WINDOW:, :wide]),
        ]
        copies = [pltpu.make_async_copy(a, b, sems.at[i]) for i, (a, b) in enumerate(pieces)]
        for copy in copies:
            copy.start()
        copies[0].wait()
        key = key_ref[...]
    else:
        copies = []
        key = qk_ref[:, keys]
    key_t = (key.astype(jnp.float32) * FEAT ** (-0.25)).T
    const_rows = jnp.where(iota((EXTRA, rows), 0) == 0, 1.0, 0.0)
    lane_id = iota((ROWS, LANES), 1)
    low_row = iota((EXTRA, LANES), 0)
    ones = jnp.ones((rows, LANES), BF16)
    half = FEAT // 2
    padded = (part + 7) // 8 * 8
    lefts = []
    for head in range(HEADS // 2):
        x = key_t[head * FEAT : (head + 1) * FEAT]
        blocks = [x * x]
        for by in range(1, half):
            blocks.append(x * jnp.concatenate([x[by:], x[:by]], axis=0))
        blocks += [x[:half] * x[half:], x, const_rows]
        lefts.append(jnp.concatenate(hi_lo(jnp.concatenate(blocks, axis=0)), axis=1))
    first_keys = key[:16].astype(jnp.float32)
    slot = low_row - BLOCK_EXTRA * (core if own else 1 - core)
    for copy in copies[1:3]:
        copy.wait()
    states = []
    extras = []
    norms = jnp.zeros((ROWS, LANES), jnp.float32)
    for pair in range(PAIRS // 2):
        lanes = slice(pair * LANES, (pair + 1) * LANES)
        at = pl.multiple_of((0 if own else core * (wide // 2)) + pair * LANES, LANES)
        value = v_ref[:, pl.ds(at, LANES)].astype(jnp.float32)
        conved = convolved(value, None, conv_ref, lanes)
        right = jnp.concatenate([conved, ones], axis=1)
        right = jnp.concatenate([right, right], axis=0)
        both = []
        for head in (2 * pair, 2 * pair + 1):
            result = dot(lefts[head], right)
            both.append(result[:, :LANES])
            norms = jnp.where(lane_id // 8 == head, result[:, LANES:], norms)
        states.append(jnp.where(lane_id < VHEAD, both[0], both[1]))
        extra = jnp.zeros((EXTRA, LANES), jnp.float32)
        for row in range(taps - 1):
            share = jnp.zeros((1, LANES), jnp.float32)
            for lag in range(row + 1, taps):
                last = rows + row - lag
                share = share + conv_ref[lag : lag + 1, lanes] * value[last : last + 1]
            extra = jnp.where(slot == row, share, extra)
            extra = jnp.where(slot == taps - 1 + row, first_keys[row : row + 1], extra)
        extras.append(extra)
    norms_t = norms.T
    for pair in range(PAIRS // 2):
        last = states[pair][CONST:]
        for place in range(2):
            at = 8 * (2 * pair + place)
            norm = norms_t[at : at + 8]
            rest = jnp.concatenate(
                [norm[:, LANES:], jnp.zeros((8, 2 * LANES - ROWS), jnp.float32)], axis=1
            )
            last = jnp.where(low_row == 1 + 2 * place, norm[:, :LANES], last)
            last = jnp.where(low_row == 2 + 2 * place, rest, last)
        state = jnp.concatenate([states[pair][:CONST], last], axis=0)
        for piece in range(ROWS // part):
            rows_of = [state[piece * part : (piece + 1) * part]]
            if padded != part:
                rows_of.append(jnp.zeros((padded - part, LANES), jnp.float32))
            message = jnp.concatenate(rows_of + [extras[pair]], axis=0)
            chunk = pair * (ROWS // part) + piece
            if own:
                out_ref[chunk] = message
            else:
                out_ref[chunk] = (own_ref[chunk] + message).astype(BF16)
    for copy in copies[3:]:
        copy.wait()


def prefix_kernel(taps, parts_ref, out_ref):
    chips, held, _ = parts_ref.shape
    part = out_ref.shape[1]
    padded = held - EXTRA
    width = chips * EXTRA
    block = lax.axis_index(BLOCK)
    start = block % 2 * (ROWS * PAIRS // 2) + (chips - 1 - block // 2) * part
    head = start // ROWS * 2 % (LANES // FEAT)
    feature = start % ROWS + iota((padded, LANES), 0)
    lane = iota((padded, LANES), 1)
    one = selector(feature, lane, False)
    two = selector(feature, lane, True)
    add_one, add_two = adders(feature[:, 0:1])
    extras = jnp.concatenate(
        [parts_ref[chips - 1 - chip].astype(jnp.float32)[padded:] for chip in range(chips)], axis=0
    )
    extras_low = extras.astype(BF16)
    upper = iota((width, LANES), 1) >= VHEAD
    lefts = []
    rights = []
    for place in range(2):
        mine = lane // FEAT == head + place
        first = dot(jnp.where(mine, one, 0.0).astype(BF16), extras_low, NT) + add_one
        second = dot(jnp.where(mine, two, 0.0).astype(BF16), extras_low, NT) + add_two
        lefts.append(pltpu.roll(first * second, width - BLOCK_EXTRA - (taps - 1), 1))
        rights.append(jnp.where(upper == (place == 1), extras, 0.0).astype(BF16))
    left = jnp.concatenate(lefts, axis=1)
    right = jnp.concatenate(rights, axis=0)
    column = iota(left.shape, 1) % width
    to_block = jnp.where(column % BLOCK_EXTRA < taps - 1, column // BLOCK_EXTRA + 1, 2 * chips)

    def one_chip(chip, total):
        seen = jnp.where(to_block <= 2 * chip, left, 0.0).astype(BF16)
        result = total + dot(seen, right)
        out_ref[chips - 1 - chip] = result[:part].astype(BF16)
        return total + parts_ref[chips - 1 - chip].astype(jnp.float32)[:padded]

    total = jnp.zeros((padded, LANES), jnp.float32)
    if chips <= 32:
        for chip in range(chips):
            total = one_chip(chip, total)
    else:
        lax.fori_loop(0, chips, one_chip, total)


def local_kernel(
    qk_ref, v_ref, conv_ref, swa_ref, tails_ref, other_qk_ref, other_v_ref,
    numer_ref, denom_ref, swa_out_ref,
):
    rows = v_ref.shape[0]
    taps = conv_ref.shape[0]
    width = HEADS * FEAT
    core = lax.axis_index(BLOCK) % 2
    second = core == 1
    first_block = lax.axis_index(BLOCK) == 0
    query = qk_ref[:, :width]
    key = qk_ref[:, width : 2 * width]
    lower = iota((rows, LANES), 1) < VHEAD
    causal = iota((rows, rows), 1) <= iota((rows, rows), 0)
    row_id = iota((rows, LANES), 0)
    ones = jnp.ones((rows, LANES), BF16)
    counted = jnp.where(second, ones, jnp.zeros_like(ones))
    more_key = jnp.where(second, other_qk_ref[:, width : 2 * width], key)
    all_keys = jnp.concatenate([key, more_key], axis=0)
    allowed = jnp.concatenate([causal, causal | True], axis=1)
    group_heads = 4
    for group in range(0, HEADS, group_heads):
        own = jnp.concatenate(
            [
                jnp.where(head_mask(head, query.shape), query, jnp.zeros_like(query))
                for head in range(group, group + group_heads)
            ],
            axis=0,
        )
        score = dot(own, all_keys, NT) * FEAT ** (-0.5)
        weight = 1.0 + score + 0.5 * score * score
        weight = jnp.where(jnp.concatenate([allowed] * group_heads, axis=0), weight, 0.0).astype(BF16)
        for at in range(group_heads // 2):
            pair = group // 2 + at
            lanes = slice(pair * LANES, (pair + 1) * LANES)
            tail = jnp.where(first_block, 0.0, tails_ref[WINDOW:, lanes].astype(jnp.float32))
            conved = convolved(v_ref[:, lanes].astype(jnp.float32), tail, conv_ref, lanes)
            before = convolved(other_v_ref[:, lanes].astype(jnp.float32), None, conv_ref, lanes)
            shares = jnp.zeros((rows, LANES), jnp.float32)
            for row in range(taps - 1):
                share = jnp.zeros((1, LANES), jnp.float32)
                for lag in range(row + 1, taps):
                    at_row = TAIL + row - lag
                    share = share + conv_ref[lag : lag + 1, lanes] * tail[at_row : at_row + 1]
                shares = jnp.where(row_id == row, -share, shares)
            before = jnp.where(second, before, shares.astype(BF16))
            right = jnp.concatenate([conved, ones], axis=1)
            right = jnp.concatenate([right, jnp.concatenate([before, counted], axis=1)], axis=0)
            result = dot(weight[2 * at * rows : (2 * at + 2) * rows], right)
            top, bottom = result[:rows], result[rows:]
            numer_ref[:, lanes] = jnp.where(lower, top[:, :LANES], bottom[:, :LANES])
            denom_ref[:, lanes] = jnp.where(lower, top[:, LANES:], bottom[:, LANES:])
    swa_width = SWA_HEADS * SWA_HEAD
    not_before = jnp.where(first_block, WINDOW, 0)
    span = 2 * WINDOW
    place = iota((WINDOW, span), 1)
    row = iota((WINDOW, span), 0)
    inside = (place > row) & (place <= row + WINDOW)
    inside_first = inside & (place >= not_before)
    for step in range(rows // WINDOW):
        mine = slice(step * WINDOW, (step + 1) * WINDOW)
        window = slice((step - 1) * WINDOW, (step + 1) * WINDOW)

        def around(head, start):
            here = slice(start + head * SWA_HEAD, start + (head + 1) * SWA_HEAD)
            if step:
                return swa_ref[window, here]
            there = slice(here.start - swa_width, here.stop - swa_width)
            return jnp.concatenate([tails_ref[:WINDOW, there], swa_ref[mine, here]], axis=0)

        scores = []
        for head in range(SWA_HEADS):
            own = swa_ref[mine, head * SWA_HEAD : (head + 1) * SWA_HEAD]
            score = dot(own, around(head, swa_width), NT) * SWA_HEAD ** (-0.5)
            scores.append(jnp.where(inside if step else inside_first, score, -jnp.inf))
        scores = jnp.concatenate(scores, axis=0)
        expo = jnp.exp(scores - jnp.max(scores, axis=-1, keepdims=True))
        probs = (expo / jnp.sum(expo, axis=-1, keepdims=True)).astype(BF16)
        for head in range(SWA_HEADS):
            own = probs[head * WINDOW : (head + 1) * WINDOW]
            swa_out_ref[mine, head * SWA_HEAD : (head + 1) * SWA_HEAD] = dot(
                own, around(head, 2 * swa_width)
            )


def readout_kernel(own, qk_ref, numer_ref, denom_ref, swa_ref, past_ref, *refs):
    core = lax.axis_index(BLOCK) % 2
    half = core if own else 1 - core
    rows = qk_ref.shape[0]
    wide = PAIRS // 2 * LANES
    copies = []
    if own:
        (out_ref,) = refs
    else:
        own_ref, out_hbm, out_ref, sems = refs
        there = pl.ds(pl.multiple_of(core * wide, wide), wide)
        copies.append(pltpu.make_async_copy(own_ref, out_hbm.at[:, there], sems.at[PAIRS // 2]))
        copies[0].start()
    lower = iota((rows, LANES), 1) < VHEAD
    query = qk_ref[:, pl.ds(pl.multiple_of(half * LANES, LANES), LANES)]
    feature = iota((LANES, ROWS), 1)
    lane = iota((LANES, ROWS), 0)
    one = selector(feature, lane, False, halved=True).astype(BF16)
    two = selector(feature, lane, True).astype(BF16)
    add_one, add_two = adders(iota((8, ROWS), 1)[0:1])
    norms = []
    for pair in range(PAIRS // 2):
        last = past_ref[(pair + 1) * ROWS - 16 : (pair + 1) * ROWS, :].astype(jnp.float32)
        for place in range(2):
            at = 16 - (ROWS - CONST) + 1 + 2 * place
            norm = jnp.concatenate([last[at : at + 1], last[at + 1 : at + 2, : ROWS - LANES]], axis=1)
            norms.append(jnp.broadcast_to(norm, (8, ROWS)))
    norms = jnp.concatenate(norms + [jnp.zeros((LANES // 2, ROWS), jnp.float32)], axis=0).T.astype(BF16)
    source = iota((LANES, LANES), 0)
    target = iota((LANES, LANES), 1)
    own_heads = [
        jnp.where(head_mask(head, query.shape), query, jnp.zeros_like(query)) for head in range(HEADS // 2)
    ]
    stacked = jnp.concatenate(own_heads, axis=0)
    high, low = hi_lo((dot(stacked, one) + add_one) * (dot(stacked, two) + add_two))
    for pair in range(PAIRS // 2):
        here = pl.ds(pl.multiple_of(half * wide + pair * LANES, LANES), LANES)
        wanted = jnp.where(target < VHEAD, 16 * pair, 16 * pair + 8)
        spread = dot(norms, jnp.where(source == wanted, 1.0, 0.0).astype(BF16)).astype(BF16)
        right = jnp.concatenate([past_ref[pair * ROWS : (pair + 1) * ROWS, :], spread], axis=1)
        mine = slice(2 * pair * rows, (2 * pair + 2) * rows)
        result = dot(high[mine], right) + dot(low[mine], right)
        numer = jnp.where(lower, result[:rows, :LANES], result[rows:, :LANES]) + numer_ref[:, here]
        denom = jnp.where(lower, result[:rows, LANES:], result[rows:, LANES:]) + denom_ref[:, here]
        mixed = (numer / denom + swa_ref[:, here]).astype(BF16)
        out_ref[:, pair * LANES : (pair + 1) * LANES] = mixed
        if not own:
            done = out_ref.at[:, pair * LANES : (pair + 1) * LANES]
            copies.append(pltpu.make_async_copy(done, out_hbm.at[:, here], sems.at[pair]))
            copies[-1].start()
    for copy in copies:
        copy.wait()


IN_VMEM = pl.BlockSpec(memory_space=pltpu.VMEM)
IN_HBM = pl.BlockSpec(memory_space=pltpu.HBM)


def call(kernel, outs, args, specs, out_specs, scratch=()):
    placed = [pltpu.with_memory_space_constraint(a, spec.memory_space) for a, spec in zip(args, specs)]
    results = jax.tree.map(lambda out, spec: spec.memory_space(out.shape, out.dtype), outs, out_specs)
    return pl.pallas_call(
        kernel,
        out_shape=results,
        in_specs=specs,
        out_specs=out_specs,
        scratch_shapes=scratch,
        compiler_params=pltpu.CompilerParams(vmem_limit_bytes=16 * 1024 * 1024),
    )(*placed)


def shards(lin_qk, lin_v, conv_w, swa_qkv):
    rows = lin_qk.shape[0]
    taps = conv_w.shape[0]
    chips = lax.axis_size(BLOCK) // 2
    part = PAIRS // 2 * ROWS // chips
    held = (part + 7) // 8 * 8 + EXTRA
    shape = jax.ShapeDtypeStruct

    def swap(array):
        return lax.ppermute(array, BLOCK, [(i, i ^ 1) for i in range(2 * chips)])

    def exchange(array):
        groups = [list(range(core, 2 * chips, 2))[::-1] for core in range(2)]
        return lax.all_to_all(array, BLOCK, 0, 0, axis_index_groups=groups, tiled=True)

    other_qk, other_v = swap(lin_qk), swap(lin_v)
    half_wide = lin_v.shape[1] // 2
    own_sums, tails, conv_half = call(
        functools.partial(state_kernel, part, True),
        [
            shape((chips, held, LANES), jnp.float32),
            shape((WINDOW + TAIL, swa_qkv.shape[1] // 3 * 2), BF16),
            shape((taps, half_wide), jnp.float32),
        ],
        [lin_qk, lin_v, conv_w, swa_qkv],
        [IN_HBM] * 4,
        [IN_VMEM] * 3,
        [
            pltpu.VMEM((rows, LANES), BF16),
            pltpu.VMEM((rows, half_wide), BF16),
            pltpu.SemaphoreType.DMA((5,)),
        ],
    )
    sums = call(
        functools.partial(state_kernel, part, False),
        shape((chips, held, LANES), BF16),
        [other_qk, other_v, conv_half, own_sums],
        [IN_VMEM] * 4,
        IN_VMEM,
    )
    sums, tails = lax.optimization_barrier((sums, tails))
    parts = exchange(sums)
    tails = lax.ppermute(tails, BLOCK, [(i, i + 1) for i in range(2 * chips - 1)])
    past = call(
        functools.partial(prefix_kernel, taps),
        shape((chips, part, LANES), BF16),
        [parts],
        [IN_VMEM],
        IN_VMEM,
    )
    here = exchange(past).reshape(chips * part, LANES)
    wide = shape(lin_v.shape, jnp.float32)
    numer, denom, swa = call(
        local_kernel,
        [wide, wide, wide],
        [lin_qk, lin_v, conv_w, swa_qkv, tails, other_qk, other_v],
        [IN_VMEM] * 7,
        [IN_VMEM] * 3,
    )
    here, numer, denom, swa = lax.optimization_barrier((here, numer, denom, swa))
    there = swap(here)
    own_out = call(
        functools.partial(readout_kernel, True),
        shape((rows, half_wide), BF16),
        [lin_qk, numer, denom, swa, here],
        [IN_VMEM] * 5,
        IN_VMEM,
    )
    return call(
        functools.partial(readout_kernel, False),
        shape(lin_v.shape, BF16),
        [lin_qk, numer, denom, swa, there, own_out],
        [IN_VMEM] * 6,
        IN_HBM,
        [pltpu.VMEM((rows, half_wide), BF16), pltpu.SemaphoreType.DMA((PAIRS // 2 + 1,))],
    )


def solution(mesh):
    blocks = jax.sharding.Mesh(mesh.devices.reshape(-1), (BLOCK,))
    return jax.shard_map(
        shards,
        mesh=blocks,
        in_specs=(P(BLOCK, None), P(BLOCK, None), P(), P(BLOCK, None)),
        out_specs=P(BLOCK, None),
        check_vma=False,
    )
```

```python
import functools

import jax
import jax.numpy as jnp
import numpy as np
from jax import lax
from jax.experimental import pallas as pl
from jax.experimental.pallas import tpu as pltpu
from jax.sharding import PartitionSpec as P

HEADS = 16
FEAT = 16
VHEAD = 64
SWA_HEADS = 8
SWA_HEAD = 128
WINDOW = 64

BLOCK = "block"
ORDER_SEED = 24
LANES = 128
PAIRS = HEADS // 2
QUADS = FEAT * (FEAT + 1) // 2
CONST = QUADS + FEAT
ROWS = 160
TAIL = 16
EXTRA = 8
BLOCK_EXTRA = 4


NT = (((1,), (1,)), ((), ()))
NN = (((1,), (0,)), ((), ()))
BF16 = jnp.bfloat16


def dot(a, b, dims=NN):
    return lax.dot_general(a, b, dims, preferred_element_type=jnp.float32)


def iota(shape, dim):
    return lax.broadcasted_iota(jnp.int32, shape, dim)


def selector(feature, lane, second, halved=False):
    scale = FEAT ** (-0.25)
    quad = feature < QUADS
    entry = feature % FEAT
    if second:
        wanted = (feature + feature // FEAT) % FEAT
        return jnp.where((lane % FEAT == wanted) & quad, scale, 0.0)
    linear = (feature >= QUADS) & (feature < CONST)
    wanted = jnp.where(quad, entry, (feature - QUADS) % FEAT)
    weight = jnp.where((feature < FEAT) & halved, 0.5 * scale, scale)
    return jnp.where((lane % FEAT == wanted) & (quad | linear), weight, 0.0)


def adders(feature):
    first = jnp.where(feature == CONST, 1.0, 0.0)
    second = jnp.where((feature >= QUADS) & (feature <= CONST), 1.0, 0.0)
    return first, second


def group_order(chips):
    return [int(chip) for chip in np.random.RandomState(ORDER_SEED).permutation(chips)]


def head_mask(head, shape):
    place = iota(shape, 1)
    return (place >= head * FEAT) & (place < (head + 1) * FEAT)


def hi_lo(values):
    high = values.astype(BF16)
    return high, (values - high.astype(jnp.float32)).astype(BF16)


def convolved(value, tail, conv_ref, lanes):
    row_id = iota(value.shape, 0)
    result = conv_ref[0:1, lanes] * value
    for lag in range(1, conv_ref.shape[0]):
        shifted = pltpu.roll(value, lag, 0)
        for row in range(lag):
            source = TAIL - lag + row
            before = 0.0 if tail is None else tail[source : source + 1]
            shifted = jnp.where(row_id == row, before, shifted)
        result = result + conv_ref[lag : lag + 1, lanes] * shifted
    return result.astype(BF16)


def state_kernel(part, own, *refs):
    core = lax.axis_index(BLOCK) % 2
    if own:
        qk_hbm, v_hbm, conv_hbm, swa_hbm, out_ref, tails_ref, conv_ref, key_ref, v_ref, sems = refs
        rows, wide = v_hbm.shape
    else:
        qk_ref, v_ref, conv_ref, own_ref, out_ref = refs
        rows, wide = v_ref.shape
    taps = conv_ref.shape[0]
    mine = pl.ds(pl.multiple_of(core * (wide // 2), wide // 2), wide // 2)
    keys = pl.ds(pl.multiple_of(HEADS * FEAT + core * LANES, LANES), LANES)
    if own:
        pieces = [
            (qk_hbm.at[:, keys], key_ref),
            (conv_hbm.at[:, mine], conv_ref),
            (v_hbm.at[:, mine], v_ref),
            (swa_hbm.at[rows - WINDOW :, tails_ref.shape[1] // 2 :], tails_ref.at[:WINDOW, :]),
            (v_hbm.at[rows - TAIL :, :], tails_ref.at[WINDOW:, :wide]),
        ]
        copies = [pltpu.make_async_copy(a, b, sems.at[i]) for i, (a, b) in enumerate(pieces)]
        for copy in copies:
            copy.start()
        copies[0].wait()
        key = key_ref[...]
    else:
        copies = []
        key = qk_ref[:, keys]
    key_t = (key.astype(jnp.float32) * FEAT ** (-0.25)).T
    const_rows = jnp.where(iota((EXTRA, rows), 0) == 0, 1.0, 0.0)
    lane_id = iota((ROWS, LANES), 1)
    low_row = iota((EXTRA, LANES), 0)
    ones = jnp.ones((rows, LANES), BF16)
    half = FEAT // 2
    padded = (part + 7) // 8 * 8
    lefts = []
    for head in range(HEADS // 2):
        x = key_t[head * FEAT : (head + 1) * FEAT]
        blocks = [x * x]
        for by in range(1, half):
            blocks.append(x * jnp.concatenate([x[by:], x[:by]], axis=0))
        blocks += [x[:half] * x[half:], x, const_rows]
        lefts.append(jnp.concatenate(hi_lo(jnp.concatenate(blocks, axis=0)), axis=1))
    first_keys = key[:16].astype(jnp.float32)
    slot = low_row - BLOCK_EXTRA * (core if own else 1 - core)
    for copy in copies[1:3]:
        copy.wait()
    states = []
    extras = []
    norms = jnp.zeros((ROWS, LANES), jnp.float32)
    for pair in range(PAIRS // 2):
        lanes = slice(pair * LANES, (pair + 1) * LANES)
        at = pl.multiple_of((0 if own else core * (wide // 2)) + pair * LANES, LANES)
        value = v_ref[:, pl.ds(at, LANES)].astype(jnp.float32)
        conved = convolved(value, None, conv_ref, lanes)
        right = jnp.concatenate([conved, ones], axis=1)
        right = jnp.concatenate([right, right], axis=0)
        both = []
        for head in (2 * pair, 2 * pair + 1):
            result = dot(lefts[head], right)
            both.append(result[:, :LANES])
            norms = jnp.where(lane_id // 8 == head, result[:, LANES:], norms)
        states.append(jnp.where(lane_id < VHEAD, both[0], both[1]))
        extra = jnp.zeros((EXTRA, LANES), jnp.float32)
        for row in range(taps - 1):
            share = jnp.zeros((1, LANES), jnp.float32)
            for lag in range(row + 1, taps):
                last = rows + row - lag
                share = share + conv_ref[lag : lag + 1, lanes] * value[last : last + 1]
            extra = jnp.where(slot == row, share, extra)
            extra = jnp.where(slot == taps - 1 + row, first_keys[row : row + 1], extra)
        extras.append(extra)
    norms_t = norms.T
    for pair in range(PAIRS // 2):
        last = states[pair][CONST:]
        for place in range(2):
            at = 8 * (2 * pair + place)
            norm = norms_t[at : at + 8]
            rest = jnp.concatenate(
                [norm[:, LANES:], jnp.zeros((8, 2 * LANES - ROWS), jnp.float32)], axis=1
            )
            last = jnp.where(low_row == 1 + 2 * place, norm[:, :LANES], last)
            last = jnp.where(low_row == 2 + 2 * place, rest, last)
        state = jnp.concatenate([states[pair][:CONST], last], axis=0)
        for piece in range(ROWS // part):
            rows_of = [state[piece * part : (piece + 1) * part]]
            if padded != part:
                rows_of.append(jnp.zeros((padded - part, LANES), jnp.float32))
            message = jnp.concatenate(rows_of + [extras[pair]], axis=0)
            chunk = pair * (ROWS // part) + piece
            if own:
                out_ref[chunk] = message
            else:
                out_ref[chunk] = (own_ref[chunk] + message).astype(BF16)
    for copy in copies[3:]:
        copy.wait()


def prefix_kernel(taps, parts_ref, out_ref):
    chips, held, _ = parts_ref.shape
    part = out_ref.shape[1]
    padded = held - EXTRA
    width = chips * EXTRA
    block = lax.axis_index(BLOCK)
    places = list(np.argsort(group_order(chips)))
    place = sum(jnp.where(block // 2 == chip, int(at), 0) for chip, at in enumerate(places))
    start = block % 2 * (ROWS * PAIRS // 2) + place * part
    head = start // ROWS * 2 % (LANES // FEAT)
    feature = start % ROWS + iota((padded, LANES), 0)
    lane = iota((padded, LANES), 1)
    one = selector(feature, lane, False)
    two = selector(feature, lane, True)
    add_one, add_two = adders(feature[:, 0:1])
    extras = jnp.concatenate(
        [parts_ref[int(at)].astype(jnp.float32)[padded:] for at in places], axis=0
    )
    extras_low = extras.astype(BF16)
    upper = iota((width, LANES), 1) >= VHEAD
    lefts = []
    rights = []
    for place in range(2):
        mine = lane // FEAT == head + place
        first = dot(jnp.where(mine, one, 0.0).astype(BF16), extras_low, NT) + add_one
        second = dot(jnp.where(mine, two, 0.0).astype(BF16), extras_low, NT) + add_two
        lefts.append(pltpu.roll(first * second, width - BLOCK_EXTRA - (taps - 1), 1))
        rights.append(jnp.where(upper == (place == 1), extras, 0.0).astype(BF16))
    left = jnp.concatenate(lefts, axis=1)
    right = jnp.concatenate(rights, axis=0)
    column = iota(left.shape, 1) % width
    to_block = jnp.where(column % BLOCK_EXTRA < taps - 1, column // BLOCK_EXTRA + 1, 2 * chips)

    total = jnp.zeros((padded, LANES), jnp.float32)
    for chip, at in enumerate(places):
        seen = jnp.where(to_block <= 2 * chip, left, 0.0).astype(BF16)
        out_ref[int(at)] = (total + dot(seen, right))[:part].astype(BF16)
        total = total + parts_ref[int(at)].astype(jnp.float32)[:padded]


def local_kernel(
    qk_ref, v_ref, conv_ref, swa_ref, tails_ref, other_qk_ref, other_v_ref,
    numer_ref, denom_ref, swa_out_ref,
):
    rows = v_ref.shape[0]
    taps = conv_ref.shape[0]
    width = HEADS * FEAT
    core = lax.axis_index(BLOCK) % 2
    second = core == 1
    first_block = lax.axis_index(BLOCK) == 0
    query = qk_ref[:, :width]
    key = qk_ref[:, width : 2 * width]
    lower = iota((rows, LANES), 1) < VHEAD
    causal = iota((rows, rows), 1) <= iota((rows, rows), 0)
    row_id = iota((rows, LANES), 0)
    ones = jnp.ones((rows, LANES), BF16)
    counted = jnp.where(second, ones, jnp.zeros_like(ones))
    more_key = jnp.where(second, other_qk_ref[:, width : 2 * width], key)
    all_keys = jnp.concatenate([key, more_key], axis=0)
    allowed = jnp.concatenate([causal, causal | True], axis=1)
    group_heads = 4
    for group in range(0, HEADS, group_heads):
        own = jnp.concatenate(
            [
                jnp.where(head_mask(head, query.shape), query, jnp.zeros_like(query))
                for head in range(group, group + group_heads)
            ],
            axis=0,
        )
        score = dot(own, all_keys, NT) * FEAT ** (-0.5)
        weight = 1.0 + score + 0.5 * score * score
        weight = jnp.where(jnp.concatenate([allowed] * group_heads, axis=0), weight, 0.0).astype(BF16)
        for at in range(group_heads // 2):
            pair = group // 2 + at
            lanes = slice(pair * LANES, (pair + 1) * LANES)
            tail = jnp.where(first_block, 0.0, tails_ref[WINDOW:, lanes].astype(jnp.float32))
            conved = convolved(v_ref[:, lanes].astype(jnp.float32), tail, conv_ref, lanes)
            before = convolved(other_v_ref[:, lanes].astype(jnp.float32), None, conv_ref, lanes)
            shares = jnp.zeros((rows, LANES), jnp.float32)
            for row in range(taps - 1):
                share = jnp.zeros((1, LANES), jnp.float32)
                for lag in range(row + 1, taps):
                    at_row = TAIL + row - lag
                    share = share + conv_ref[lag : lag + 1, lanes] * tail[at_row : at_row + 1]
                shares = jnp.where(row_id == row, -share, shares)
            before = jnp.where(second, before, shares.astype(BF16))
            right = jnp.concatenate([conved, ones], axis=1)
            right = jnp.concatenate([right, jnp.concatenate([before, counted], axis=1)], axis=0)
            result = dot(weight[2 * at * rows : (2 * at + 2) * rows], right)
            top, bottom = result[:rows], result[rows:]
            numer_ref[:, lanes] = jnp.where(lower, top[:, :LANES], bottom[:, :LANES])
            denom_ref[:, lanes] = jnp.where(lower, top[:, LANES:], bottom[:, LANES:])
    swa_width = SWA_HEADS * SWA_HEAD
    not_before = jnp.where(first_block, WINDOW, 0)
    span = 2 * WINDOW
    place = iota((WINDOW, span), 1)
    row = iota((WINDOW, span), 0)
    inside = (place > row) & (place <= row + WINDOW)
    inside_first = inside & (place >= not_before)
    for step in range(rows // WINDOW):
        mine = slice(step * WINDOW, (step + 1) * WINDOW)
        window = slice((step - 1) * WINDOW, (step + 1) * WINDOW)

        def around(head, start):
            here = slice(start + head * SWA_HEAD, start + (head + 1) * SWA_HEAD)
            if step:
                return swa_ref[window, here]
            there = slice(here.start - swa_width, here.stop - swa_width)
            return jnp.concatenate([tails_ref[:WINDOW, there], swa_ref[mine, here]], axis=0)

        scores = []
        for head in range(SWA_HEADS):
            own = swa_ref[mine, head * SWA_HEAD : (head + 1) * SWA_HEAD]
            score = dot(own, around(head, swa_width), NT) * SWA_HEAD ** (-0.5)
            scores.append(jnp.where(inside if step else inside_first, score, -jnp.inf))
        scores = jnp.concatenate(scores, axis=0)
        expo = jnp.exp(scores - jnp.max(scores, axis=-1, keepdims=True))
        probs = (expo / jnp.sum(expo, axis=-1, keepdims=True)).astype(BF16)
        for head in range(SWA_HEADS):
            own = probs[head * WINDOW : (head + 1) * WINDOW]
            swa_out_ref[mine, head * SWA_HEAD : (head + 1) * SWA_HEAD] = dot(
                own, around(head, 2 * swa_width)
            )


def readout_kernel(own, qk_ref, numer_ref, denom_ref, swa_ref, past_ref, *refs):
    core = lax.axis_index(BLOCK) % 2
    half = core if own else 1 - core
    rows = qk_ref.shape[0]
    wide = PAIRS // 2 * LANES
    copies = []
    if own:
        (out_ref,) = refs
    else:
        own_ref, out_hbm, out_ref, sems = refs
        there = pl.ds(pl.multiple_of(core * wide, wide), wide)
        copies.append(pltpu.make_async_copy(own_ref, out_hbm.at[:, there], sems.at[PAIRS // 2]))
        copies[0].start()
    lower = iota((rows, LANES), 1) < VHEAD
    query = qk_ref[:, pl.ds(pl.multiple_of(half * LANES, LANES), LANES)]
    feature = iota((LANES, ROWS), 1)
    lane = iota((LANES, ROWS), 0)
    one = selector(feature, lane, False, halved=True).astype(BF16)
    two = selector(feature, lane, True).astype(BF16)
    add_one, add_two = adders(iota((8, ROWS), 1)[0:1])
    norms = []
    for pair in range(PAIRS // 2):
        last = past_ref[(pair + 1) * ROWS - 16 : (pair + 1) * ROWS, :].astype(jnp.float32)
        for place in range(2):
            at = 16 - (ROWS - CONST) + 1 + 2 * place
            norm = jnp.concatenate([last[at : at + 1], last[at + 1 : at + 2, : ROWS - LANES]], axis=1)
            norms.append(jnp.broadcast_to(norm, (8, ROWS)))
    norms = jnp.concatenate(norms + [jnp.zeros((LANES // 2, ROWS), jnp.float32)], axis=0).T.astype(BF16)
    source = iota((LANES, LANES), 0)
    target = iota((LANES, LANES), 1)
    own_heads = [
        jnp.where(head_mask(head, query.shape), query, jnp.zeros_like(query)) for head in range(HEADS // 2)
    ]
    stacked = jnp.concatenate(own_heads, axis=0)
    high, low = hi_lo((dot(stacked, one) + add_one) * (dot(stacked, two) + add_two))
    for pair in range(PAIRS // 2):
        here = pl.ds(pl.multiple_of(half * wide + pair * LANES, LANES), LANES)
        wanted = jnp.where(target < VHEAD, 16 * pair, 16 * pair + 8)
        spread = dot(norms, jnp.where(source == wanted, 1.0, 0.0).astype(BF16)).astype(BF16)
        right = jnp.concatenate([past_ref[pair * ROWS : (pair + 1) * ROWS, :], spread], axis=1)
        mine = slice(2 * pair * rows, (2 * pair + 2) * rows)
        result = dot(high[mine], right) + dot(low[mine], right)
        numer = jnp.where(lower, result[:rows, :LANES], result[rows:, :LANES]) + numer_ref[:, here]
        denom = jnp.where(lower, result[:rows, LANES:], result[rows:, LANES:]) + denom_ref[:, here]
        mixed = (numer / denom + swa_ref[:, here]).astype(BF16)
        out_ref[:, pair * LANES : (pair + 1) * LANES] = mixed
        if not own:
            done = out_ref.at[:, pair * LANES : (pair + 1) * LANES]
            copies.append(pltpu.make_async_copy(done, out_hbm.at[:, here], sems.at[pair]))
            copies[-1].start()
    for copy in copies:
        copy.wait()


IN_VMEM = pl.BlockSpec(memory_space=pltpu.VMEM)
IN_HBM = pl.BlockSpec(memory_space=pltpu.HBM)


def call(kernel, outs, args, specs, out_specs, scratch=()):
    placed = [pltpu.with_memory_space_constraint(a, spec.memory_space) for a, spec in zip(args, specs)]
    results = jax.tree.map(lambda out, spec: spec.memory_space(out.shape, out.dtype), outs, out_specs)
    return pl.pallas_call(
        kernel,
        out_shape=results,
        in_specs=specs,
        out_specs=out_specs,
        scratch_shapes=scratch,
        compiler_params=pltpu.CompilerParams(vmem_limit_bytes=16 * 1024 * 1024),
    )(*placed)


def shards(lin_qk, lin_v, conv_w, swa_qkv):
    rows = lin_qk.shape[0]
    taps = conv_w.shape[0]
    chips = lax.axis_size(BLOCK) // 2
    part = PAIRS // 2 * ROWS // chips
    held = (part + 7) // 8 * 8 + EXTRA
    shape = jax.ShapeDtypeStruct

    def swap(array):
        return lax.ppermute(array, BLOCK, [(i, i ^ 1) for i in range(2 * chips)])

    def exchange(array):
        groups = [[2 * chip + core for chip in group_order(chips)] for core in range(2)]
        return lax.all_to_all(array, BLOCK, 0, 0, axis_index_groups=groups, tiled=True)

    other_qk, other_v = swap(lin_qk), swap(lin_v)
    half_wide = lin_v.shape[1] // 2
    own_sums, tails, conv_half = call(
        functools.partial(state_kernel, part, True),
        [
            shape((chips, held, LANES), jnp.float32),
            shape((WINDOW + TAIL, swa_qkv.shape[1] // 3 * 2), BF16),
            shape((taps, half_wide), jnp.float32),
        ],
        [lin_qk, lin_v, conv_w, swa_qkv],
        [IN_HBM] * 4,
        [IN_VMEM] * 3,
        [
            pltpu.VMEM((rows, LANES), BF16),
            pltpu.VMEM((rows, half_wide), BF16),
            pltpu.SemaphoreType.DMA((5,)),
        ],
    )
    sums = call(
        functools.partial(state_kernel, part, False),
        shape((chips, held, LANES), BF16),
        [other_qk, other_v, conv_half, own_sums],
        [IN_VMEM] * 4,
        IN_VMEM,
    )
    sums, tails = lax.optimization_barrier((sums, tails))
    parts = exchange(sums)
    tails = lax.ppermute(tails, BLOCK, [(i, i + 1) for i in range(2 * chips - 1)])
    past = call(
        functools.partial(prefix_kernel, taps),
        shape((chips, part, LANES), BF16),
        [parts],
        [IN_VMEM],
        IN_VMEM,
    )
    here = exchange(past).reshape(chips * part, LANES)
    wide = shape(lin_v.shape, jnp.float32)
    numer, denom, swa = call(
        local_kernel,
        [wide, wide, wide],
        [lin_qk, lin_v, conv_w, swa_qkv, tails, other_qk, other_v],
        [IN_VMEM] * 7,
        [IN_VMEM] * 3,
    )
    here, numer, denom, swa = lax.optimization_barrier((here, numer, denom, swa))
    there = swap(here)
    own_out = call(
        functools.partial(readout_kernel, True),
        shape((rows, half_wide), BF16),
        [lin_qk, numer, denom, swa, here],
        [IN_VMEM] * 5,
        IN_VMEM,
    )
    return call(
        functools.partial(readout_kernel, False),
        shape(lin_v.shape, BF16),
        [lin_qk, numer, denom, swa, there, own_out],
        [IN_VMEM] * 6,
        IN_HBM,
        [pltpu.VMEM((rows, half_wide), BF16), pltpu.SemaphoreType.DMA((PAIRS // 2 + 1,))],
    )


def solution(mesh):
    blocks = jax.sharding.Mesh(mesh.devices.reshape(-1), (BLOCK,))
    return jax.shard_map(
        shards,
        mesh=blocks,
        in_specs=(P(BLOCK, None), P(BLOCK, None), P(), P(BLOCK, None)),
        out_specs=P(BLOCK, None),
        check_vma=False,
    )
```

```python
import functools

import jax
import jax.numpy as jnp
import numpy as np
from jax import lax
from jax.experimental import pallas as pl
from jax.experimental.pallas import tpu as pltpu
from jax.sharding import PartitionSpec as P

HEADS = 16
FEAT = 16
VHEAD = 64
SWA_HEADS = 8
SWA_HEAD = 128
WINDOW = 64

BLOCK = "block"
ORDER_SEED = 81
LANES = 128
PAIRS = HEADS // 2
QUADS = FEAT * (FEAT + 1) // 2
CONST = QUADS + FEAT
ROWS = 160
TAIL = 16
EXTRA = 8
BLOCK_EXTRA = 4


NT = (((1,), (1,)), ((), ()))
NN = (((1,), (0,)), ((), ()))
BF16 = jnp.bfloat16


def dot(a, b, dims=NN):
    return lax.dot_general(a, b, dims, preferred_element_type=jnp.float32)


def iota(shape, dim):
    return lax.broadcasted_iota(jnp.int32, shape, dim)


def selector(feature, lane, second, halved=False):
    scale = FEAT ** (-0.25)
    quad = feature < QUADS
    entry = feature % FEAT
    if second:
        wanted = (feature + feature // FEAT) % FEAT
        return jnp.where((lane % FEAT == wanted) & quad, scale, 0.0)
    linear = (feature >= QUADS) & (feature < CONST)
    wanted = jnp.where(quad, entry, (feature - QUADS) % FEAT)
    weight = jnp.where((feature < FEAT) & halved, 0.5 * scale, scale)
    return jnp.where((lane % FEAT == wanted) & (quad | linear), weight, 0.0)


def adders(feature):
    first = jnp.where(feature == CONST, 1.0, 0.0)
    second = jnp.where((feature >= QUADS) & (feature <= CONST), 1.0, 0.0)
    return first, second


def group_order(chips):
    return [int(chip) for chip in np.random.RandomState(ORDER_SEED).permutation(chips)]


def head_mask(head, shape):
    place = iota(shape, 1)
    return (place >= head * FEAT) & (place < (head + 1) * FEAT)


def hi_lo(values):
    high = values.astype(BF16)
    return high, (values - high.astype(jnp.float32)).astype(BF16)


def convolved(value, tail, conv_ref, lanes):
    row_id = iota(value.shape, 0)
    result = conv_ref[0:1, lanes] * value
    for lag in range(1, conv_ref.shape[0]):
        shifted = pltpu.roll(value, lag, 0)
        for row in range(lag):
            source = TAIL - lag + row
            before = 0.0 if tail is None else tail[source : source + 1]
            shifted = jnp.where(row_id == row, before, shifted)
        result = result + conv_ref[lag : lag + 1, lanes] * shifted
    return result.astype(BF16)


def state_kernel(part, own, *refs):
    core = lax.axis_index(BLOCK) % 2
    if own:
        qk_hbm, v_hbm, conv_hbm, swa_hbm, out_ref, tails_ref, conv_ref, key_ref, v_ref, sems = refs
        rows, wide = v_hbm.shape
    else:
        qk_ref, v_ref, conv_ref, own_ref, out_ref = refs
        rows, wide = v_ref.shape
    taps = conv_ref.shape[0]
    mine = pl.ds(pl.multiple_of(core * (wide // 2), wide // 2), wide // 2)
    keys = pl.ds(pl.multiple_of(HEADS * FEAT + core * LANES, LANES), LANES)
    if own:
        pieces = [
            (qk_hbm.at[:, keys], key_ref),
            (conv_hbm.at[:, mine], conv_ref),
            (v_hbm.at[:, mine], v_ref),
            (swa_hbm.at[rows - WINDOW :, tails_ref.shape[1] // 2 :], tails_ref.at[:WINDOW, :]),
            (v_hbm.at[rows - TAIL :, :], tails_ref.at[WINDOW:, :wide]),
        ]
        copies = [pltpu.make_async_copy(a, b, sems.at[i]) for i, (a, b) in enumerate(pieces)]
        for copy in copies:
            copy.start()
        copies[0].wait()
        key = key_ref[...]
    else:
        copies = []
        key = qk_ref[:, keys]
    key_t = (key.astype(jnp.float32) * FEAT ** (-0.25)).T
    const_rows = jnp.where(iota((EXTRA, rows), 0) == 0, 1.0, 0.0)
    lane_id = iota((ROWS, LANES), 1)
    low_row = iota((EXTRA, LANES), 0)
    ones = jnp.ones((rows, LANES), BF16)
    half = FEAT // 2
    padded = (part + 7) // 8 * 8
    lefts = []
    for head in range(HEADS // 2):
        x = key_t[head * FEAT : (head + 1) * FEAT]
        blocks = [x * x]
        for by in range(1, half):
            blocks.append(x * jnp.concatenate([x[by:], x[:by]], axis=0))
        blocks += [x[:half] * x[half:], x, const_rows]
        lefts.append(jnp.concatenate(hi_lo(jnp.concatenate(blocks, axis=0)), axis=1))
    first_keys = key[:16].astype(jnp.float32)
    slot = low_row - BLOCK_EXTRA * (core if own else 1 - core)
    for copy in copies[1:3]:
        copy.wait()
    states = []
    extras = []
    norms = jnp.zeros((ROWS, LANES), jnp.float32)
    for pair in range(PAIRS // 2):
        lanes = slice(pair * LANES, (pair + 1) * LANES)
        at = pl.multiple_of((0 if own else core * (wide // 2)) + pair * LANES, LANES)
        value = v_ref[:, pl.ds(at, LANES)].astype(jnp.float32)
        conved = convolved(value, None, conv_ref, lanes)
        right = jnp.concatenate([conved, ones], axis=1)
        right = jnp.concatenate([right, right], axis=0)
        both = []
        for head in (2 * pair, 2 * pair + 1):
            result = dot(lefts[head], right)
            both.append(result[:, :LANES])
            norms = jnp.where(lane_id // 8 == head, result[:, LANES:], norms)
        states.append(jnp.where(lane_id < VHEAD, both[0], both[1]))
        extra = jnp.zeros((EXTRA, LANES), jnp.float32)
        for row in range(taps - 1):
            share = jnp.zeros((1, LANES), jnp.float32)
            for lag in range(row + 1, taps):
                last = rows + row - lag
                share = share + conv_ref[lag : lag + 1, lanes] * value[last : last + 1]
            extra = jnp.where(slot == row, share, extra)
            extra = jnp.where(slot == taps - 1 + row, first_keys[row : row + 1], extra)
        extras.append(extra)
    norms_t = norms.T
    for pair in range(PAIRS // 2):
        last = states[pair][CONST:]
        for place in range(2):
            at = 8 * (2 * pair + place)
            norm = norms_t[at : at + 8]
            rest = jnp.concatenate(
                [norm[:, LANES:], jnp.zeros((8, 2 * LANES - ROWS), jnp.float32)], axis=1
            )
            last = jnp.where(low_row == 1 + 2 * place, norm[:, :LANES], last)
            last = jnp.where(low_row == 2 + 2 * place, rest, last)
        state = jnp.concatenate([states[pair][:CONST], last], axis=0)
        for piece in range(ROWS // part):
            rows_of = [state[piece * part : (piece + 1) * part]]
            if padded != part:
                rows_of.append(jnp.zeros((padded - part, LANES), jnp.float32))
            message = jnp.concatenate(rows_of + [extras[pair]], axis=0)
            chunk = pair * (ROWS // part) + piece
            if own:
                out_ref[chunk] = message
            else:
                out_ref[chunk] = (own_ref[chunk] + message).astype(BF16)
    for copy in copies[3:]:
        copy.wait()


def prefix_kernel(taps, parts_ref, out_ref):
    chips, held, _ = parts_ref.shape
    part = out_ref.shape[1]
    padded = held - EXTRA
    width = chips * EXTRA
    block = lax.axis_index(BLOCK)
    places = list(np.argsort(group_order(chips)))
    place = sum(jnp.where(block // 2 == chip, int(at), 0) for chip, at in enumerate(places))
    start = block % 2 * (ROWS * PAIRS // 2) + place * part
    head = start // ROWS * 2 % (LANES // FEAT)
    feature = start % ROWS + iota((padded, LANES), 0)
    lane = iota((padded, LANES), 1)
    one = selector(feature, lane, False)
    two = selector(feature, lane, True)
    add_one, add_two = adders(feature[:, 0:1])
    extras = jnp.concatenate(
        [parts_ref[int(at)].astype(jnp.float32)[padded:] for at in places], axis=0
    )
    extras_low = extras.astype(BF16)
    upper = iota((width, LANES), 1) >= VHEAD
    lefts = []
    rights = []
    for place in range(2):
        mine = lane // FEAT == head + place
        first = dot(jnp.where(mine, one, 0.0).astype(BF16), extras_low, NT) + add_one
        second = dot(jnp.where(mine, two, 0.0).astype(BF16), extras_low, NT) + add_two
        lefts.append(pltpu.roll(first * second, width - BLOCK_EXTRA - (taps - 1), 1))
        rights.append(jnp.where(upper == (place == 1), extras, 0.0).astype(BF16))
    left = jnp.concatenate(lefts, axis=1)
    right = jnp.concatenate(rights, axis=0)
    column = iota(left.shape, 1) % width
    to_block = jnp.where(column % BLOCK_EXTRA < taps - 1, column // BLOCK_EXTRA + 1, 2 * chips)

    total = jnp.zeros((padded, LANES), jnp.float32)
    for chip, at in enumerate(places):
        seen = jnp.where(to_block <= 2 * chip, left, 0.0).astype(BF16)
        out_ref[int(at)] = (total + dot(seen, right))[:part].astype(BF16)
        total = total + parts_ref[int(at)].astype(jnp.float32)[:padded]


def local_kernel(
    qk_ref, v_ref, conv_ref, swa_ref, tails_ref, other_qk_ref, other_v_ref,
    numer_ref, denom_ref, swa_out_ref,
):
    rows = v_ref.shape[0]
    taps = conv_ref.shape[0]
    width = HEADS * FEAT
    core = lax.axis_index(BLOCK) % 2
    second = core == 1
    first_block = lax.axis_index(BLOCK) == 0
    query = qk_ref[:, :width]
    key = qk_ref[:, width : 2 * width]
    lower = iota((rows, LANES), 1) < VHEAD
    causal = iota((rows, rows), 1) <= iota((rows, rows), 0)
    row_id = iota((rows, LANES), 0)
    ones = jnp.ones((rows, LANES), BF16)
    counted = jnp.where(second, ones, jnp.zeros_like(ones))
    more_key = jnp.where(second, other_qk_ref[:, width : 2 * width], key)
    all_keys = jnp.concatenate([key, more_key], axis=0)
    allowed = jnp.concatenate([causal, causal | True], axis=1)
    group_heads = 4
    for group in range(0, HEADS, group_heads):
        own = jnp.concatenate(
            [
                jnp.where(head_mask(head, query.shape), query, jnp.zeros_like(query))
                for head in range(group, group + group_heads)
            ],
            axis=0,
        )
        score = dot(own, all_keys, NT) * FEAT ** (-0.5)
        weight = 1.0 + score + 0.5 * score * score
        weight = jnp.where(jnp.concatenate([allowed] * group_heads, axis=0), weight, 0.0).astype(BF16)
        for at in range(group_heads // 2):
            pair = group // 2 + at
            lanes = slice(pair * LANES, (pair + 1) * LANES)
            tail = jnp.where(first_block, 0.0, tails_ref[WINDOW:, lanes].astype(jnp.float32))
            conved = convolved(v_ref[:, lanes].astype(jnp.float32), tail, conv_ref, lanes)
            before = convolved(other_v_ref[:, lanes].astype(jnp.float32), None, conv_ref, lanes)
            shares = jnp.zeros((rows, LANES), jnp.float32)
            for row in range(taps - 1):
                share = jnp.zeros((1, LANES), jnp.float32)
                for lag in range(row + 1, taps):
                    at_row = TAIL + row - lag
                    share = share + conv_ref[lag : lag + 1, lanes] * tail[at_row : at_row + 1]
                shares = jnp.where(row_id == row, -share, shares)
            before = jnp.where(second, before, shares.astype(BF16))
            right = jnp.concatenate([conved, ones], axis=1)
            right = jnp.concatenate([right, jnp.concatenate([before, counted], axis=1)], axis=0)
            result = dot(weight[2 * at * rows : (2 * at + 2) * rows], right)
            top, bottom = result[:rows], result[rows:]
            numer_ref[:, lanes] = jnp.where(lower, top[:, :LANES], bottom[:, :LANES])
            denom_ref[:, lanes] = jnp.where(lower, top[:, LANES:], bottom[:, LANES:])
    swa_width = SWA_HEADS * SWA_HEAD
    not_before = jnp.where(first_block, WINDOW, 0)
    span = 2 * WINDOW
    place = iota((WINDOW, span), 1)
    row = iota((WINDOW, span), 0)
    inside = (place > row) & (place <= row + WINDOW)
    inside_first = inside & (place >= not_before)
    for step in range(rows // WINDOW):
        mine = slice(step * WINDOW, (step + 1) * WINDOW)
        window = slice((step - 1) * WINDOW, (step + 1) * WINDOW)

        def around(head, start):
            here = slice(start + head * SWA_HEAD, start + (head + 1) * SWA_HEAD)
            if step:
                return swa_ref[window, here]
            there = slice(here.start - swa_width, here.stop - swa_width)
            return jnp.concatenate([tails_ref[:WINDOW, there], swa_ref[mine, here]], axis=0)

        scores = []
        for head in range(SWA_HEADS):
            own = swa_ref[mine, head * SWA_HEAD : (head + 1) * SWA_HEAD]
            score = dot(own, around(head, swa_width), NT) * SWA_HEAD ** (-0.5)
            scores.append(jnp.where(inside if step else inside_first, score, -jnp.inf))
        scores = jnp.concatenate(scores, axis=0)
        expo = jnp.exp(scores - jnp.max(scores, axis=-1, keepdims=True))
        probs = (expo / jnp.sum(expo, axis=-1, keepdims=True)).astype(BF16)
        for head in range(SWA_HEADS):
            own = probs[head * WINDOW : (head + 1) * WINDOW]
            swa_out_ref[mine, head * SWA_HEAD : (head + 1) * SWA_HEAD] = dot(
                own, around(head, 2 * swa_width)
            )


def readout_kernel(own, qk_ref, numer_ref, denom_ref, swa_ref, past_ref, *refs):
    core = lax.axis_index(BLOCK) % 2
    half = core if own else 1 - core
    rows = qk_ref.shape[0]
    wide = PAIRS // 2 * LANES
    copies = []
    if own:
        (out_ref,) = refs
    else:
        own_ref, out_hbm, out_ref, sems = refs
        there = pl.ds(pl.multiple_of(core * wide, wide), wide)
        copies.append(pltpu.make_async_copy(own_ref, out_hbm.at[:, there], sems.at[PAIRS // 2]))
        copies[0].start()
    lower = iota((rows, LANES), 1) < VHEAD
    query = qk_ref[:, pl.ds(pl.multiple_of(half * LANES, LANES), LANES)]
    feature = iota((LANES, ROWS), 1)
    lane = iota((LANES, ROWS), 0)
    one = selector(feature, lane, False, halved=True).astype(BF16)
    two = selector(feature, lane, True).astype(BF16)
    add_one, add_two = adders(iota((8, ROWS), 1)[0:1])
    norms = []
    for pair in range(PAIRS // 2):
        last = past_ref[(pair + 1) * ROWS - 16 : (pair + 1) * ROWS, :].astype(jnp.float32)
        for place in range(2):
            at = 16 - (ROWS - CONST) + 1 + 2 * place
            norm = jnp.concatenate([last[at : at + 1], last[at + 1 : at + 2, : ROWS - LANES]], axis=1)
            norms.append(jnp.broadcast_to(norm, (8, ROWS)))
    norms = jnp.concatenate(norms + [jnp.zeros((LANES // 2, ROWS), jnp.float32)], axis=0).T.astype(BF16)
    source = iota((LANES, LANES), 0)
    target = iota((LANES, LANES), 1)
    own_heads = [
        jnp.where(head_mask(head, query.shape), query, jnp.zeros_like(query)) for head in range(HEADS // 2)
    ]
    stacked = jnp.concatenate(own_heads, axis=0)
    high, low = hi_lo((dot(stacked, one) + add_one) * (dot(stacked, two) + add_two))
    for pair in range(PAIRS // 2):
        here = pl.ds(pl.multiple_of(half * wide + pair * LANES, LANES), LANES)
        wanted = jnp.where(target < VHEAD, 16 * pair, 16 * pair + 8)
        spread = dot(norms, jnp.where(source == wanted, 1.0, 0.0).astype(BF16)).astype(BF16)
        right = jnp.concatenate([past_ref[pair * ROWS : (pair + 1) * ROWS, :], spread], axis=1)
        mine = slice(2 * pair * rows, (2 * pair + 2) * rows)
        result = dot(high[mine], right) + dot(low[mine], right)
        numer = jnp.where(lower, result[:rows, :LANES], result[rows:, :LANES]) + numer_ref[:, here]
        denom = jnp.where(lower, result[:rows, LANES:], result[rows:, LANES:]) + denom_ref[:, here]
        mixed = (numer / denom + swa_ref[:, here]).astype(BF16)
        out_ref[:, pair * LANES : (pair + 1) * LANES] = mixed
        if not own:
            done = out_ref.at[:, pair * LANES : (pair + 1) * LANES]
            copies.append(pltpu.make_async_copy(done, out_hbm.at[:, here], sems.at[pair]))
            copies[-1].start()
    for copy in copies:
        copy.wait()


IN_VMEM = pl.BlockSpec(memory_space=pltpu.VMEM)
IN_HBM = pl.BlockSpec(memory_space=pltpu.HBM)


def call(kernel, outs, args, specs, out_specs, scratch=()):
    placed = [pltpu.with_memory_space_constraint(a, spec.memory_space) for a, spec in zip(args, specs)]
    results = jax.tree.map(lambda out, spec: spec.memory_space(out.shape, out.dtype), outs, out_specs)
    return pl.pallas_call(
        kernel,
        out_shape=results,
        in_specs=specs,
        out_specs=out_specs,
        scratch_shapes=scratch,
        compiler_params=pltpu.CompilerParams(vmem_limit_bytes=16 * 1024 * 1024),
    )(*placed)


def shards(lin_qk, lin_v, conv_w, swa_qkv):
    rows = lin_qk.shape[0]
    taps = conv_w.shape[0]
    chips = lax.axis_size(BLOCK) // 2
    part = PAIRS // 2 * ROWS // chips
    held = (part + 7) // 8 * 8 + EXTRA
    shape = jax.ShapeDtypeStruct

    def swap(array):
        return lax.ppermute(array, BLOCK, [(i, i ^ 1) for i in range(2 * chips)])

    def exchange(array):
        groups = [[2 * chip + core for chip in group_order(chips)] for core in range(2)]
        return lax.all_to_all(array, BLOCK, 0, 0, axis_index_groups=groups, tiled=True)

    other_qk, other_v = swap(lin_qk), swap(lin_v)
    half_wide = lin_v.shape[1] // 2
    own_sums, tails, conv_half = call(
        functools.partial(state_kernel, part, True),
        [
            shape((chips, held, LANES), jnp.float32),
            shape((WINDOW + TAIL, swa_qkv.shape[1] // 3 * 2), BF16),
            shape((taps, half_wide), jnp.float32),
        ],
        [lin_qk, lin_v, conv_w, swa_qkv],
        [IN_HBM] * 4,
        [IN_VMEM] * 3,
        [
            pltpu.VMEM((rows, LANES), BF16),
            pltpu.VMEM((rows, half_wide), BF16),
            pltpu.SemaphoreType.DMA((5,)),
        ],
    )
    sums = call(
        functools.partial(state_kernel, part, False),
        shape((chips, held, LANES), BF16),
        [other_qk, other_v, conv_half, own_sums],
        [IN_VMEM] * 4,
        IN_VMEM,
    )
    sums, tails = lax.optimization_barrier((sums, tails))
    parts = exchange(sums)
    tails = lax.ppermute(tails, BLOCK, [(i, i + 1) for i in range(2 * chips - 1)])
    past = call(
        functools.partial(prefix_kernel, taps),
        shape((chips, part, LANES), BF16),
        [parts],
        [IN_VMEM],
        IN_VMEM,
    )
    here = exchange(past).reshape(chips * part, LANES)
    wide = shape(lin_v.shape, jnp.float32)
    numer, denom, swa = call(
        local_kernel,
        [wide, wide, wide],
        [lin_qk, lin_v, conv_w, swa_qkv, tails, other_qk, other_v],
        [IN_VMEM] * 7,
        [IN_VMEM] * 3,
    )
    here, numer, denom, swa = lax.optimization_barrier((here, numer, denom, swa))
    there = swap(here)
    own_out = call(
        functools.partial(readout_kernel, True),
        shape((rows, half_wide), BF16),
        [lin_qk, numer, denom, swa, here],
        [IN_VMEM] * 5,
        IN_VMEM,
    )
    return call(
        functools.partial(readout_kernel, False),
        shape(lin_v.shape, BF16),
        [lin_qk, numer, denom, swa, there, own_out],
        [IN_VMEM] * 6,
        IN_HBM,
        [pltpu.VMEM((rows, half_wide), BF16), pltpu.SemaphoreType.DMA((PAIRS // 2 + 1,))],
    )


def solution(mesh):
    blocks = jax.sharding.Mesh(mesh.devices.reshape(-1), (BLOCK,))
    return jax.shard_map(
        shards,
        mesh=blocks,
        in_specs=(P(BLOCK, None), P(BLOCK, None), P(), P(BLOCK, None)),
        out_specs=P(BLOCK, None),
        check_vma=False,
    )
```

```python
import functools

import jax
import jax.numpy as jnp
import numpy as np
from jax import lax
from jax.experimental import pallas as pl
from jax.experimental.pallas import tpu as pltpu
from jax.sharding import PartitionSpec as P

HEADS = 16
FEAT = 16
VHEAD = 64
SWA_HEADS = 8
SWA_HEAD = 128
WINDOW = 64

BLOCK = "block"
ORDER_SEED = 81
LANES = 128
PAIRS = HEADS // 2
QUADS = FEAT * (FEAT + 1) // 2
CONST = QUADS + FEAT
ROWS = 160
TAIL = 16
EXTRA = 8
BLOCK_EXTRA = 4


NT = (((1,), (1,)), ((), ()))
NN = (((1,), (0,)), ((), ()))
BF16 = jnp.bfloat16


def dot(a, b, dims=NN):
    return lax.dot_general(a, b, dims, preferred_element_type=jnp.float32)


def iota(shape, dim):
    return lax.broadcasted_iota(jnp.int32, shape, dim)


def selector(feature, lane, second, halved=False):
    scale = FEAT ** (-0.25)
    quad = feature < QUADS
    entry = feature % FEAT
    if second:
        wanted = (feature + feature // FEAT) % FEAT
        return jnp.where((lane % FEAT == wanted) & quad, scale, 0.0)
    linear = (feature >= QUADS) & (feature < CONST)
    wanted = jnp.where(quad, entry, (feature - QUADS) % FEAT)
    weight = jnp.where((feature < FEAT) & halved, 0.5 * scale, scale)
    return jnp.where((lane % FEAT == wanted) & (quad | linear), weight, 0.0)


def adders(feature):
    first = jnp.where(feature == CONST, 1.0, 0.0)
    second = jnp.where((feature >= QUADS) & (feature <= CONST), 1.0, 0.0)
    return first, second


def group_order(chips):
    return [int(chip) for chip in np.random.RandomState(ORDER_SEED).permutation(chips)]


def head_mask(head, shape):
    place = iota(shape, 1)
    return (place >= head * FEAT) & (place < (head + 1) * FEAT)


def hi_lo(values):
    high = values.astype(BF16)
    return high, (values - high.astype(jnp.float32)).astype(BF16)


def convolved(value, tail, conv_ref, lanes):
    row_id = iota(value.shape, 0)
    result = conv_ref[0:1, lanes] * value
    for lag in range(1, conv_ref.shape[0]):
        shifted = pltpu.roll(value, lag, 0)
        for row in range(lag):
            source = TAIL - lag + row
            before = 0.0 if tail is None else tail[source : source + 1]
            shifted = jnp.where(row_id == row, before, shifted)
        result = result + conv_ref[lag : lag + 1, lanes] * shifted
    return result.astype(BF16)


def state_kernel(part, own, *refs):
    core = lax.axis_index(BLOCK) % 2
    if own:
        qk_hbm, v_hbm, conv_hbm, swa_hbm, out_ref, tails_ref, conv_ref, key_ref, v_ref, sems = refs
        rows, wide = v_hbm.shape
    else:
        qk_ref, v_ref, conv_ref, own_ref, out_ref = refs
        rows, wide = v_ref.shape
    taps = conv_ref.shape[0]
    mine = pl.ds(pl.multiple_of(core * (wide // 2), wide // 2), wide // 2)
    keys = pl.ds(pl.multiple_of(HEADS * FEAT + core * LANES, LANES), LANES)
    if own:
        pieces = [
            (qk_hbm.at[:, keys], key_ref),
            (conv_hbm.at[:, mine], conv_ref),
            (v_hbm.at[:, mine], v_ref),
            (swa_hbm.at[rows - WINDOW :, tails_ref.shape[1] // 2 :], tails_ref.at[:WINDOW, :]),
            (v_hbm.at[rows - TAIL :, :], tails_ref.at[WINDOW:, :wide]),
        ]
        copies = [pltpu.make_async_copy(a, b, sems.at[i]) for i, (a, b) in enumerate(pieces)]
        for copy in copies:
            copy.start()
        copies[0].wait()
        key = key_ref[...]
    else:
        copies = []
        key = qk_ref[:, keys]
    key_t = (key.astype(jnp.float32) * FEAT ** (-0.25)).T
    const_rows = jnp.where(iota((EXTRA, rows), 0) == 0, 1.0, 0.0)
    lane_id = iota((ROWS, LANES), 1)
    low_row = iota((EXTRA, LANES), 0)
    ones = jnp.ones((rows, LANES), BF16)
    half = FEAT // 2
    padded = (part + 7) // 8 * 8
    lefts = []
    for head in range(HEADS // 2):
        x = key_t[head * FEAT : (head + 1) * FEAT]
        blocks = [x * x]
        for by in range(1, half):
            blocks.append(x * jnp.concatenate([x[by:], x[:by]], axis=0))
        blocks += [x[:half] * x[half:], x, const_rows]
        lefts.append(jnp.concatenate(hi_lo(jnp.concatenate(blocks, axis=0)), axis=1))
    first_keys = key[:16].astype(jnp.float32)
    slot = low_row - BLOCK_EXTRA * (core if own else 1 - core)
    for copy in copies[1:3]:
        copy.wait()
    states = []
    extras = []
    norms = jnp.zeros((ROWS, LANES), jnp.float32)
    for pair in range(PAIRS // 2):
        lanes = slice(pair * LANES, (pair + 1) * LANES)
        at = pl.multiple_of((0 if own else core * (wide // 2)) + pair * LANES, LANES)
        value = v_ref[:, pl.ds(at, LANES)].astype(jnp.float32)
        conved = convolved(value, None, conv_ref, lanes)
        right = jnp.concatenate([conved, ones], axis=1)
        right = jnp.concatenate([right, right], axis=0)
        both = []
        for head in (2 * pair, 2 * pair + 1):
            result = dot(lefts[head], right)
            both.append(result[:, :LANES])
            norms = jnp.where(lane_id // 8 == head, result[:, LANES:], norms)
        states.append(jnp.where(lane_id < VHEAD, both[0], both[1]))
        extra = jnp.zeros((EXTRA, LANES), jnp.float32)
        for row in range(taps - 1):
            share = jnp.zeros((1, LANES), jnp.float32)
            for lag in range(row + 1, taps):
                last = rows + row - lag
                share = share + conv_ref[lag : lag + 1, lanes] * value[last : last + 1]
            extra = jnp.where(slot == row, share, extra)
            extra = jnp.where(slot == taps - 1 + row, first_keys[row : row + 1], extra)
        extras.append(extra)
    norms_t = norms.T
    for pair in range(PAIRS // 2):
        last = states[pair][CONST:]
        for place in range(2):
            at = 8 * (2 * pair + place)
            norm = norms_t[at : at + 8]
            rest = jnp.concatenate(
                [norm[:, LANES:], jnp.zeros((8, 2 * LANES - ROWS), jnp.float32)], axis=1
            )
            last = jnp.where(low_row == 1 + 2 * place, norm[:, :LANES], last)
            last = jnp.where(low_row == 2 + 2 * place, rest, last)
        state = jnp.concatenate([states[pair][:CONST], last], axis=0)
        for piece in range(ROWS // part):
            rows_of = [state[piece * part : (piece + 1) * part]]
            if padded != part:
                rows_of.append(jnp.zeros((padded - part, LANES), jnp.float32))
            message = jnp.concatenate(rows_of + [extras[pair]], axis=0)
            chunk = pair * (ROWS // part) + piece
            if own:
                out_ref[chunk] = message
            else:
                out_ref[chunk] = (own_ref[chunk] + message).astype(BF16)
    for copy in copies[3:]:
        copy.wait()


def prefix_kernel(taps, parts_ref, out_ref):
    chips, held, _ = parts_ref.shape
    part = out_ref.shape[1]
    padded = held - EXTRA
    width = chips * EXTRA
    block = lax.axis_index(BLOCK)
    places = list(np.argsort(group_order(chips)))
    place = sum(jnp.where(block // 2 == chip, int(at), 0) for chip, at in enumerate(places))
    start = block % 2 * (ROWS * PAIRS // 2) + place * part
    head = start // ROWS * 2 % (LANES // FEAT)
    feature = start % ROWS + iota((padded, LANES), 0)
    lane = iota((padded, LANES), 1)
    one = selector(feature, lane, False)
    two = selector(feature, lane, True)
    add_one, add_two = adders(feature[:, 0:1])
    extras = jnp.concatenate(
        [parts_ref[int(at)].astype(jnp.float32)[padded:] for at in places], axis=0
    )
    extras_low = extras.astype(BF16)
    upper = iota((width, LANES), 1) >= VHEAD
    heads = [lane // FEAT == head + place for place in range(2)]
    factors = [jnp.where(mine, factor, 0.0) for factor in (one, two) for mine in heads]
    products = dot(jnp.concatenate(factors, axis=0).astype(BF16), extras_low, NT)
    lefts = []
    rights = []
    for side in range(2):
        first = products[side * padded : (side + 1) * padded] + add_one
        second = products[(side + 2) * padded : (side + 3) * padded] + add_two
        lefts.append(pltpu.roll(first * second, width - BLOCK_EXTRA - (taps - 1), 1))
        rights.append(jnp.where(upper == (side == 1), extras, 0.0).astype(BF16))
    left = jnp.concatenate(lefts, axis=1)
    right = jnp.concatenate(rights, axis=0)
    column = iota(left.shape, 1) % width
    to_block = jnp.where(column % BLOCK_EXTRA < taps - 1, column // BLOCK_EXTRA + 1, 2 * chips)

    seen = [jnp.where(to_block <= 2 * chip, left, 0.0).astype(BF16) for chip in range(chips)]
    added = dot(jnp.concatenate(seen, axis=0), right)
    total = jnp.zeros((padded, LANES), jnp.float32)
    for chip, at in enumerate(places):
        result = total + added[chip * padded : (chip + 1) * padded]
        out_ref[int(at)] = result[:part].astype(BF16)
        total = total + parts_ref[int(at)].astype(jnp.float32)[:padded]


def local_kernel(
    qk_ref, v_ref, conv_ref, swa_ref, tails_ref, other_qk_ref, other_v_ref,
    numer_ref, denom_ref, swa_out_ref,
):
    rows = v_ref.shape[0]
    taps = conv_ref.shape[0]
    width = HEADS * FEAT
    core = lax.axis_index(BLOCK) % 2
    second = core == 1
    first_block = lax.axis_index(BLOCK) == 0
    query = qk_ref[:, :width]
    key = qk_ref[:, width : 2 * width]
    lower = iota((rows, LANES), 1) < VHEAD
    causal = iota((rows, rows), 1) <= iota((rows, rows), 0)
    row_id = iota((rows, LANES), 0)
    ones = jnp.ones((rows, LANES), BF16)
    counted = jnp.where(second, ones, jnp.zeros_like(ones))
    more_key = jnp.where(second, other_qk_ref[:, width : 2 * width], key)
    all_keys = jnp.concatenate([key, more_key], axis=0)
    allowed = jnp.concatenate([causal, causal | True], axis=1)
    group_heads = 4
    for group in range(0, HEADS, group_heads):
        own = jnp.concatenate(
            [
                jnp.where(head_mask(head, query.shape), query, jnp.zeros_like(query))
                for head in range(group, group + group_heads)
            ],
            axis=0,
        )
        score = dot(own, all_keys, NT) * FEAT ** (-0.5)
        weight = 1.0 + score + 0.5 * score * score
        weight = jnp.where(jnp.concatenate([allowed] * group_heads, axis=0), weight, 0.0).astype(BF16)
        for at in range(group_heads // 2):
            pair = group // 2 + at
            lanes = slice(pair * LANES, (pair + 1) * LANES)
            tail = jnp.where(first_block, 0.0, tails_ref[WINDOW:, lanes].astype(jnp.float32))
            conved = convolved(v_ref[:, lanes].astype(jnp.float32), tail, conv_ref, lanes)
            before = convolved(other_v_ref[:, lanes].astype(jnp.float32), None, conv_ref, lanes)
            shares = jnp.zeros((rows, LANES), jnp.float32)
            for row in range(taps - 1):
                share = jnp.zeros((1, LANES), jnp.float32)
                for lag in range(row + 1, taps):
                    at_row = TAIL + row - lag
                    share = share + conv_ref[lag : lag + 1, lanes] * tail[at_row : at_row + 1]
                shares = jnp.where(row_id == row, -share, shares)
            before = jnp.where(second, before, shares.astype(BF16))
            right = jnp.concatenate([conved, ones], axis=1)
            right = jnp.concatenate([right, jnp.concatenate([before, counted], axis=1)], axis=0)
            result = dot(weight[2 * at * rows : (2 * at + 2) * rows], right)
            top, bottom = result[:rows], result[rows:]
            numer_ref[:, lanes] = jnp.where(lower, top[:, :LANES], bottom[:, :LANES])
            denom_ref[:, lanes] = jnp.where(lower, top[:, LANES:], bottom[:, LANES:])
    swa_width = SWA_HEADS * SWA_HEAD
    not_before = jnp.where(first_block, WINDOW, 0)
    span = 2 * WINDOW
    place = iota((WINDOW, span), 1)
    row = iota((WINDOW, span), 0)
    inside = (place > row) & (place <= row + WINDOW)
    inside_first = inside & (place >= not_before)
    for step in range(rows // WINDOW):
        mine = slice(step * WINDOW, (step + 1) * WINDOW)
        window = slice((step - 1) * WINDOW, (step + 1) * WINDOW)

        def around(head, start):
            here = slice(start + head * SWA_HEAD, start + (head + 1) * SWA_HEAD)
            if step:
                return swa_ref[window, here]
            there = slice(here.start - swa_width, here.stop - swa_width)
            return jnp.concatenate([tails_ref[:WINDOW, there], swa_ref[mine, here]], axis=0)

        scores = []
        for head in range(SWA_HEADS):
            own = swa_ref[mine, head * SWA_HEAD : (head + 1) * SWA_HEAD]
            score = dot(own, around(head, swa_width), NT) * SWA_HEAD ** (-0.5)
            scores.append(jnp.where(inside if step else inside_first, score, -jnp.inf))
        scores = jnp.concatenate(scores, axis=0)
        expo = jnp.exp(scores - jnp.max(scores, axis=-1, keepdims=True))
        probs = (expo / jnp.sum(expo, axis=-1, keepdims=True)).astype(BF16)
        for head in range(SWA_HEADS):
            own = probs[head * WINDOW : (head + 1) * WINDOW]
            swa_out_ref[mine, head * SWA_HEAD : (head + 1) * SWA_HEAD] = dot(
                own, around(head, 2 * swa_width)
            )


def readout_kernel(own, qk_ref, numer_ref, denom_ref, swa_ref, past_ref, *refs):
    core = lax.axis_index(BLOCK) % 2
    half = core if own else 1 - core
    rows = qk_ref.shape[0]
    wide = PAIRS // 2 * LANES
    copies = []
    if own:
        (out_ref,) = refs
    else:
        own_ref, out_hbm, out_ref, sems = refs
        there = pl.ds(pl.multiple_of(core * wide, wide), wide)
        copies.append(pltpu.make_async_copy(own_ref, out_hbm.at[:, there], sems.at[PAIRS // 2]))
        copies[0].start()
    lower = iota((rows, LANES), 1) < VHEAD
    query = qk_ref[:, pl.ds(pl.multiple_of(half * LANES, LANES), LANES)]
    feature = iota((LANES, ROWS), 1)
    lane = iota((LANES, ROWS), 0)
    one = selector(feature, lane, False, halved=True).astype(BF16)
    two = selector(feature, lane, True).astype(BF16)
    add_one, add_two = adders(iota((8, ROWS), 1)[0:1])
    norms = []
    for pair in range(PAIRS // 2):
        last = past_ref[(pair + 1) * ROWS - 16 : (pair + 1) * ROWS, :].astype(jnp.float32)
        for place in range(2):
            at = 16 - (ROWS - CONST) + 1 + 2 * place
            norm = jnp.concatenate([last[at : at + 1], last[at + 1 : at + 2, : ROWS - LANES]], axis=1)
            norms.append(jnp.broadcast_to(norm, (8, ROWS)))
    norms = jnp.concatenate(norms + [jnp.zeros((LANES // 2, ROWS), jnp.float32)], axis=0).T.astype(BF16)
    source = iota((LANES, LANES), 0)
    target = iota((LANES, LANES), 1)
    own_heads = [
        jnp.where(head_mask(head, query.shape), query, jnp.zeros_like(query)) for head in range(HEADS // 2)
    ]
    stacked = jnp.concatenate(own_heads, axis=0)
    high, low = hi_lo((dot(stacked, one) + add_one) * (dot(stacked, two) + add_two))
    for pair in range(PAIRS // 2):
        here = pl.ds(pl.multiple_of(half * wide + pair * LANES, LANES), LANES)
        wanted = jnp.where(target < VHEAD, 16 * pair, 16 * pair + 8)
        spread = dot(norms, jnp.where(source == wanted, 1.0, 0.0).astype(BF16)).astype(BF16)
        right = jnp.concatenate([past_ref[pair * ROWS : (pair + 1) * ROWS, :], spread], axis=1)
        mine = slice(2 * pair * rows, (2 * pair + 2) * rows)
        result = dot(high[mine], right) + dot(low[mine], right)
        numer = jnp.where(lower, result[:rows, :LANES], result[rows:, :LANES]) + numer_ref[:, here]
        denom = jnp.where(lower, result[:rows, LANES:], result[rows:, LANES:]) + denom_ref[:, here]
        mixed = (numer / denom + swa_ref[:, here]).astype(BF16)
        out_ref[:, pair * LANES : (pair + 1) * LANES] = mixed
        if not own:
            done = out_ref.at[:, pair * LANES : (pair + 1) * LANES]
            copies.append(pltpu.make_async_copy(done, out_hbm.at[:, here], sems.at[pair]))
            copies[-1].start()
    for copy in copies:
        copy.wait()


IN_VMEM = pl.BlockSpec(memory_space=pltpu.VMEM)
IN_HBM = pl.BlockSpec(memory_space=pltpu.HBM)


def call(kernel, outs, args, specs, out_specs, scratch=()):
    placed = [pltpu.with_memory_space_constraint(a, spec.memory_space) for a, spec in zip(args, specs)]
    results = jax.tree.map(lambda out, spec: spec.memory_space(out.shape, out.dtype), outs, out_specs)
    return pl.pallas_call(
        kernel,
        out_shape=results,
        in_specs=specs,
        out_specs=out_specs,
        scratch_shapes=scratch,
        compiler_params=pltpu.CompilerParams(vmem_limit_bytes=16 * 1024 * 1024),
    )(*placed)


def shards(lin_qk, lin_v, conv_w, swa_qkv):
    rows = lin_qk.shape[0]
    taps = conv_w.shape[0]
    chips = lax.axis_size(BLOCK) // 2
    part = PAIRS // 2 * ROWS // chips
    held = (part + 7) // 8 * 8 + EXTRA
    shape = jax.ShapeDtypeStruct

    def swap(array):
        return lax.ppermute(array, BLOCK, [(i, i ^ 1) for i in range(2 * chips)])

    def exchange(array):
        groups = [[2 * chip + core for chip in group_order(chips)] for core in range(2)]
        return lax.all_to_all(array, BLOCK, 0, 0, axis_index_groups=groups, tiled=True)

    other_qk, other_v = swap(lin_qk), swap(lin_v)
    half_wide = lin_v.shape[1] // 2
    own_sums, tails, conv_half = call(
        functools.partial(state_kernel, part, True),
        [
            shape((chips, held, LANES), jnp.float32),
            shape((WINDOW + TAIL, swa_qkv.shape[1] // 3 * 2), BF16),
            shape((taps, half_wide), jnp.float32),
        ],
        [lin_qk, lin_v, conv_w, swa_qkv],
        [IN_HBM] * 4,
        [IN_VMEM] * 3,
        [
            pltpu.VMEM((rows, LANES), BF16),
            pltpu.VMEM((rows, half_wide), BF16),
            pltpu.SemaphoreType.DMA((5,)),
        ],
    )
    sums = call(
        functools.partial(state_kernel, part, False),
        shape((chips, held, LANES), BF16),
        [other_qk, other_v, conv_half, own_sums],
        [IN_VMEM] * 4,
        IN_VMEM,
    )
    sums, tails = lax.optimization_barrier((sums, tails))
    parts = exchange(sums)
    tails = lax.ppermute(tails, BLOCK, [(i, i + 1) for i in range(2 * chips - 1)])
    past = call(
        functools.partial(prefix_kernel, taps),
        shape((chips, part, LANES), BF16),
        [parts],
        [IN_VMEM],
        IN_VMEM,
    )
    here = exchange(past).reshape(chips * part, LANES)
    wide = shape(lin_v.shape, jnp.float32)
    numer, denom, swa = call(
        local_kernel,
        [wide, wide, wide],
        [lin_qk, lin_v, conv_w, swa_qkv, tails, other_qk, other_v],
        [IN_VMEM] * 7,
        [IN_VMEM] * 3,
    )
    here, numer, denom, swa = lax.optimization_barrier((here, numer, denom, swa))
    there = swap(here)
    own_out = call(
        functools.partial(readout_kernel, True),
        shape((rows, half_wide), BF16),
        [lin_qk, numer, denom, swa, here],
        [IN_VMEM] * 5,
        IN_VMEM,
    )
    return call(
        functools.partial(readout_kernel, False),
        shape(lin_v.shape, BF16),
        [lin_qk, numer, denom, swa, there, own_out],
        [IN_VMEM] * 6,
        IN_HBM,
        [pltpu.VMEM((rows, half_wide), BF16), pltpu.SemaphoreType.DMA((PAIRS // 2 + 1,))],
    )


def solution(mesh):
    blocks = jax.sharding.Mesh(mesh.devices.reshape(-1), (BLOCK,))
    return jax.shard_map(
        shards,
        mesh=blocks,
        in_specs=(P(BLOCK, None), P(BLOCK, None), P(), P(BLOCK, None)),
        out_specs=P(BLOCK, None),
        check_vma=False,
    )
```

```python
import functools

import jax
import jax.numpy as jnp
import numpy as np
from jax import lax
from jax.experimental import pallas as pl
from jax.experimental.pallas import tpu as pltpu
from jax.sharding import PartitionSpec as P

HEADS = 16
FEAT = 16
VHEAD = 64
SWA_HEADS = 8
SWA_HEAD = 128
WINDOW = 64

BLOCK = "block"
ORDER_SEED = 81
LANES = 128
PAIRS = HEADS // 2
QUADS = FEAT * (FEAT + 1) // 2
CONST = QUADS + FEAT
ROWS = 160
TAIL = 16
EXTRA = 8
BLOCK_EXTRA = 4


NT = (((1,), (1,)), ((), ()))
NN = (((1,), (0,)), ((), ()))
BF16 = jnp.bfloat16


def dot(a, b, dims=NN):
    return lax.dot_general(a, b, dims, preferred_element_type=jnp.float32)


def iota(shape, dim):
    return lax.broadcasted_iota(jnp.int32, shape, dim)


def selector(feature, lane, second, halved=False):
    scale = FEAT ** (-0.25)
    quad = feature < QUADS
    entry = feature % FEAT
    if second:
        wanted = (feature + feature // FEAT) % FEAT
        return jnp.where((lane % FEAT == wanted) & quad, scale, 0.0)
    linear = (feature >= QUADS) & (feature < CONST)
    wanted = jnp.where(quad, entry, (feature - QUADS) % FEAT)
    weight = jnp.where((feature < FEAT) & halved, 0.5 * scale, scale)
    return jnp.where((lane % FEAT == wanted) & (quad | linear), weight, 0.0)


def adders(feature):
    first = jnp.where(feature == CONST, 1.0, 0.0)
    second = jnp.where((feature >= QUADS) & (feature <= CONST), 1.0, 0.0)
    return first, second


def group_order(chips):
    return [int(chip) for chip in np.random.RandomState(ORDER_SEED).permutation(chips)]


def head_mask(head, shape):
    place = iota(shape, 1)
    return (place >= head * FEAT) & (place < (head + 1) * FEAT)


def hi_lo(values):
    high = values.astype(BF16)
    return high, (values - high.astype(jnp.float32)).astype(BF16)


def convolved(value, tail, conv_ref, lanes):
    row_id = iota(value.shape, 0)
    result = conv_ref[0:1, lanes] * value
    for lag in range(1, conv_ref.shape[0]):
        shifted = pltpu.roll(value, lag, 0)
        for row in range(lag):
            source = TAIL - lag + row
            before = 0.0 if tail is None else tail[source : source + 1]
            shifted = jnp.where(row_id == row, before, shifted)
        result = result + conv_ref[lag : lag + 1, lanes] * shifted
    return result.astype(BF16)


def state_kernel(part, own, *refs):
    core = lax.axis_index(BLOCK) % 2
    if own:
        qk_hbm, v_hbm, conv_hbm, swa_hbm, out_ref, tails_ref, conv_ref, key_ref, v_ref, sems = refs
        rows, wide = v_hbm.shape
    else:
        qk_ref, v_ref, conv_ref, own_ref, out_ref = refs
        rows, wide = v_ref.shape
    taps = conv_ref.shape[0]
    mine = pl.ds(pl.multiple_of(core * (wide // 2), wide // 2), wide // 2)
    keys = pl.ds(pl.multiple_of(HEADS * FEAT + core * LANES, LANES), LANES)
    if own:
        pieces = [
            (qk_hbm.at[:, keys], key_ref),
            (conv_hbm.at[:, mine], conv_ref),
            (v_hbm.at[:, mine], v_ref),
            (swa_hbm.at[rows - WINDOW :, tails_ref.shape[1] // 2 :], tails_ref.at[:WINDOW, :]),
            (v_hbm.at[rows - TAIL :, :], tails_ref.at[WINDOW:, :wide]),
        ]
        copies = [pltpu.make_async_copy(a, b, sems.at[i]) for i, (a, b) in enumerate(pieces)]
        for copy in copies:
            copy.start()
        copies[0].wait()
        key = key_ref[...]
    else:
        copies = []
        key = qk_ref[:, keys]
    key_t = (key.astype(jnp.float32) * FEAT ** (-0.25)).T
    const_rows = jnp.where(iota((EXTRA, rows), 0) == 0, 1.0, 0.0)
    lane_id = iota((ROWS, LANES), 1)
    low_row = iota((EXTRA, LANES), 0)
    ones = jnp.ones((rows, LANES), BF16)
    half = FEAT // 2
    padded = (part + 7) // 8 * 8
    lefts = []
    for head in range(HEADS // 2):
        x = key_t[head * FEAT : (head + 1) * FEAT]
        blocks = [x * x]
        for by in range(1, half):
            blocks.append(x * jnp.concatenate([x[by:], x[:by]], axis=0))
        blocks += [x[:half] * x[half:], x, const_rows]
        lefts.append(jnp.concatenate(hi_lo(jnp.concatenate(blocks, axis=0)), axis=1))
    first_keys = key[:16].astype(jnp.float32)
    slot = low_row - BLOCK_EXTRA * (core if own else 1 - core)
    for copy in copies[1:3]:
        copy.wait()
    states = []
    extras = []
    norms = jnp.zeros((ROWS, LANES), jnp.float32)
    for pair in range(PAIRS // 2):
        lanes = slice(pair * LANES, (pair + 1) * LANES)
        at = pl.multiple_of((0 if own else core * (wide // 2)) + pair * LANES, LANES)
        value = v_ref[:, pl.ds(at, LANES)].astype(jnp.float32)
        conved = convolved(value, None, conv_ref, lanes)
        right = jnp.concatenate([conved, ones], axis=1)
        right = jnp.concatenate([right, right], axis=0)
        both = []
        for head in (2 * pair, 2 * pair + 1):
            result = dot(lefts[head], right)
            both.append(result[:, :LANES])
            norms = jnp.where(lane_id // 8 == head, result[:, LANES:], norms)
        states.append(jnp.where(lane_id < VHEAD, both[0], both[1]))
        extra = jnp.zeros((EXTRA, LANES), jnp.float32)
        for row in range(taps - 1):
            share = jnp.zeros((1, LANES), jnp.float32)
            for lag in range(row + 1, taps):
                last = rows + row - lag
                share = share + conv_ref[lag : lag + 1, lanes] * value[last : last + 1]
            extra = jnp.where(slot == row, share, extra)
            extra = jnp.where(slot == taps - 1 + row, first_keys[row : row + 1], extra)
        extras.append(extra)
    norms_t = norms.T
    for pair in range(PAIRS // 2):
        last = states[pair][CONST:]
        for place in range(2):
            at = 8 * (2 * pair + place)
            norm = norms_t[at : at + 8]
            rest = jnp.concatenate(
                [norm[:, LANES:], jnp.zeros((8, 2 * LANES - ROWS), jnp.float32)], axis=1
            )
            last = jnp.where(low_row == 1 + 2 * place, norm[:, :LANES], last)
            last = jnp.where(low_row == 2 + 2 * place, rest, last)
        state = jnp.concatenate([states[pair][:CONST], last], axis=0)
        for piece in range(ROWS // part):
            rows_of = [state[piece * part : (piece + 1) * part]]
            if padded != part:
                rows_of.append(jnp.zeros((padded - part, LANES), jnp.float32))
            message = jnp.concatenate(rows_of + [extras[pair]], axis=0)
            chunk = pair * (ROWS // part) + piece
            if own:
                out_ref[chunk] = message
            else:
                out_ref[chunk] = (own_ref[chunk] + message).astype(BF16)
    for copy in copies[3:]:
        copy.wait()


def prefix_kernel(taps, parts_ref, out_ref):
    chips, held, _ = parts_ref.shape
    part = out_ref.shape[1]
    padded = held - EXTRA
    width = chips * EXTRA
    block = lax.axis_index(BLOCK)
    places = list(np.argsort(group_order(chips)))
    place = sum(jnp.where(block // 2 == chip, int(at), 0) for chip, at in enumerate(places))
    start = block % 2 * (ROWS * PAIRS // 2) + place * part
    head = start // ROWS * 2 % (LANES // FEAT)
    feature = start % ROWS + iota((padded, LANES), 0)
    lane = iota((padded, LANES), 1)
    one = selector(feature, lane, False)
    two = selector(feature, lane, True)
    add_one, add_two = adders(feature[:, 0:1])
    extras = jnp.concatenate(
        [parts_ref[int(at)].astype(jnp.float32)[padded:] for at in places], axis=0
    )
    extras_low = extras.astype(BF16)
    upper = iota((width, LANES), 1) >= VHEAD
    heads = [lane // FEAT == head + place for place in range(2)]
    factors = [jnp.where(mine, factor, 0.0) for factor in (one, two) for mine in heads]
    products = dot(jnp.concatenate(factors, axis=0).astype(BF16), extras_low, NT)
    lefts = []
    rights = []
    for side in range(2):
        first = products[side * padded : (side + 1) * padded] + add_one
        second = products[(side + 2) * padded : (side + 3) * padded] + add_two
        lefts.append(pltpu.roll(first * second, width - BLOCK_EXTRA - (taps - 1), 1))
        rights.append(jnp.where(upper == (side == 1), extras, 0.0).astype(BF16))
    left = jnp.concatenate(lefts, axis=1)
    right = jnp.concatenate(rights, axis=0)
    column = iota(left.shape, 1) % width
    to_block = jnp.where(column % BLOCK_EXTRA < taps - 1, column // BLOCK_EXTRA + 1, 2 * chips)

    seen = [jnp.where(to_block <= 2 * chip, left, 0.0).astype(BF16) for chip in range(chips)]
    added = dot(jnp.concatenate(seen, axis=0), right)
    total = jnp.zeros((padded, LANES), jnp.float32)
    for chip, at in enumerate(places):
        result = total + added[chip * padded : (chip + 1) * padded]
        out_ref[int(at)] = result[:part].astype(BF16)
        total = total + parts_ref[int(at)].astype(jnp.float32)[:padded]


def local_kernel(
    qk_ref, v_ref, conv_ref, swa_ref, tails_ref, other_qk_ref, other_v_ref,
    numer_ref, denom_ref, swa_out_ref,
):
    rows = v_ref.shape[0]
    taps = conv_ref.shape[0]
    width = HEADS * FEAT
    core = lax.axis_index(BLOCK) % 2
    second = core == 1
    first_block = lax.axis_index(BLOCK) == 0
    query = qk_ref[:, :width]
    key = qk_ref[:, width : 2 * width]
    lower = iota((rows, LANES), 1) < VHEAD
    causal = iota((rows, rows), 1) <= iota((rows, rows), 0)
    row_id = iota((rows, LANES), 0)
    ones = jnp.ones((rows, LANES), BF16)
    counted = jnp.where(second, ones, jnp.zeros_like(ones))
    more_key = jnp.where(second, other_qk_ref[:, width : 2 * width], key)
    all_keys = jnp.concatenate([key, more_key], axis=0)
    allowed = jnp.concatenate([causal, causal | True], axis=1)
    group_heads = 4
    for group in range(0, HEADS, group_heads):
        own = jnp.concatenate(
            [
                jnp.where(head_mask(head, query.shape), query, jnp.zeros_like(query))
                for head in range(group, group + group_heads)
            ],
            axis=0,
        )
        score = dot(own, all_keys, NT) * FEAT ** (-0.5)
        weight = 1.0 + score + 0.5 * score * score
        weight = jnp.where(jnp.concatenate([allowed] * group_heads, axis=0), weight, 0.0).astype(BF16)
        for at in range(group_heads // 2):
            pair = group // 2 + at
            lanes = slice(pair * LANES, (pair + 1) * LANES)
            tail = jnp.where(first_block, 0.0, tails_ref[WINDOW:, lanes].astype(jnp.float32))
            conved = convolved(v_ref[:, lanes].astype(jnp.float32), tail, conv_ref, lanes)
            before = convolved(other_v_ref[:, lanes].astype(jnp.float32), None, conv_ref, lanes)
            shares = jnp.zeros((rows, LANES), jnp.float32)
            for row in range(taps - 1):
                share = jnp.zeros((1, LANES), jnp.float32)
                for lag in range(row + 1, taps):
                    at_row = TAIL + row - lag
                    share = share + conv_ref[lag : lag + 1, lanes] * tail[at_row : at_row + 1]
                shares = jnp.where(row_id == row, -share, shares)
            before = jnp.where(second, before, shares.astype(BF16))
            right = jnp.concatenate([conved, ones], axis=1)
            right = jnp.concatenate([right, jnp.concatenate([before, counted], axis=1)], axis=0)
            result = dot(weight[2 * at * rows : (2 * at + 2) * rows], right)
            top, bottom = result[:rows], result[rows:]
            numer_ref[:, lanes] = jnp.where(lower, top[:, :LANES], bottom[:, :LANES])
            denom_ref[:, lanes] = jnp.where(lower, top[:, LANES:], bottom[:, LANES:])
    swa_width = SWA_HEADS * SWA_HEAD
    not_before = jnp.where(first_block, WINDOW, 0)
    span = 2 * WINDOW
    place = iota((WINDOW, span), 1)
    row = iota((WINDOW, span), 0)
    inside = (place > row) & (place <= row + WINDOW)
    inside_first = inside & (place >= not_before)
    for step in range(rows // WINDOW):
        mine = slice(step * WINDOW, (step + 1) * WINDOW)
        window = slice((step - 1) * WINDOW, (step + 1) * WINDOW)

        def around(head, start):
            here = slice(start + head * SWA_HEAD, start + (head + 1) * SWA_HEAD)
            if step:
                return swa_ref[window, here]
            there = slice(here.start - swa_width, here.stop - swa_width)
            return jnp.concatenate([tails_ref[:WINDOW, there], swa_ref[mine, here]], axis=0)

        scores = []
        for head in range(SWA_HEADS):
            own = swa_ref[mine, head * SWA_HEAD : (head + 1) * SWA_HEAD]
            score = dot(own, around(head, swa_width), NT) * SWA_HEAD ** (-0.5)
            scores.append(jnp.where(inside if step else inside_first, score, -jnp.inf))
        scores = jnp.concatenate(scores, axis=0)
        expo = jnp.exp(scores - jnp.max(scores, axis=-1, keepdims=True))
        probs = (expo / jnp.sum(expo, axis=-1, keepdims=True)).astype(BF16)
        for head in range(SWA_HEADS):
            own = probs[head * WINDOW : (head + 1) * WINDOW]
            swa_out_ref[mine, head * SWA_HEAD : (head + 1) * SWA_HEAD] = dot(
                own, around(head, 2 * swa_width)
            )


def readout_kernel(own, qk_ref, numer_ref, denom_ref, swa_ref, past_ref, *refs):
    core = lax.axis_index(BLOCK) % 2
    half = core if own else 1 - core
    rows = qk_ref.shape[0]
    wide = PAIRS // 2 * LANES
    copies = []
    if own:
        (out_ref,) = refs
    else:
        own_ref, out_hbm, out_ref, sems = refs
        there = pl.ds(pl.multiple_of(core * wide, wide), wide)
        copies.append(pltpu.make_async_copy(own_ref, out_hbm.at[:, there], sems.at[PAIRS // 2]))
        copies[0].start()
    lower = iota((rows, LANES), 1) < VHEAD
    query = qk_ref[:, pl.ds(pl.multiple_of(half * LANES, LANES), LANES)]
    feature = iota((LANES, ROWS), 1)
    lane = iota((LANES, ROWS), 0)
    one = selector(feature, lane, False, halved=True).astype(BF16)
    two = selector(feature, lane, True).astype(BF16)
    add_one, add_two = adders(iota((8, ROWS), 1)[0:1])
    norms = []
    for pair in range(PAIRS // 2):
        last = past_ref[(pair + 1) * ROWS - 16 : (pair + 1) * ROWS, :].astype(jnp.float32)
        for place in range(2):
            at = 16 - (ROWS - CONST) + 1 + 2 * place
            norm = jnp.concatenate([last[at : at + 1], last[at + 1 : at + 2, : ROWS - LANES]], axis=1)
            norms.append(jnp.broadcast_to(norm, (8, ROWS)))
    norms = jnp.concatenate(norms + [jnp.zeros((LANES // 2, ROWS), jnp.float32)], axis=0).T.astype(BF16)
    source = iota((LANES, wide), 0)
    target = iota((LANES, wide), 1)
    spreads = dot(norms, jnp.where(source == target // VHEAD * 8, 1.0, 0.0).astype(BF16)).astype(BF16)
    own_heads = [
        jnp.where(head_mask(head, query.shape), query, jnp.zeros_like(query)) for head in range(HEADS // 2)
    ]
    stacked = jnp.concatenate(own_heads, axis=0)
    high, low = hi_lo((dot(stacked, one) + add_one) * (dot(stacked, two) + add_two))
    for pair in range(PAIRS // 2):
        here = pl.ds(pl.multiple_of(half * wide + pair * LANES, LANES), LANES)
        spread = spreads[:, pair * LANES : (pair + 1) * LANES]
        right = jnp.concatenate([past_ref[pair * ROWS : (pair + 1) * ROWS, :], spread], axis=1)
        mine = slice(2 * pair * rows, (2 * pair + 2) * rows)
        result = dot(high[mine], right) + dot(low[mine], right)
        numer = jnp.where(lower, result[:rows, :LANES], result[rows:, :LANES]) + numer_ref[:, here]
        denom = jnp.where(lower, result[:rows, LANES:], result[rows:, LANES:]) + denom_ref[:, here]
        mixed = (numer / denom + swa_ref[:, here]).astype(BF16)
        out_ref[:, pair * LANES : (pair + 1) * LANES] = mixed
        if not own:
            done = out_ref.at[:, pair * LANES : (pair + 1) * LANES]
            copies.append(pltpu.make_async_copy(done, out_hbm.at[:, here], sems.at[pair]))
            copies[-1].start()
    for copy in copies:
        copy.wait()


IN_VMEM = pl.BlockSpec(memory_space=pltpu.VMEM)
IN_HBM = pl.BlockSpec(memory_space=pltpu.HBM)


def call(kernel, outs, args, specs, out_specs, scratch=()):
    placed = [pltpu.with_memory_space_constraint(a, spec.memory_space) for a, spec in zip(args, specs)]
    results = jax.tree.map(lambda out, spec: spec.memory_space(out.shape, out.dtype), outs, out_specs)
    return pl.pallas_call(
        kernel,
        out_shape=results,
        in_specs=specs,
        out_specs=out_specs,
        scratch_shapes=scratch,
        compiler_params=pltpu.CompilerParams(vmem_limit_bytes=16 * 1024 * 1024),
    )(*placed)


def shards(lin_qk, lin_v, conv_w, swa_qkv):
    rows = lin_qk.shape[0]
    taps = conv_w.shape[0]
    chips = lax.axis_size(BLOCK) // 2
    part = PAIRS // 2 * ROWS // chips
    held = (part + 7) // 8 * 8 + EXTRA
    shape = jax.ShapeDtypeStruct

    def swap(array):
        return lax.ppermute(array, BLOCK, [(i, i ^ 1) for i in range(2 * chips)])

    def exchange(array):
        groups = [[2 * chip + core for chip in group_order(chips)] for core in range(2)]
        return lax.all_to_all(array, BLOCK, 0, 0, axis_index_groups=groups, tiled=True)

    other_qk, other_v = swap(lin_qk), swap(lin_v)
    half_wide = lin_v.shape[1] // 2
    own_sums, tails, conv_half = call(
        functools.partial(state_kernel, part, True),
        [
            shape((chips, held, LANES), jnp.float32),
            shape((WINDOW + TAIL, swa_qkv.shape[1] // 3 * 2), BF16),
            shape((taps, half_wide), jnp.float32),
        ],
        [lin_qk, lin_v, conv_w, swa_qkv],
        [IN_HBM] * 4,
        [IN_VMEM] * 3,
        [
            pltpu.VMEM((rows, LANES), BF16),
            pltpu.VMEM((rows, half_wide), BF16),
            pltpu.SemaphoreType.DMA((5,)),
        ],
    )
    sums = call(
        functools.partial(state_kernel, part, False),
        shape((chips, held, LANES), BF16),
        [other_qk, other_v, conv_half, own_sums],
        [IN_VMEM] * 4,
        IN_VMEM,
    )
    sums, tails = lax.optimization_barrier((sums, tails))
    parts = exchange(sums)
    tails = lax.ppermute(tails, BLOCK, [(i, i + 1) for i in range(2 * chips - 1)])
    past = call(
        functools.partial(prefix_kernel, taps),
        shape((chips, part, LANES), BF16),
        [parts],
        [IN_VMEM],
        IN_VMEM,
    )
    here = exchange(past).reshape(chips * part, LANES)
    wide = shape(lin_v.shape, jnp.float32)
    numer, denom, swa = call(
        local_kernel,
        [wide, wide, wide],
        [lin_qk, lin_v, conv_w, swa_qkv, tails, other_qk, other_v],
        [IN_VMEM] * 7,
        [IN_VMEM] * 3,
    )
    here, numer, denom, swa = lax.optimization_barrier((here, numer, denom, swa))
    there = swap(here)
    own_out = call(
        functools.partial(readout_kernel, True),
        shape((rows, half_wide), BF16),
        [lin_qk, numer, denom, swa, here],
        [IN_VMEM] * 5,
        IN_VMEM,
    )
    return call(
        functools.partial(readout_kernel, False),
        shape(lin_v.shape, BF16),
        [lin_qk, numer, denom, swa, there, own_out],
        [IN_VMEM] * 6,
        IN_HBM,
        [pltpu.VMEM((rows, half_wide), BF16), pltpu.SemaphoreType.DMA((PAIRS // 2 + 1,))],
    )


def solution(mesh):
    blocks = jax.sharding.Mesh(mesh.devices.reshape(-1), (BLOCK,))
    return jax.shard_map(
        shards,
        mesh=blocks,
        in_specs=(P(BLOCK, None), P(BLOCK, None), P(), P(BLOCK, None)),
        out_specs=P(BLOCK, None),
        check_vma=False,
    )
```
